32 devices in a mesh: fsdp: 16 (over z, y, x), dp: 2 (over core).
Axes of the slice: x: 2, y: 2, z: 4, core: 2. Of those that a mesh axis runs over, the one named last changes fastest.
Arguments:
- tokens: bfloat16 [32, 1024, 768], P(('fsdp', 'dp')), may hold values from -16 to 16
- segment_ids: int32 [32, 1024], P(('fsdp', 'dp')), may hold values from 0 to 8, as said below
- cotangent: bfloat16 [32, 1024, 768], P(('fsdp', 'dp')), may hold values from -6 to 6
- weight_query: bfloat16 [768, 768], P(None, 'fsdp'), may hold values from -0.21875 to 0.21875
- weight_key: bfloat16 [768, 768], P(None, 'fsdp'), may hold values from -0.21875 to 0.21875
- weight_value: bfloat16 [768, 768], P(None, 'fsdp'), may hold values from -0.21875 to 0.21875
- weight_output: bfloat16 [768, 768], P(None, 'fsdp'), may hold values from -2.5 to 2.5
- weight_inner: bfloat16 [768, 3072], P(None, 'fsdp'), may hold values from -0.21875 to 0.21875
- weight_outer: bfloat16 [3072, 768], P(None, 'fsdp'), may hold values from -0.109375 to 0.109375
- bias_query: bfloat16 [768], P('fsdp'), may hold values from -3 to 3
- bias_value: bfloat16 [768], P('fsdp'), may hold values from -3 to 3
- bias_output: bfloat16 [768], P('fsdp'), may hold values from -3 to 3
- bias_inner: bfloat16 [3072], P('fsdp'), may hold values from -3 to 3
- bias_outer: bfloat16 [768], P('fsdp'), may hold values from -3 to 3
- gain_attn: bfloat16 [768], P('fsdp'), may hold values from 0.5 to 1.5
- shift_attn: bfloat16 [768], P('fsdp'), may hold values from -2 to 2
- gain_ffn: bfloat16 [768], P('fsdp'), may hold values from 0.5 to 1.5
- shift_ffn: bfloat16 [768], P('fsdp'), may hold values from -2 to 2
Outputs:
- output: bfloat16 [32, 1024, 768], P(('fsdp', 'dp'))
- grad_tokens: bfloat16 [32, 1024, 768], P(('fsdp', 'dp'))
- grad_weight_query: float32 [768, 768], P(None, 'fsdp')
- grad_weight_key: float32 [768, 768], P(None, 'fsdp')
- grad_weight_value: float32 [768, 768], P(None, 'fsdp')
- grad_weight_output: float32 [768, 768], P(None, 'fsdp')
- grad_weight_inner: float32 [768, 3072], P(None, 'fsdp')
- grad_weight_outer: float32 [3072, 768], P(None, 'fsdp')
- grad_bias_query: float32 [768], P('fsdp')
- grad_bias_value: float32 [768], P('fsdp')
- grad_bias_output: float32 [768], P('fsdp')
- grad_bias_inner: float32 [3072], P('fsdp')
- grad_bias_outer: float32 [768], P('fsdp')
- grad_gain_attn: float32 [768], P('fsdp')
- grad_shift_attn: float32 [768], P('fsdp')
- grad_gain_ffn: float32 [768], P('fsdp')
- grad_shift_ffn: float32 [768], P('fsdp')
- rms_stats: float32 [4], replicated
The draws below stay inside these ranges and needn't reach their ends.
Inputs may be any that keep to these rules, and one draw needn't show every extreme that they name: `segment_ids`: within each sequence the ids start at 1 on its first token, never fall and grow by one at each new document; a new document begins at least at every multiple of 128 positions until the id reaches 8, after which the rest of the sequence is one document; 0 marks padding, which fills only a sequence's end.
All inputs are finite; a program needn't handle non-finite values.
Results may differ from the reference program's by a relative error of at most 0.013.
Values may be sent and summed in bfloat16 or wider, within the bound.
A program may use at most 192 MiB of HBM per device.

```python
import math
import jax
import jax.numpy as jnp
from jax import lax

D = 768
H = 12
HD = 64
FF = 3072
LEN = 1024
DOC_MEAN = 128
SEQS = 32


def draw_tokens(key, part):
    place = jnp.arange(SEQS, dtype=jnp.float32) / max(SEQS - 1, 1)
    base = jnp.clip(jax.random.normal(key, (SEQS, LEN, D), jnp.float32), -5.0, 5.0)
    scale = jnp.exp(jnp.log(3.0) * place)
    return (base * scale[:, None, None]).astype(jnp.bfloat16)


def draw_segment_ids(key, part):
    begins = jax.random.randint(jax.random.fold_in(key, 11), (SEQS, LEN), 0, DOC_MEAN)
    position = jnp.arange(LEN, dtype=jnp.int32)[None, :]
    starts = jnp.where((begins == 0) | (position % DOC_MEAN == 0), 1, 0).astype(jnp.int32)
    doc_ids = jnp.minimum(jnp.cumsum(starts, axis=1), LEN // DOC_MEAN).astype(jnp.int32)
    limit = 2 * LEN // 3 * jnp.arange(SEQS, dtype=jnp.int32) // max(SEQS - 1, 1)
    padding = jax.random.randint(jax.random.fold_in(key, 12), (SEQS,), 0, limit + 1)
    return jnp.where(position >= LEN - padding[:, None], 0, doc_ids).astype(jnp.int32)


def with_spikes(values, stream_key, source, target, parts, factor):
    owner, partner = [(jnp.arange(values.shape[axis_at]) // (values.shape[axis_at] // parts)).reshape([-1 if axis == axis_at else 1 for axis in range(values.ndim)]) for axis_at in (source, target)]
    chosen = jax.random.permutation(stream_key, parts)[partner]
    strong = (owner == chosen) | (owner == (partner + parts // 2) % parts)
    return jnp.where(strong, factor * values, values)


def level_of(stream_key, shape, cuts, least, top_value):
    factor_of, own = 1.0, jax.random.fold_in(stream_key, 6)
    for axis_at, blocks in cuts:
        heights = jnp.exp(jax.random.uniform(jax.random.fold_in(own, axis_at), (blocks,), jnp.float32, least / len(cuts), top_value / len(cuts)))
        factor_of = factor_of * jnp.repeat(heights, shape[axis_at] // blocks).reshape([-1 if axis == axis_at else 1 for axis in range(len(shape))])
    return factor_of


def gaussian(stream_key, extent, scale, reach, cuts=(), held_as=jnp.bfloat16):
    drawn = scale * jax.random.normal(stream_key, extent, jnp.float32)
    if cuts:
        drawn = drawn * level_of(stream_key, extent, cuts, -0.22, 0.18)
    return jnp.clip(drawn, -reach, reach).astype(held_as)


def heavy_noise(rng, extent, deviation, most, cuts, heavy, held_as=jnp.bfloat16):
    drawn = deviation * jax.random.normal(rng, extent, jnp.float32)
    if cuts:
        drawn = drawn * level_of(rng, extent, cuts, -0.22, 0.18)
    return jnp.clip(with_spikes(drawn, jax.random.fold_in(rng, 3), *heavy), -most, most).astype(held_as)


def setup_inputs(seed: int = 0) -> dict:
    seeds = jax.random.split(jax.random.key(seed), 19)
    return {
        "tokens": draw_tokens(jax.random.fold_in(seeds[18], 71), 0),
        "segment_ids": draw_segment_ids(jax.random.fold_in(seeds[18], 71), 0),
        "cotangent": heavy_noise(seeds[2], (SEQS, LEN, D), 1.0, 6.0, ((0, 32),), (0, 2, 32, 2.75)),
        "weight_query": gaussian(seeds[3], (D, D), D ** -0.5, 0.21875, ((1, 16),)),
        "weight_key": gaussian(seeds[4], (D, D), D ** -0.5, 0.21875, ((1, 16),)),
        "weight_value": gaussian(seeds[5], (D, D), D ** -0.5, 0.21875, ((1, 16),)),
        "weight_output": gaussian(seeds[6], (D, D), (D // DOC_MEAN) ** -0.5, 2.5, ((1, 16),)),
        "weight_inner": gaussian(seeds[7], (D, FF), D ** -0.5, 0.21875, ((1, 16),)),
        "weight_outer": gaussian(seeds[8], (FF, D), FF ** -0.5, 0.109375, ((1, 16),)),
        "bias_query": gaussian(seeds[9], (D,), 0.5, 3.0, ((0, 16),)),
        "bias_value": gaussian(seeds[10], (D,), 0.5, 3.0, ((0, 16),)),
        "bias_output": gaussian(seeds[11], (D,), 0.5, 3.0, ((0, 16),)),
        "bias_inner": gaussian(seeds[12], (FF,), 0.5, 3.0, ((0, 16),)),
        "bias_outer": gaussian(seeds[13], (D,), 0.5, 3.0, ((0, 16),)),
        "gain_attn": jnp.clip(1.0 + 0.1 * jax.random.normal(seeds[14], (D,), jnp.float32), 0.5, 1.5).astype(jnp.bfloat16),
        "shift_attn": gaussian(seeds[15], (D,), 0.3, 2.0, ((0, 16),)),
        "gain_ffn": jnp.clip(1.0 + 0.1 * jax.random.normal(seeds[16], (D,), jnp.float32), 0.5, 1.5).astype(jnp.bfloat16),
        "shift_ffn": gaussian(seeds[17], (D,), 0.3, 2.0, ((0, 16),)),
    }


@jax.custom_vjp
def low(v):
    return lax.optimization_barrier(v.astype(jnp.bfloat16)).astype(jnp.float32)

@jax.custom_vjp
def low_back(v):
    return v

def low_keep(v):
    return (low(v), None)

def low_pass(kept, grad):
    return (grad,)

def back_keep(v):
    return (v, None)

def back_low(kept, grad):
    return (low(grad),)
low.defvjp(low_keep, low_pass)
low_back.defvjp(back_keep, back_low)

def round_both(values):
    return low(low_back(values))

def normalize(values, gain_vec, shift_vec):
    average = lax.optimization_barrier(jnp.mean(values, axis=-1, keepdims=True))
    centered = values - average
    spread = lax.optimization_barrier(jnp.mean(centered * centered, axis=-1, keepdims=True))
    return centered * lax.rsqrt(spread + 1e-06) * gain_vec + shift_vec

def product(operand, matrix):
    return jnp.einsum('...d,de->...e', operand, matrix, precision=lax.Precision.HIGHEST)

def attend_one(packed):
    queries, key_rows, value_rows, doc_ids = packed
    seq_len = queries.shape[0]
    query_heads = queries.reshape(seq_len, H, HD)
    key_heads = key_rows.reshape(seq_len, H, HD)
    value_heads = value_rows.reshape(seq_len, H, HD)
    scores = jnp.einsum('qhd,khd->hqk', query_heads, key_heads, precision=lax.Precision.HIGHEST) * (1.0 / math.sqrt(HD))
    scores = low_back(scores)
    same_doc = (doc_ids[:, None] == doc_ids[None, :])[None]
    scores = jnp.where(same_doc, scores, -1e+30)
    largest = lax.optimization_barrier(jnp.max(scores, axis=-1, keepdims=True))
    exponent = jnp.exp(scores - largest)
    probability = low(exponent / lax.optimization_barrier(jnp.sum(exponent, axis=-1, keepdims=True)))
    attended = jnp.einsum('hqk,khd->qhd', probability, value_heads, precision=lax.Precision.HIGHEST)
    return attended.reshape(seq_len, H * HD)

def forward(stream, params, doc_ids):
    w_query, w_key, w_value, w_output, w_inner, w_outer, b_query, b_value, b_output, b_inner, b_outer, attn_gain, attn_shift, ffn_gain, ffn_shift = params
    normed = low(normalize(stream, attn_gain, attn_shift))
    queries = round_both(product(normed, w_query) + b_query)
    key_rows = round_both(product(normed, w_key))
    value_rows = round_both(product(normed, w_value) + b_value)
    attended = lax.map(jax.checkpoint(attend_one), (queries, key_rows, value_rows, doc_ids))
    attended = round_both(attended)
    branch = low_back(product(attended, w_output) + b_output)
    middle = stream + branch
    second = low(normalize(middle, ffn_gain, ffn_shift))
    hidden = low_back(product(second, w_inner) + b_inner)
    active = low(jax.nn.gelu(hidden, approximate=False))
    ffn_out = product(active, w_outer) + b_outer
    return (middle + ffn_out, (branch, middle, ffn_out))

def reference(tokens, segment_ids, cotangent, weight_query, weight_key, weight_value, weight_output, weight_inner, weight_outer, bias_query, bias_value, bias_output, bias_inner, bias_outer, gain_attn, shift_attn, gain_ffn, shift_ffn):
    params = tuple((p.astype(jnp.float32) for p in (weight_query, weight_key, weight_value, weight_output, weight_inner, weight_outer, bias_query, bias_value, bias_output, bias_inner, bias_outer, gain_attn, shift_attn, gain_ffn, shift_ffn)))
    group_size = 4
    group_count = tokens.shape[0] // group_size
    token_groups = tokens.reshape(group_count, group_size, LEN, D)
    id_groups = segment_ids.reshape(group_count, group_size, LEN)
    cot_groups = cotangent.reshape(group_count, group_size, LEN, D)

    def one_group(carry, packed):
        totals, stat_sums = carry
        token_block, id_block, cot_block = packed
        stream = token_block.astype(jnp.float32)

        def layer_fn(stream_in, params_in):
            return forward(stream_in, params_in, id_block)
        result, back_fn, extras = jax.vjp(layer_fn, stream, params, has_aux=True)
        grad_stream, grad_params = back_fn(cot_block.astype(jnp.float32))
        valid_mask = (id_block != 0).astype(jnp.float32)
        pieces = (stream, extras[0], extras[1], extras[2])
        squares = jnp.stack([jnp.sum(lax.optimization_barrier(jnp.sum(piece * piece, axis=-1)) * valid_mask) for piece in pieces])
        stat_sums = stat_sums + jnp.concatenate([squares, jnp.sum(valid_mask)[None]])
        totals = jax.tree.map(lambda acc, new: acc + new, totals, grad_params)
        return ((totals, stat_sums), (result.astype(jnp.bfloat16), grad_stream.astype(jnp.bfloat16)))
    initial = (tuple((jnp.zeros(p.shape, jnp.float32) for p in params)), jnp.zeros((5,), jnp.float32))
    (totals, stat_sums), (outputs, grad_inputs) = lax.scan(one_group, initial, (token_groups, id_groups, cot_groups))
    rms_stats = jnp.sqrt(stat_sums[:4] / (stat_sums[4] * D))
    return (outputs.reshape(tokens.shape), grad_inputs.reshape(tokens.shape), totals[0], totals[1], totals[2], totals[3], totals[4], totals[5], totals[6], totals[7], totals[8], totals[9], totals[10], totals[11], totals[12], totals[13], totals[14], rms_stats)
```

```python
import math

import jax
import jax.numpy as jnp
import numpy as np
from jax import lax
from jax.experimental import pallas as pl
from jax.experimental.pallas import tpu as pltpu
from jax.sharding import PartitionSpec as P

HD = 64
BF, F32 = jnp.bfloat16, jnp.float32
MESH = pl.DeviceIdType.MESH
SEQ, WIDTH, PIECE, BLOCK = 1024, 768, 48, 256
EVERY = slice(None)


def dg(lhs, rhs, lhs_dim, rhs_dim):
    return lax.dot_general(
        lhs, rhs, (((lhs_dim,), (rhs_dim,)), ((), ())), preferred_element_type=F32
    )


def lanes(rows):
    return lax.broadcasted_iota(jnp.int32, (rows, 128), 1)


def aligned(start, size, unit=128):
    return pl.ds(pl.multiple_of(start, unit), size)


class Place:
    def __init__(self):
        index = lax.axis_index("fsdp")
        self.core = lax.axis_index("dp")
        self.x = lax.rem(index, 2)
        self.y = lax.rem(lax.div(index, 2), 2)
        self.z = lax.div(index, 4)

    def at(self, z=None, y=None, x=None, core=None):
        z = self.z if z is None else z
        y = self.y if y is None else y
        x = self.x if x is None else x
        return (z * 4 + y * 2 + x, self.core if core is None else core)

    def z_after(self, step):
        return lax.rem(self.z + step, 4)

    def z_peer(self, step):
        return self.at(z=self.z_after(step))

    def y_peer(self):
        return self.at(y=1 - self.y)

    def x_peer(self):
        return self.at(x=1 - self.x)

    def core_peer(self):
        return self.at(core=1 - self.core)

    def greet(self):
        ready = pltpu.get_barrier_semaphore()
        peers = [self.z_peer(1), self.z_peer(2), self.z_peer(3)]
        peers += [self.y_peer(), self.x_peer(), self.core_peer()]
        for peer in peers:
            pl.semaphore_signal(ready, inc=1, device_id=peer, device_id_type=MESH)
        pl.semaphore_wait(ready, len(peers))


class Moves:
    def __init__(self, send, recv, first):
        self.send, self.recv, self.first, self.made = send, recv, first, {}

    def add(self, name, src, dst, peer):
        slot = self.first + len(self.made)
        self.made[name] = lambda: pltpu.make_async_remote_copy(
            src_ref=src(),
            dst_ref=dst(),
            send_sem=self.send.at[slot],
            recv_sem=self.recv.at[slot],
            device_id=peer(),
            device_id_type=MESH,
        )

    def start(self, *names):
        for name in names:
            self.made[name]().start()

    def landed(self, *names):
        for name in names:
            self.made[name]().wait_recv()

    def sent(self):
        for make in self.made.values():
            make().wait_send()


GATHER_MOVES = 11


class Gather(Moves):
    def __init__(self, me, src, out, local, send, recv, slot, first, half):
        super().__init__(send, recv, slot * GATHER_MOVES)
        self.me, self.src, self.out = me, src, out
        self.local_sem = local.at[slot]
        cut = half * 2 // 3 if half == 384 else half // 2
        start = first + me.core * half
        mine = aligned(start, half)
        a, b = aligned(start, cut), aligned(start + cut, half - cut)
        own = lambda: out.at[me.z, me.y, me.x, :, mine]
        self.mine, self.own = mine, own
        for step in (1, 2, 3):
            self.add(("z", step), lambda: src.at[:, mine], own, lambda step=step: me.z_peer(step))

        def same(name, view, peer):
            self.add(name, view, view, peer)

        same("a1", lambda: out.at[:, me.y, me.x, :, a], me.y_peer)
        same("b1", lambda: out.at[:, me.y, me.x, :, b], me.x_peer)
        same("a2", lambda: out.at[:, :, me.x, :, a], me.x_peer)
        same("b2", lambda: out.at[:, me.y, :, :, b], me.y_peer)
        same("near a", lambda: out.at[:, :, me.x, :, a], me.core_peer)
        same("near b", lambda: out.at[:, me.y, :, :, b], me.core_peer)
        same("far a", lambda: out.at[:, :, 1 - me.x, :, a], me.core_peer)
        same("far b", lambda: out.at[:, 1 - me.y, :, :, b], me.core_peer)

    def local(self):
        return pltpu.make_async_copy(self.src.at[:, self.mine], self.own(), self.local_sem)

    def step(self, number):
        if number == 0:
            self.start(("z", 2), ("z", 1), ("z", 3))
            self.local().start()
        if number == 1:
            self.local().wait()
            self.landed(("z", 1), ("z", 2), ("z", 3))
            self.start("a1", "b1")
        if number == 2:
            self.landed("a1", "b1")
            self.start("a2", "b2", "near a", "near b")
        if number == 3:
            self.landed("a2", "b2")
            self.start("far a", "far b")
        if number == 4:
            self.landed("near a", "near b", "far a", "far b")
            self.sent()


class VectorGather(Moves):
    def __init__(self, me, src, out, local, send, recv, first):
        super().__init__(send, recv, first)
        own = lambda: out.at[me.z, me.y, me.x]
        self.copy = lambda: pltpu.make_async_copy(src, own(), local)
        for step in (1, 2, 3):
            self.add(("z", step), lambda: src, own, lambda step=step: me.z_peer(step))
        self.add("y", lambda: out.at[:, me.y, me.x], lambda: out.at[:, me.y, me.x], me.y_peer)
        self.add("x", lambda: out.at[:, :, me.x], lambda: out.at[:, :, me.x], me.x_peer)

    def step(self, number):
        if number == 0:
            self.copy().start()
            self.start(("z", 1), ("z", 2), ("z", 3))
        if number == 1:
            self.copy().wait()
            self.landed(("z", 1), ("z", 2), ("z", 3))
            self.start("y")
        if number == 2:
            self.landed("y")
            self.start("x")
        if number == 3:
            self.landed("x")
            self.sent()


REDUCE_MOVES = 9


class Reduce(Moves):
    def __init__(self, me, grads, total, boxes, send, recv, slot, first, half, group):
        super().__init__(send, recv, slot * REDUCE_MOVES)
        from_core, from_a1, from_b1, from_a2, from_b2, from_z = boxes
        self.me, self.grads, self.total, self.boxes = me, grads, total, boxes
        cut = half * 2 // 3 if half == 384 else half // 2
        start = first + me.core * half
        self.half = half
        self.mine = mine = aligned(start, half)
        theirs = aligned(first + (1 - me.core) * half, half)
        self.a, self.b = a, b = aligned(start, cut), aligned(start + cut, half - cut)
        self.group = group
        self.add("core", lambda: grads.at[:, :, :, :, theirs], lambda: from_core, me.core_peer)
        self.add("a1", lambda: grads.at[:, 1 - me.y, :, :, a], lambda: from_a1, me.y_peer)
        self.add("b1", lambda: grads.at[:, :, 1 - me.x, :, b], lambda: from_b1, me.x_peer)
        self.add("a2", lambda: grads.at[:, me.y, 1 - me.x, :, a], lambda: from_a2, me.x_peer)
        self.add("b2", lambda: grads.at[:, 1 - me.y, me.x, :, b], lambda: from_b2, me.y_peer)
        for step in (1, 2, 3):
            self.add(
                ("z", step),
                lambda step=step: grads.at[me.z_after(step), me.y, me.x, :, mine],
                lambda step=step: from_z.at[step - 1],
                lambda step=step: me.z_peer(step),
            )
        self.add("last", lambda: total.at[group, :, mine], lambda: total.at[group, :, mine], me.core_peer)

    def step(self, number):
        me, grads = self.me, self.grads
        from_core, from_a1, from_b1, from_a2, from_b2, from_z = self.boxes
        a, b, mine = self.a, self.b, self.mine

        def plus(left, right):
            return (left.astype(F32) + right.astype(F32)).astype(BF)

        if number == 0:
            self.start("core")
        if number == 1:
            self.landed("core")

            @pl.loop(0, 4)
            def _(z):
                for y in range(2):
                    for x in range(2):
                        grads[z, y, x, :, mine] = plus(
                            grads[z, y, x, :, mine], from_core[z, y, x]
                        )

            self.start("a1", "b1")
        if number == 2:
            self.landed("a1", "b1")

            @pl.loop(0, 4)
            def _(z):
                for k in range(2):
                    grads[z, me.y, k, :, a] = plus(grads[z, me.y, k, :, a], from_a1[z, k])
                    grads[z, k, me.x, :, b] = plus(grads[z, k, me.x, :, b], from_b1[z, k])

            self.start("a2", "b2")
        if number == 3:
            self.landed("a2", "b2")

            @pl.loop(0, 4)
            def _(z):
                grads[z, me.y, me.x, :, a] = plus(grads[z, me.y, me.x, :, a], from_a2[z])
                grads[z, me.y, me.x, :, b] = plus(grads[z, me.y, me.x, :, b], from_b2[z])

            self.start(("z", 2), ("z", 1), ("z", 3))
        if number == 4:
            self.landed(("z", 1), ("z", 2), ("z", 3))
            terms = [from_z[k].astype(F32) for k in range(3)]
            own = grads[me.z, me.y, me.x, :, mine].astype(F32)
            self.total[self.group, :, mine] = (own + terms[0]) + (terms[1] + terms[2])
            self.start("last")
        if number == 5:
            self.landed("last")
            self.sent()


def boxes_for(half):
    cut = half * 2 // 3 if half == 384 else half // 2
    return [
        pltpu.VMEM((4, 2, 2, PIECE, half), BF),
        pltpu.VMEM((4, 2, PIECE, cut), BF),
        pltpu.VMEM((4, 2, PIECE, half - cut), BF),
        pltpu.VMEM((4, PIECE, cut), BF),
        pltpu.VMEM((4, PIECE, half - cut), BF),
        pltpu.VMEM((3, PIECE, half), BF),
    ]


class VectorSum(Moves):
    def __init__(self, me, table, boxes, send, recv, first):
        super().__init__(send, recv, first)
        self.table, self.boxes = table, boxes
        for k, peer in enumerate((me.core_peer, me.x_peer, me.y_peer)):
            self.add(k, lambda k=k: table.at[k], lambda k=k: boxes.at[k], peer)
        for step in (1, 2, 3):
            self.add(
                ("z", step),
                lambda: table.at[3],
                lambda step=step: boxes.at[2 + step],
                lambda step=step: me.z_peer(step),
            )

    def step(self, number):
        table, boxes = self.table, self.boxes
        if 1 <= number <= 3:
            self.landed(number - 1)
            table[number] = table[number - 1] + boxes[number - 1]
        if number < 3:
            self.start(number)
        if number == 3:
            self.start(("z", 1), ("z", 2), ("z", 3))
        if number == 4:
            self.landed(("z", 1), ("z", 2), ("z", 3))
            table[4] = (table[3] + boxes[3]) + (boxes[4] + boxes[5])
            self.sent()


def normalized(values):
    average = jnp.mean(values, axis=-1, keepdims=True)
    centered = values - average
    spread = jnp.mean(centered * centered, axis=-1, keepdims=True)
    scale = lax.rsqrt(spread + 1e-06)
    return centered * scale, scale


def norm_grad(grad_scaled, unit, scale):
    mean_grad = jnp.mean(grad_scaled, axis=-1, keepdims=True)
    mean_both = jnp.mean(grad_scaled * unit, axis=-1, keepdims=True)
    return scale * (grad_scaled - mean_grad - unit * mean_both)


def tile_of(whole, group_cols):
    return whole[:, :, :, :, aligned(group_cols, WIDTH)].reshape(WIDTH, WIDTH)


def blocks(count, body):
    @pl.loop(0, SEQ // count)
    def _(step):
        body(aligned(step * count, count, count))


N_GATHERS = 8
FORWARD_SENDS = N_GATHERS * GATHER_MOVES + 5


def forward_kernel(
    tok, seg, sh_qkvo, sh_in, sh_out, pack, pick, rows_of,
    result, w_qkvo, w_in, w_out, qkv_out, att_out, lse_out, normed_out, mid_out, second_out, act_out, slope_out, vec, stats,
    b_qkvo, b_in, b_out, got, qkv, att, lse, normed, mid, second, act, slope, res, qa, ka, va, send, recv, local,
):
    me = Place()
    me.greet()
    vectors = VectorGather(me, pack, got, local.at[8], send, recv, N_GATHERS * GATHER_MOVES)
    spans = [(sh_qkvo, b_qkvo, 768 * k, 384) for k in range(4)]
    spans += [(sh_in, b_in, 0, 768), (sh_in, b_in, 1536, 768)]
    spans += [(sh_out, b_out, 0, 768), (sh_out, b_out, 1536, 768)]
    chunks = [
        Gather(me, src, out, local, send, recv, k, first, half)
        for k, (src, out, first, half) in enumerate(spans)
    ]

    def tick(number):
        for k, chunk in enumerate(chunks):
            if 0 <= number - k <= 4:
                chunk.step(number - k)

    saves = []

    def save(src, dst):
        slot = 9 + len(saves)
        make = lambda: pltpu.make_async_copy(src, dst, local.at[slot])
        saves.append(make)
        make().start()

    vectors.step(0)
    tick(0)
    vectors.step(1)
    tick(1)
    vectors.step(2)
    tick(2)
    vectors.step(3)
    spread = dg(got[...].reshape(256, 128), pick[...], 1, 0)
    table = jnp.zeros((16, WIDTH), F32)
    for k in range(16):
        table += spread[16 * k : 16 * k + 16] * rows_of[k : k + 1]
    vec[...] = table
    stats[...] = jnp.zeros_like(stats)
    lse[...] = jnp.zeros_like(lse)

    def tally(k, piece, valid):
        stats[k : k + 1] += jnp.sum(piece * piece * valid, axis=0, keepdims=True)

    def valid_of(rows):
        return jnp.where(seg[rows] != 0, 1.0, 0.0)

    def first_norm(rows):
        stream = tok[rows].astype(F32)
        valid = valid_of(rows)
        tally(0, stream, valid)
        stats[4:5] += jnp.sum(jnp.broadcast_to(valid, stream.shape), axis=0, keepdims=True)
        unit, _ = normalized(stream)
        normed[rows] = (unit * vec[0:1] + vec[1:2]).astype(BF)

    blocks(BLOCK, first_norm)
    save(normed, normed_out)
    tick(3)
    tick(4)
    tick(5)
    tick(6)
    for k, bias in enumerate((2, None, 3)):
        def project(rows, k=k, bias=bias):
            made = dg(normed[rows], tile_of(b_qkvo, WIDTH * k), 1, 1)
            if bias is not None:
                made = made + vec[bias : bias + 1]
            qkv[rows, WIDTH * k : WIDTH * k + WIDTH] = made.astype(BF)

        blocks(512, project)
    tick(7)
    save(qkv, qkv_out)
    save(b_qkvo, w_qkvo)

    lane = lanes(SEQ)
    hot = seg[...] == lane
    for h in range(2):
        qa[h, :, 128:] = jnp.where(hot, 1.0, 0.0).astype(BF)
    ka[:, 128:] = jnp.where(hot | (lane > 8), 0.0, -1e30).astype(BF)
    va[:, 128:] = jnp.ones((SEQ, 128), BF)

    @pl.loop(0, WIDTH // 128)
    def _(pair):
        @pl.when(pair == 2)
        def _():
            tick(8)

        @pl.when(pair == 5)
        def _():
            tick(9)

        query = qkv[:, aligned(pair * 128, 128)].astype(F32) * 0.125
        lane = lanes(SEQ)
        qa[0, :, :128] = jnp.where(lane < 64, query, 0.0).astype(BF)
        qa[1, :, :128] = jnp.where(lane < 64, 0.0, query).astype(BF)
        ka[:, :128] = qkv[:, aligned(WIDTH + pair * 128, 128)]
        va[:, :128] = qkv[:, aligned(2 * WIDTH + pair * 128, 128)]
        lane = lanes(BLOCK)
        for step in range(SEQ // BLOCK):
            rows = slice(step * BLOCK, (step + 1) * BLOCK)
            mixed = []
            for h in range(2):
                scores = dg(qa[h, rows], ka[...], 1, 1)
                largest = jnp.max(scores, axis=1, keepdims=True)
                prob = jnp.exp(scores - largest).astype(BF)
                both = dg(prob, va[...], 1, 0)
                total = both[:, 128:]
                mixed.append(both[:, :128] / total)
                lse[rows] = jnp.where(lane == 2 * pair + h, largest + jnp.log(total), lse[rows])
            att[rows, aligned(pair * 128, 128)] = jnp.where(lane < 64, mixed[0], mixed[1]).astype(BF)

    save(att, att_out)
    save(lse, lse_out)

    def second_norm(rows):
        valid = valid_of(rows)
        branch = dg(att[rows], tile_of(b_qkvo, 3 * WIDTH), 1, 1) + vec[4:5]
        middle = tok[rows].astype(F32) + branch
        tally(1, branch, valid)
        tally(2, middle, valid)
        mid[rows] = middle
        unit, _ = normalized(middle)
        second[rows] = (unit * vec[6:7] + vec[7:8]).astype(BF)

    blocks(BLOCK, second_norm)
    save(mid, mid_out)
    save(second, second_out)
    save(b_in, w_in)
    tick(10)
    for k in range(4):
        def expand(rows, k=k):
            cols = slice(k * WIDTH, (k + 1) * WIDTH)
            hidden = dg(second[rows], tile_of(b_in, k * WIDTH), 1, 1) + vec[8 + k : 9 + k]
            phi = 0.5 + 0.5 * lax.erf(hidden * (0.5**0.5))
            bell = jnp.exp(hidden * hidden * -0.5) * 0.3989422804014327
            act[rows, cols] = (hidden * phi).astype(BF)
            slope[rows, cols] = (phi + hidden * bell).astype(BF)

        blocks(BLOCK, expand)
    save(act, act_out)
    save(slope, slope_out)
    tick(11)
    save(b_out, w_out)

    def contract(rows):
        valid = valid_of(rows)
        ffn_out = dg(act[rows], b_out[...].reshape(WIDTH, 4 * WIDTH), 1, 1) + vec[5:6]
        tally(3, ffn_out, valid)
        res[rows] = (mid[rows] + ffn_out).astype(BF)

    blocks(BLOCK, contract)
    save(res, result)
    for make in saves:
        make().wait()


def forward_call(tok, seg, sh_qkvo, sh_in, sh_out, pack):
    whole = jax.ShapeDtypeStruct((4, 2, 2, PIECE, 4 * WIDTH), BF)
    wide = lambda k, kind: jax.ShapeDtypeStruct((SEQ, k), kind)
    outs = [
        wide(WIDTH, BF), whole, whole, whole, wide(3 * WIDTH, BF), wide(WIDTH, BF), wide(128, F32), wide(WIDTH, BF),
        wide(WIDTH, F32), wide(WIDTH, BF), wide(4 * WIDTH, BF), wide(4 * WIDTH, BF),
        jax.ShapeDtypeStruct((16, WIDTH), F32), jax.ShapeDtypeStruct((8, WIDTH), F32),
    ]
    vmem, anywhere = pl.BlockSpec(memory_space=pltpu.VMEM), pl.BlockSpec(memory_space=pl.ANY)
    spot = lambda shape: pltpu.VMEM(shape.shape, shape.dtype)
    scratch = [spot(whole)] * 3 + [pltpu.VMEM((4, 2, 2, 16, 128), BF)]
    scratch += [spot(shape) for shape in outs[4:5] + outs[5:6] + outs[6:7] + outs[7:8] + outs[8:12]]
    scratch += [spot(outs[0]), pltpu.VMEM((2, SEQ, 256), BF), pltpu.VMEM((SEQ, 256), BF), pltpu.VMEM((SEQ, 256), BF)]
    scratch += [pltpu.SemaphoreType.DMA((FORWARD_SENDS,))] * 2 + [pltpu.SemaphoreType.DMA((22,))]
    place = np.arange(WIDTH)
    pick = jnp.asarray((place[None, :] % PIECE == np.arange(128)[:, None]), BF)
    rows_of = jnp.asarray((place[None, :] // PIECE == np.arange(16)[:, None]), F32)
    return pl.pallas_call(
        forward_kernel,
        out_shape=outs,
        in_specs=[vmem] * 8,
        out_specs=[anywhere] * 12 + [vmem] * 2,
        scratch_shapes=scratch,
        compiler_params=pltpu.CompilerParams(
            collective_id=1, has_side_effects=True, vmem_limit_bytes=60 * 2**20
        ),
        name="forward",
    )(tok, seg, sh_qkvo, sh_in, sh_out, pack, pick, rows_of)


def packed_inputs(
    weight_query, weight_key, weight_value, weight_output, weight_inner, weight_outer,
    bias_query, bias_value, bias_output, bias_inner, bias_outer, gain_attn, shift_attn, gain_ffn, shift_ffn,
):
    four = (weight_query, weight_key, weight_value, weight_output)
    sh_qkvo = jnp.concatenate([w.T for w in four], axis=1)
    sh_in = weight_inner.T.reshape(4, PIECE, WIDTH).transpose(1, 0, 2).reshape(PIECE, 4 * WIDTH)
    sh_out = weight_outer.T.reshape(PIECE, 16, 4, PIECE).transpose(0, 2, 1, 3).reshape(PIECE, 4 * WIDTH)
    vectors = (gain_attn, shift_attn, bias_query, bias_value, bias_output, bias_outer, gain_ffn, shift_ffn)
    pack = jnp.concatenate([jnp.stack(vectors), bias_inner.reshape(4, PIECE)])
    pack = jnp.pad(pack, ((0, 4), (0, 128 - PIECE)))
    return sh_qkvo, sh_in, sh_out, pack


N_REDUCES = 8
BACKWARD_SENDS = N_REDUCES * REDUCE_MOVES + 6


def three_terms(values, lane, first, rest):
    high = values.astype(BF).astype(F32)
    left = values - high
    middle = left.astype(BF).astype(F32)
    low = left - middle
    for k, term in enumerate((high, middle, low)):
        rest = jnp.where(lane == first + k, term, rest)
    return rest.astype(BF)


def backward_kernel(
    tok, cot, seg, vec, stats, w_qkvo, w_in, w_out, qkv_in, att_in, lse_in, normed_in, mid_in, second_in, act_in, slope_in,
    grad_tok, total, sums,
    big_a, big_b, first, middle, last, small_a, small_b, mid, lse, qa, ka, va, da, acc, table, tables, send, recv, local, *boxes,
):
    me = Place()
    me.greet()
    spans = [(last, 0, 768, 2), (last, 1536, 768, 2), (middle, 0, 768, 1), (middle, 1536, 768, 1)]
    spans += [(first, 2304, 384, 0)] + [(first, 768 * k, 384, 0) for k in range(3)]
    chunks = [
        Reduce(me, grads, total, boxes[6 * k : 6 * k + 6], send, recv, k, start, half, group)
        for k, (grads, start, half, group) in enumerate(spans)
    ]
    vectors = VectorSum(me, table, tables, send, recv, N_REDUCES * REDUCE_MOVES)
    u01, u23, i01, i23, out, que, key, val = chunks

    def load(slot, src, dst):
        make = lambda: pltpu.make_async_copy(src(), dst(), local.at[slot])
        make().start()
        return make

    act_here = load(0, lambda: act_in, lambda: big_a)
    w_out_here = load(1, lambda: w_out, lambda: first)
    slope_here = load(2, lambda: slope_in, lambda: big_b)
    w_in_here = load(3, lambda: w_in, lambda: middle)
    mid_here = load(4, lambda: mid_in, lambda: mid)
    second_here = load(5, lambda: second_in, lambda: small_a)
    att_here = load(6, lambda: att_in, lambda: small_b)
    lse_here = load(7, lambda: lse_in, lambda: lse)

    sums_ref = table.at[0]
    sums_ref[...] = jnp.zeros_like(sums_ref)
    sums_ref[12:20] = stats[...]

    def tally(row, values):
        sums_ref[row : row + 1] += jnp.sum(values, axis=0, keepdims=True)

    def piece(k):
        return slice(k * WIDTH, (k + 1) * WIDTH)

    def store_grad(whole, k, left, right):
        made = dg(left, right, 0, 0).astype(BF)
        whole[:, :, :, :, piece(k)] = made.reshape(4, 2, 2, PIECE, WIDTH)

    act_here().wait()
    store_grad(last, 0, cot[...], big_a[:, piece(0)])
    store_grad(last, 1, cot[...], big_a[:, piece(1)])
    u01.step(0)
    store_grad(last, 2, cot[...], big_a[:, piece(2)])
    store_grad(last, 3, cot[...], big_a[:, piece(3)])
    u01.step(1)
    u23.step(0)
    qkv_here = load(8, lambda: qkv_in, lambda: big_a.at[:, 0 : 3 * WIDTH])
    w_out_here().wait()
    slope_here().wait()
    for k in range(4):
        def through_gelu(rows, k=k):
            grad_active = dg(cot[rows], tile_of(first, k * WIDTH), 1, 0)
            grad_hidden = (grad_active * big_b[rows, piece(k)].astype(F32)).astype(BF)
            big_b[rows, piece(k)] = grad_hidden
            tally(8 + k, grad_hidden.astype(F32))

        blocks(BLOCK, through_gelu)
    u01.step(2)
    u23.step(1)
    o_cols = slice(3 * WIDTH, 4 * WIDTH)
    w_o_here = load(
        9, lambda: w_qkvo.at[:, :, :, :, o_cols], lambda: first.at[:, :, :, :, o_cols]
    )
    w_in_here().wait()
    mid_here().wait()

    def ffn_norm_back(rows):
        grad_second = dg(big_b[rows, piece(0)], tile_of(middle, 0), 1, 0)
        for k in range(1, 4):
            grad_second += dg(big_b[rows, piece(k)], tile_of(middle, k * WIDTH), 1, 0)
        unit, scale = normalized(mid[rows])
        tally(6, grad_second * unit)
        tally(7, grad_second)
        upper = cot[rows].astype(F32)
        tally(5, upper)
        grad_middle = upper + norm_grad(grad_second * vec[6:7], unit, scale)
        mid[rows] = grad_middle
        tally(4, grad_middle.astype(BF).astype(F32))

    blocks(BLOCK, ffn_norm_back)
    u01.step(3)
    u23.step(2)
    second_here().wait()
    store_grad(middle, 0, big_b[:, piece(0)], small_a[...])
    store_grad(middle, 1, big_b[:, piece(1)], small_a[...])
    i01.step(0)
    store_grad(middle, 2, big_b[:, piece(2)], small_a[...])
    store_grad(middle, 3, big_b[:, piece(3)], small_a[...])
    i01.step(1)
    i23.step(0)
    u01.step(4)
    u23.step(3)
    tok_here = load(10, lambda: tok, lambda: small_a)
    normed_here = load(11, lambda: normed_in, lambda: big_b.at[:, o_cols])
    w_o_here().wait()
    qkv_here().wait()

    def to_attended(rows):
        big_a[rows, o_cols] = dg(mid[rows].astype(BF), tile_of(first, 3 * WIDTH), 1, 0).astype(BF)

    blocks(512, to_attended)
    att_here().wait()
    store_grad(first, 3, mid[...].astype(BF), small_b[...])
    u01.step(5)
    out.step(0)
    lse_here().wait()

    lane = lanes(SEQ)
    hot = seg[...] == lane
    ones = (lane > 8) & (lane < 12)
    ka[:, 128:] = jnp.where(ones, 1.0, jnp.where(hot | (lane > 8), 0.0, -1e30)).astype(BF)
    va[:, 128:] = jnp.where(lane < 3, 1.0, 0.0).astype(BF)

    w_qkv_cols = slice(0, 3 * WIDTH)
    w_qkv_make = lambda: pltpu.make_async_copy(
        w_qkvo.at[:, :, :, :, w_qkv_cols], last.at[:, :, :, :, w_qkv_cols], local.at[12]
    )

    @pl.loop(0, WIDTH // 128)
    def _(pair):
        @pl.when(pair == 1)
        def _():
            u23.step(4)
            i01.step(2)
            i23.step(1)

        @pl.when(pair == 2)
        def _():
            u23.step(5)
            w_qkv_make().start()
            i01.step(3)
            i23.step(2)
            out.step(1)

        @pl.when(pair == 3)
        def _():
            i01.step(4)
            i23.step(3)
            out.step(2)

        @pl.when(pair == 4)
        def _():
            i01.step(5)
            i23.step(4)
            out.step(3)

        @pl.when(pair == 5)
        def _():
            i23.step(5)
            out.step(4)

        spot = pair * 128
        lane = lanes(SEQ)
        hot = jnp.where(seg[...] == lane, 1.0, 0.0)
        query = big_a[:, aligned(spot, 128)].astype(F32) * 0.125
        ka[:, :128] = big_a[:, aligned(WIDTH + spot, 128)]
        va[:, :128] = big_a[:, aligned(2 * WIDTH + spot, 128)]
        upper = big_a[:, aligned(3 * WIDTH + spot, 128)].astype(F32)
        both = small_b[:, aligned(spot, 128)].astype(F32) * upper
        for h in range(2):
            mine = (lane < 64) if h == 0 else (lane >= 64)
            qa[h, :, :128] = jnp.where(mine, query, 0.0).astype(BF)
            da[h, :, :128] = jnp.where(mine, upper, 0.0).astype(BF)
            level = jnp.sum(jnp.where(lane == 2 * pair + h, lse[...], 0.0), axis=1, keepdims=True)
            qa[h, :, 128:] = three_terms(jnp.broadcast_to(-level, hot.shape), lane, 9, hot)
            weighted = jnp.sum(jnp.where(mine, both, 0.0), axis=1, keepdims=True)
            da[h, :, 128:] = three_terms(
                jnp.broadcast_to(-weighted, hot.shape), lane, 0, jnp.zeros_like(hot)
            )
        lane_b = lanes(BLOCK)
        for step in range(SEQ // BLOCK):
            rows = slice(step * BLOCK, (step + 1) * BLOCK)
            for_keys, for_values = [], []
            for h in range(2):
                prob = jnp.exp(dg(ka[rows], qa[h], 1, 1))
                grad_score = (prob * dg(va[rows], da[h], 1, 1)).astype(BF)
                for_values.append(dg(prob.astype(BF), da[h, :, :128], 1, 0))
                for_keys.append(dg(grad_score, qa[h, :, :128], 1, 0))
                for_queries = dg(grad_score, ka[rows, :128], 0, 0)
                acc[h] = for_queries if step == 0 else acc[h] + for_queries
            big_b[rows, aligned(WIDTH + spot, 128)] = (for_keys[0] + for_keys[1]).astype(BF)
            big_b[rows, aligned(2 * WIDTH + spot, 128)] = (for_values[0] + for_values[1]).astype(BF)
        big_b[:, aligned(spot, 128)] = (jnp.where(lane < 64, acc[0], acc[1]) * 0.125).astype(BF)

    out.step(5)
    normed_here().wait()
    store_grad(first, 0, big_b[:, piece(0)], big_b[:, o_cols])
    que.step(0)
    store_grad(first, 1, big_b[:, piece(1)], big_b[:, o_cols])
    que.step(1)
    key.step(0)
    store_grad(first, 2, big_b[:, piece(2)], big_b[:, o_cols])
    key.step(1)
    val.step(0)
    tok_here().wait()
    w_qkv_make().wait()

    @pl.loop(0, SEQ // BLOCK)
    def _(step):
        rows = aligned(step * BLOCK, BLOCK, BLOCK)
        grad_normed = dg(big_b[rows, piece(0)], tile_of(last, 0), 1, 0)
        for k in range(1, 3):
            grad_normed += dg(big_b[rows, piece(k)], tile_of(last, k * WIDTH), 1, 0)
        tally(2, big_b[rows, piece(0)].astype(F32))
        tally(3, big_b[rows, piece(2)].astype(F32))
        unit, scale = normalized(small_a[rows].astype(F32))
        tally(0, grad_normed * unit)
        tally(1, grad_normed)
        grad_stream = mid[rows] + norm_grad(grad_normed * vec[0:1], unit, scale)
        small_b[rows] = grad_stream.astype(BF)

        @pl.when(step == 0)
        def _():
            que.step(2)
            val.step(1)

        @pl.when(step == 2)
        def _():
            que.step(3)
            key.step(2)

    save = load(13, lambda: small_b, lambda: grad_tok)
    vectors.step(0)
    val.step(2)
    key.step(3)
    vectors.step(1)
    que.step(4)
    vectors.step(2)
    val.step(3)
    vectors.step(3)
    key.step(4)
    que.step(5)
    vectors.step(4)
    sums[...] = table[4]
    val.step(4)
    key.step(5)
    val.step(5)
    save().wait()


def backward_call(tok, cot, seg, vec, stats, *kept):
    vmem, anywhere = pl.BlockSpec(memory_space=pltpu.VMEM), pl.BlockSpec(memory_space=pl.ANY)
    whole = pltpu.VMEM((4, 2, 2, PIECE, 4 * WIDTH), BF)
    wide = lambda k, kind: pltpu.VMEM((SEQ, k), kind)
    scratch = [wide(4 * WIDTH, BF)] * 2 + [whole] * 3 + [wide(WIDTH, BF)] * 2
    scratch += [wide(WIDTH, F32), wide(128, F32)]
    scratch += [pltpu.VMEM((2, SEQ, 256), BF), wide(256, BF), wide(256, BF), pltpu.VMEM((2, SEQ, 256), BF)]
    scratch += [pltpu.VMEM((2, SEQ, 128), F32), pltpu.VMEM((5, 24, WIDTH), F32), pltpu.VMEM((6, 24, WIDTH), F32)]
    scratch += [pltpu.SemaphoreType.DMA((BACKWARD_SENDS,))] * 2 + [pltpu.SemaphoreType.DMA((14,))]
    for half in [768] * 4 + [384] * 4:
        scratch += boxes_for(half)
    return pl.pallas_call(
        backward_kernel,
        out_shape=[
            jax.ShapeDtypeStruct((SEQ, WIDTH), BF),
            jax.ShapeDtypeStruct((3, PIECE, 4 * WIDTH), F32),
            jax.ShapeDtypeStruct((24, WIDTH), F32),
        ],
        in_specs=[anywhere] + [vmem] * 4 + [anywhere] * 11,
        out_specs=[anywhere, vmem, vmem],
        scratch_shapes=scratch,
        compiler_params=pltpu.CompilerParams(
            collective_id=2, has_side_effects=True, vmem_limit_bytes=60 * 2**20
        ),
        name="backward",
    )(tok, cot, seg, vec, stats, *kept)


def fast_body(tokens, segment_ids, cotangent, *params):
    tok, cot = tokens.reshape(SEQ, WIDTH), cotangent.reshape(SEQ, WIDTH)
    seg = segment_ids.reshape(SEQ, 1)
    made = forward_call(tok, seg, *packed_inputs(*params))
    result, kept, vec, stats = made[0], made[1:12], made[12], made[13]
    grad_tok, total, sums = backward_call(tok, cot, seg, vec, stats, *kept)
    index = lax.axis_index("fsdp")
    own = lax.dynamic_slice_in_dim(sums[:12], index * PIECE, PIECE, 1)
    grad_gain_attn, grad_shift_attn, grad_query, grad_value, grad_output, grad_outer, grad_gain_ffn, grad_shift_ffn = own[:8]
    grad_inner = own[8:12].reshape(4 * PIECE)
    squares = jnp.sum(sums[12:16], axis=1)
    rms_stats = jnp.sqrt(squares / (sums[16, 0] * WIDTH))
    four = [total[0, :, k * WIDTH : (k + 1) * WIDTH].T for k in range(4)]
    inner = total[1].reshape(PIECE, 4, WIDTH).transpose(2, 1, 0).reshape(WIDTH, 4 * PIECE)
    outer = total[2].reshape(PIECE, 4, 16, PIECE).transpose(2, 1, 3, 0).reshape(4 * WIDTH, PIECE)
    return (
        result.reshape(tokens.shape), grad_tok.reshape(tokens.shape), *four, inner, outer,
        grad_query, grad_value, grad_output, grad_inner, grad_outer,
        grad_gain_attn, grad_shift_attn, grad_gain_ffn, grad_shift_ffn, rms_stats,
    )


def scaled(values, gain_vec):
    average = jnp.mean(values, axis=-1, keepdims=True)
    centered = values - average
    spread = jnp.mean(centered * centered, axis=-1, keepdims=True)
    return centered * lax.rsqrt(spread + 1e-06) * gain_vec


def matmul(operand, matrix):
    return jnp.dot(operand, matrix, preferred_element_type=jnp.float32)


def over_rows(operand, other):
    return lax.dot_general(
        operand, other, (((0,), (0,)), ((), ())), preferred_element_type=jnp.float32
    )


def against(operand, matrix):
    return lax.dot_general(
        operand, matrix, (((1,), (1,)), ((), ())), preferred_element_type=jnp.float32
    )


def pair_of(block, offset, seq_len):
    return lax.dynamic_slice_in_dim(block, offset, 2 * HD, 1).reshape(seq_len, 2, HD)


def masked_scores(query_pair, key_pair, same_doc, factor):
    scores = (
        jnp.einsum("qhd,khd->hqk", query_pair, key_pair, preferred_element_type=jnp.float32)
        * factor
    )
    return jnp.where(same_doc, scores, -1e30)


def attend_forward(queries, key_rows, value_rows, doc_ids):
    seq_len, features = queries.shape
    pair_width = 2 * HD
    factor = 1.0 / math.sqrt(HD)
    same_doc = (doc_ids[:, None] == doc_ids[None, :])[None]

    def one_pair(which, buffers):
        attended, logsum = buffers
        offset = which * pair_width
        query_pair = pair_of(queries, offset, seq_len)
        key_pair = pair_of(key_rows, offset, seq_len)
        value_pair = pair_of(value_rows, offset, seq_len)
        scores = masked_scores(query_pair, key_pair, same_doc, factor)
        largest = jnp.max(scores, axis=-1, keepdims=True)
        exponent = jnp.exp(scores - largest)
        denominator = jnp.sum(exponent, axis=-1, keepdims=True)
        probability = (exponent / denominator).astype(jnp.bfloat16)
        mixed_pair = jnp.einsum(
            "hqk,khd->qhd", probability, value_pair, preferred_element_type=jnp.float32
        )
        attended = lax.dynamic_update_slice_in_dim(
            attended, mixed_pair.reshape(seq_len, pair_width), offset, 1
        )
        logsum = lax.dynamic_update_slice_in_dim(
            logsum, (largest + jnp.log(denominator))[:, :, 0], which * 2, 0
        )
        return (attended, logsum)

    initial = (
        jnp.zeros((seq_len, features), jnp.float32),
        jnp.zeros((features // HD, seq_len), jnp.float32),
    )
    return lax.fori_loop(0, features // pair_width, one_pair, initial)


def attend_backward(queries, key_rows, value_rows, upstream, logsum, doc_ids):
    seq_len, features = queries.shape
    pair_width = 2 * HD
    factor = 1.0 / math.sqrt(HD)
    same_doc = (doc_ids[:, None] == doc_ids[None, :])[None]

    def one_pair(which, buffers):
        grad_queries, grad_keys, grad_values = buffers
        offset = which * pair_width
        query_pair = pair_of(queries, offset, seq_len)
        key_pair = pair_of(key_rows, offset, seq_len)
        value_pair = pair_of(value_rows, offset, seq_len)
        upper_pair = pair_of(upstream, offset, seq_len)
        logsum_pair = lax.dynamic_slice_in_dim(logsum, which * 2, 2, 0)
        scores = masked_scores(query_pair, key_pair, same_doc, factor)
        probability = jnp.exp(scores - logsum_pair[:, :, None])
        rounded = probability.astype(jnp.bfloat16)
        value_part = jnp.einsum(
            "hqk,qhd->khd", rounded, upper_pair, preferred_element_type=jnp.float32
        )
        prob_grad = jnp.einsum(
            "qhd,khd->hqk", upper_pair, value_pair, preferred_element_type=jnp.float32
        )
        weighted = jnp.sum(probability * prob_grad, axis=-1, keepdims=True)
        score_grad = (probability * (prob_grad - weighted)).astype(jnp.bfloat16)
        query_part = (
            jnp.einsum("hqk,khd->qhd", score_grad, key_pair, preferred_element_type=jnp.float32)
            * factor
        )
        key_part = (
            jnp.einsum("hqk,qhd->khd", score_grad, query_pair, preferred_element_type=jnp.float32)
            * factor
        )
        grad_queries = lax.dynamic_update_slice_in_dim(
            grad_queries, query_part.reshape(seq_len, pair_width), offset, 1
        )
        grad_keys = lax.dynamic_update_slice_in_dim(
            grad_keys, key_part.reshape(seq_len, pair_width), offset, 1
        )
        grad_values = lax.dynamic_update_slice_in_dim(
            grad_values, value_part.reshape(seq_len, pair_width), offset, 1
        )
        return (grad_queries, grad_keys, grad_values)

    empty_buf = jnp.zeros((seq_len, features), jnp.float32)
    return lax.fori_loop(0, features // pair_width, one_pair, (empty_buf, empty_buf, empty_buf))


def plain_body(
    tokens,
    segment_ids,
    cotangent,
    weight_query,
    weight_key,
    weight_value,
    weight_output,
    weight_inner,
    weight_outer,
    bias_query,
    bias_value,
    bias_output,
    bias_inner,
    bias_outer,
    gain_attn,
    shift_attn,
    gain_ffn,
    shift_ffn,
):
    gathered = (
        lax.all_gather(weight_query, "fsdp", axis=1, tiled=True),
        lax.all_gather(weight_key, "fsdp", axis=1, tiled=True),
        lax.all_gather(weight_value, "fsdp", axis=1, tiled=True),
        lax.all_gather(weight_output, "fsdp", axis=1, tiled=True),
        lax.all_gather(weight_inner, "fsdp", axis=1, tiled=True),
        lax.all_gather(weight_outer, "fsdp", axis=1, tiled=True),
        lax.all_gather(bias_query, "fsdp", axis=0, tiled=True),
        lax.all_gather(bias_value, "fsdp", axis=0, tiled=True),
        lax.all_gather(bias_output, "fsdp", axis=0, tiled=True),
        lax.all_gather(bias_inner, "fsdp", axis=0, tiled=True),
        lax.all_gather(bias_outer, "fsdp", axis=0, tiled=True),
        lax.all_gather(gain_attn, "fsdp", axis=0, tiled=True),
        lax.all_gather(shift_attn, "fsdp", axis=0, tiled=True),
        lax.all_gather(gain_ffn, "fsdp", axis=0, tiled=True),
        lax.all_gather(shift_ffn, "fsdp", axis=0, tiled=True),
    )
    (
        whole_query,
        whole_key,
        whole_value,
        whole_output,
        whole_inner,
        whole_outer,
        query_bias,
        value_bias,
        output_bias,
        inner_bias,
        outer_bias,
        attn_gain,
        attn_shift,
        ffn_gain,
        ffn_shift,
    ) = gathered
    count_seq, seq_len, features = tokens.shape
    row_count = count_seq * seq_len
    stream = tokens.reshape(row_count, features).astype(jnp.float32)
    normed = (
        scaled(stream, attn_gain.astype(jnp.float32)) + attn_shift.astype(jnp.float32)
    ).astype(jnp.bfloat16)
    queries = (matmul(normed, whole_query) + query_bias.astype(jnp.float32)).astype(jnp.bfloat16)
    key_rows = matmul(normed, whole_key).astype(jnp.bfloat16)
    value_rows = (matmul(normed, whole_value) + value_bias.astype(jnp.float32)).astype(jnp.bfloat16)
    query_seq = queries.reshape(count_seq, seq_len, features)
    key_seq = key_rows.reshape(count_seq, seq_len, features)
    value_seq = value_rows.reshape(count_seq, seq_len, features)
    attended, logsum = lax.map(
        lambda packed: attend_forward(*packed), (query_seq, key_seq, value_seq, segment_ids)
    )
    attended = attended.reshape(row_count, features).astype(jnp.bfloat16)
    branch = matmul(attended, whole_output) + output_bias.astype(jnp.float32)
    middle = stream + branch
    second = (scaled(middle, ffn_gain.astype(jnp.float32)) + ffn_shift.astype(jnp.float32)).astype(
        jnp.bfloat16
    )
    hidden = matmul(second, whole_inner) + inner_bias.astype(jnp.float32)
    active = jax.nn.gelu(hidden, approximate=False).astype(jnp.bfloat16)
    ffn_out = matmul(active, whole_outer) + outer_bias.astype(jnp.float32)
    result = middle + ffn_out
    valid_mask = (segment_ids != 0).reshape(row_count).astype(jnp.float32)
    squares = jnp.stack(
        [
            jnp.sum(jnp.sum(piece * piece, axis=-1) * valid_mask)
            for piece in (stream, branch, middle, ffn_out)
        ]
    )
    counted = jnp.sum(valid_mask)
    regathered = (
        lax.all_gather(weight_query, "fsdp", axis=1, tiled=True),
        lax.all_gather(weight_key, "fsdp", axis=1, tiled=True),
        lax.all_gather(weight_value, "fsdp", axis=1, tiled=True),
        lax.all_gather(weight_output, "fsdp", axis=1, tiled=True),
        lax.all_gather(weight_inner, "fsdp", axis=1, tiled=True),
        lax.all_gather(weight_outer, "fsdp", axis=1, tiled=True),
        lax.all_gather(gain_attn, "fsdp", axis=0, tiled=True),
        lax.all_gather(gain_ffn, "fsdp", axis=0, tiled=True),
    )
    (
        back_query,
        back_key,
        back_value,
        back_output,
        back_inner,
        back_outer,
        back_attn_gain,
        back_ffn_gain,
    ) = regathered
    grad_out = cotangent.reshape(row_count, features)
    grad_outer = over_rows(active, grad_out)
    biasgrad_outer = jnp.sum(grad_out.astype(jnp.float32), axis=0)
    grad_active = against(grad_out, back_outer)
    _, gelu_back = jax.vjp(lambda values: jax.nn.gelu(values, approximate=False), hidden)
    grad_hidden = gelu_back(grad_active)[0].astype(jnp.bfloat16)
    grad_inner = over_rows(second, grad_hidden)
    biasgrad_inner = jnp.sum(grad_hidden.astype(jnp.float32), axis=0)
    grad_second = against(grad_hidden, back_inner)
    _, norm_back_ffn = jax.vjp(scaled, middle, back_ffn_gain.astype(jnp.float32))
    grad_middle, gaingrad_ffn = norm_back_ffn(grad_second)
    shiftgrad_ffn = jnp.sum(grad_second, axis=0)
    grad_middle = grad_middle + grad_out.astype(jnp.float32)
    grad_branch = grad_middle.astype(jnp.bfloat16)
    grad_output = over_rows(attended, grad_branch)
    biasgrad_output = jnp.sum(grad_branch.astype(jnp.float32), axis=0)
    grad_attended = against(grad_branch, back_output).astype(jnp.bfloat16)
    upstream_seq = grad_attended.reshape(count_seq, seq_len, features)
    grad_q_seq, grad_k_seq, grad_v_seq = lax.map(
        lambda packed: attend_backward(*packed),
        (query_seq, key_seq, value_seq, upstream_seq, logsum, segment_ids),
    )
    grad_queries = grad_q_seq.reshape(row_count, features).astype(jnp.bfloat16)
    grad_keys = grad_k_seq.reshape(row_count, features).astype(jnp.bfloat16)
    grad_values = grad_v_seq.reshape(row_count, features).astype(jnp.bfloat16)
    grad_query = over_rows(normed, grad_queries)
    grad_key = over_rows(normed, grad_keys)
    grad_value = over_rows(normed, grad_values)
    biasgrad_query = jnp.sum(grad_queries.astype(jnp.float32), axis=0)
    biasgrad_value = jnp.sum(grad_values.astype(jnp.float32), axis=0)
    grad_normed = (
        against(grad_queries, back_query)
        + against(grad_keys, back_key)
        + against(grad_values, back_value)
    )
    _, norm_back_attn = jax.vjp(scaled, stream, back_attn_gain.astype(jnp.float32))
    grad_stream, gaingrad_attn = norm_back_attn(grad_normed)
    shiftgrad_attn = jnp.sum(grad_normed, axis=0)
    grad_input = (grad_middle + grad_stream).astype(jnp.bfloat16).reshape(tokens.shape)
    square_total, count_total = lax.psum((squares, counted), ("fsdp", "dp"))
    reduced = (
        lax.psum_scatter(grad_query, "fsdp", scatter_dimension=1, tiled=True),
        lax.psum_scatter(grad_key, "fsdp", scatter_dimension=1, tiled=True),
        lax.psum_scatter(grad_value, "fsdp", scatter_dimension=1, tiled=True),
        lax.psum_scatter(grad_output, "fsdp", scatter_dimension=1, tiled=True),
        lax.psum_scatter(grad_inner, "fsdp", scatter_dimension=1, tiled=True),
        lax.psum_scatter(grad_outer, "fsdp", scatter_dimension=1, tiled=True),
        lax.psum_scatter(biasgrad_query, "fsdp", scatter_dimension=0, tiled=True),
        lax.psum_scatter(biasgrad_value, "fsdp", scatter_dimension=0, tiled=True),
        lax.psum_scatter(biasgrad_output, "fsdp", scatter_dimension=0, tiled=True),
        lax.psum_scatter(biasgrad_inner, "fsdp", scatter_dimension=0, tiled=True),
        lax.psum_scatter(biasgrad_outer, "fsdp", scatter_dimension=0, tiled=True),
        lax.psum_scatter(gaingrad_attn, "fsdp", scatter_dimension=0, tiled=True),
        lax.psum_scatter(shiftgrad_attn, "fsdp", scatter_dimension=0, tiled=True),
        lax.psum_scatter(gaingrad_ffn, "fsdp", scatter_dimension=0, tiled=True),
        lax.psum_scatter(shiftgrad_ffn, "fsdp", scatter_dimension=0, tiled=True),
    )
    summed = (
        lax.psum(reduced[0].astype(jnp.bfloat16), "dp").astype(jnp.float32),
        lax.psum(reduced[1].astype(jnp.bfloat16), "dp").astype(jnp.float32),
        lax.psum(reduced[2].astype(jnp.bfloat16), "dp").astype(jnp.float32),
        lax.psum(reduced[3].astype(jnp.bfloat16), "dp").astype(jnp.float32),
        lax.psum(reduced[4].astype(jnp.bfloat16), "dp").astype(jnp.float32),
        lax.psum(reduced[5].astype(jnp.bfloat16), "dp").astype(jnp.float32),
        lax.psum(reduced[6].astype(jnp.bfloat16), "dp").astype(jnp.float32),
        lax.psum(reduced[7].astype(jnp.bfloat16), "dp").astype(jnp.float32),
        lax.psum(reduced[8].astype(jnp.bfloat16), "dp").astype(jnp.float32),
        lax.psum(reduced[9].astype(jnp.bfloat16), "dp").astype(jnp.float32),
        lax.psum(reduced[10].astype(jnp.bfloat16), "dp").astype(jnp.float32),
        lax.psum(reduced[11].astype(jnp.bfloat16), "dp").astype(jnp.float32),
        lax.psum(reduced[12].astype(jnp.bfloat16), "dp").astype(jnp.float32),
        lax.psum(reduced[13].astype(jnp.bfloat16), "dp").astype(jnp.float32),
        lax.psum(reduced[14].astype(jnp.bfloat16), "dp").astype(jnp.float32),
    )
    rms_stats = jnp.sqrt(square_total / (count_total * features))
    return (
        result.astype(jnp.bfloat16).reshape(tokens.shape),
        grad_input,
        summed[0],
        summed[1],
        summed[2],
        summed[3],
        summed[4],
        summed[5],
        summed[6],
        summed[7],
        summed[8],
        summed[9],
        summed[10],
        summed[11],
        summed[12],
        summed[13],
        summed[14],
        rms_stats,
    )


def solution(mesh):
    in_specs = (
        P(("fsdp", "dp"), None, None),
        P(("fsdp", "dp"), None),
        P(("fsdp", "dp"), None, None),
        P(None, "fsdp"),
        P(None, "fsdp"),
        P(None, "fsdp"),
        P(None, "fsdp"),
        P(None, "fsdp"),
        P(None, "fsdp"),
        P("fsdp"),
        P("fsdp"),
        P("fsdp"),
        P("fsdp"),
        P("fsdp"),
        P("fsdp"),
        P("fsdp"),
        P("fsdp"),
        P("fsdp"),
    )
    out_specs = (
        P(("fsdp", "dp"), None, None),
        P(("fsdp", "dp"), None, None),
        P(None, "fsdp"),
        P(None, "fsdp"),
        P(None, "fsdp"),
        P(None, "fsdp"),
        P(None, "fsdp"),
        P(None, "fsdp"),
        P("fsdp"),
        P("fsdp"),
        P("fsdp"),
        P("fsdp"),
        P("fsdp"),
        P("fsdp"),
        P("fsdp"),
        P("fsdp"),
        P("fsdp"),
        P(),
    )
    body = fast_body if dict(mesh.shape) == {"fsdp": 16, "dp": 2} else plain_body
    return jax.shard_map(body, mesh=mesh, in_specs=in_specs, out_specs=out_specs, check_vma=False)
```

```python
import math

import jax
import jax.numpy as jnp
import numpy as np
from jax import lax
from jax.experimental import pallas as pl
from jax.experimental.pallas import tpu as pltpu
from jax.sharding import PartitionSpec as P

HD = 64
BF, F32 = jnp.bfloat16, jnp.float32
MESH = pl.DeviceIdType.MESH
SEQ, WIDTH, PIECE, BLOCK, KEYS = 1024, 768, 48, 256, 512
EVERY = slice(None)


def dg(lhs, rhs, lhs_dim, rhs_dim):
    return lax.dot_general(
        lhs, rhs, (((lhs_dim,), (rhs_dim,)), ((), ())), preferred_element_type=F32
    )


def lanes(rows):
    return lax.broadcasted_iota(jnp.int32, (rows, 128), 1)


def piece(k):
    return slice(k * WIDTH, (k + 1) * WIDTH)


def aligned(start, size, unit=128):
    return pl.ds(pl.multiple_of(start, unit), size)


def iota_of(shape, axis):
    return lax.broadcasted_iota(jnp.int32, shape, axis)


def chosen(mask):
    return jnp.where(mask, 1.0, 0.0)


class Place:
    def __init__(self):
        index = lax.axis_index("fsdp")
        self.core = lax.axis_index("dp")
        self.x = lax.rem(index, 2)
        self.y = lax.rem(lax.div(index, 2), 2)
        self.z = lax.div(index, 4)

    def at(self, z=None, y=None, x=None, core=None):
        z = self.z if z is None else z
        y = self.y if y is None else y
        x = self.x if x is None else x
        return (z * 4 + y * 2 + x, self.core if core is None else core)

    def z_after(self, step):
        return lax.rem(self.z + step, 4)

    def z_peer(self, step):
        return self.at(z=self.z_after(step))

    def y_peer(self):
        return self.at(y=1 - self.y)

    def x_peer(self):
        return self.at(x=1 - self.x)

    def core_peer(self):
        return self.at(core=1 - self.core)

    def greet(self):
        ready = pltpu.get_barrier_semaphore()
        peers = [self.z_peer(1), self.z_peer(2), self.z_peer(3)]
        peers += [self.y_peer(), self.x_peer(), self.core_peer()]
        for peer in peers:
            pl.semaphore_signal(ready, inc=1, device_id=peer, device_id_type=MESH)
        pl.semaphore_wait(ready, len(peers))


class Moves:
    def __init__(self, send, recv, first):
        self.send, self.recv, self.first, self.made = send, recv, first, {}

    def add(self, name, src, dst, peer):
        slot = self.first + len(self.made)
        self.made[name] = lambda: pltpu.make_async_remote_copy(
            src_ref=src(),
            dst_ref=dst(),
            send_sem=self.send.at[slot],
            recv_sem=self.recv.at[slot],
            device_id=peer(),
            device_id_type=MESH,
        )

    def start(self, *names):
        for name in names:
            self.made[name]().start()

    def landed(self, *names):
        for name in names:
            self.made[name]().wait_recv()

    def sent(self):
        for make in self.made.values():
            make().wait_send()


GATHER_MOVES = 11


class Gather(Moves):
    def __init__(self, me, view, out, local, send, recv, slot, first, half):
        super().__init__(send, recv, slot * GATHER_MOVES)
        self.view = view
        self.local_sem = local.at[slot]
        cut = half * 2 // 3 if half == 384 else half // 2
        start = first + me.core * half
        mine = aligned(start, half)
        a, b = aligned(start, cut), aligned(start + cut, half - cut)
        own = lambda: out.at[me.z, me.y, me.x, :, mine]
        self.own = own
        for step in (1, 2, 3):
            self.add(("z", step), view, own, lambda step=step: me.z_peer(step))

        def same(name, view, peer):
            self.add(name, view, view, peer)

        same("a1", lambda: out.at[:, me.y, me.x, :, a], me.y_peer)
        same("b1", lambda: out.at[:, me.y, me.x, :, b], me.x_peer)
        same("a2", lambda: out.at[:, :, me.x, :, a], me.x_peer)
        same("b2", lambda: out.at[:, me.y, :, :, b], me.y_peer)
        same("near a", lambda: out.at[:, :, me.x, :, a], me.core_peer)
        same("near b", lambda: out.at[:, me.y, :, :, b], me.core_peer)
        same("far a", lambda: out.at[:, :, 1 - me.x, :, a], me.core_peer)
        same("far b", lambda: out.at[:, 1 - me.y, :, :, b], me.core_peer)

    def local(self):
        return pltpu.make_async_copy(self.view(), self.own(), self.local_sem)

    def step(self, number):
        if number == 0:
            self.start(("z", 2), ("z", 1), ("z", 3))
            self.local().start()
        if number == 1:
            self.local().wait()
            self.landed(("z", 1), ("z", 2), ("z", 3))
            self.start("a1", "b1")
        if number == 2:
            self.landed("a1", "b1")
            self.start("a2", "b2", "near a", "near b")
        if number == 3:
            self.landed("a2", "b2")
            self.start("far a", "far b")
        if number == 4:
            self.landed("near a", "near b", "far a", "far b")
            self.sent()


class VectorGather(Moves):
    def __init__(self, me, src, out, local, send, recv, first):
        super().__init__(send, recv, first)
        own = lambda: out.at[me.z, me.y, me.x]
        self.copy = lambda: pltpu.make_async_copy(src, own(), local)
        for step in (1, 2, 3):
            self.add(("z", step), lambda: src, own, lambda step=step: me.z_peer(step))
        self.add("y", lambda: out.at[:, me.y, me.x], lambda: out.at[:, me.y, me.x], me.y_peer)
        self.add("x", lambda: out.at[:, :, me.x], lambda: out.at[:, :, me.x], me.x_peer)

    def step(self, number):
        if number == 0:
            self.copy().start()
            self.start(("z", 1), ("z", 2), ("z", 3))
        if number == 1:
            self.copy().wait()
            self.landed(("z", 1), ("z", 2), ("z", 3))
            self.start("y")
        if number == 2:
            self.landed("y")
            self.start("x")
        if number == 3:
            self.landed("x")
            self.sent()


REDUCE_MOVES = 9


class Reduce(Moves):
    def __init__(self, me, grads, total, boxes, send, recv, slot, first, half, group):
        super().__init__(send, recv, slot)
        from_core, from_a1, from_b1, from_a2, from_b2, from_z = boxes
        self.me, self.grads, self.total, self.boxes = me, grads, total, boxes
        cut = half * 2 // 3 if half == 384 else half // 2
        start = first + me.core * half
        self.half = half
        self.mine = mine = aligned(start, half)
        theirs = aligned(first + (1 - me.core) * half, half)
        self.a, self.b = a, b = aligned(start, cut), aligned(start + cut, half - cut)
        self.group = group
        self.add("core", lambda: grads.at[:, :, :, :, theirs], lambda: from_core, me.core_peer)
        self.add("a1", lambda: grads.at[:, 1 - me.y, :, :, a], lambda: from_a1, me.y_peer)
        self.add("b1", lambda: grads.at[:, :, 1 - me.x, :, b], lambda: from_b1, me.x_peer)
        self.add("a2", lambda: grads.at[:, me.y, 1 - me.x, :, a], lambda: from_a2, me.x_peer)
        self.add("b2", lambda: grads.at[:, 1 - me.y, me.x, :, b], lambda: from_b2, me.y_peer)
        for step in (1, 2, 3):
            self.add(
                ("z", step),
                lambda step=step: grads.at[me.z_after(step), me.y, me.x, :, mine],
                lambda step=step: from_z.at[step - 1],
                lambda step=step: me.z_peer(step),
            )
        self.add("last", lambda: total.at[group, :, mine], lambda: total.at[group, :, mine], me.core_peer)

    def step(self, number):
        me, grads = self.me, self.grads
        from_core, from_a1, from_b1, from_a2, from_b2, from_z = self.boxes
        a, b, mine = self.a, self.b, self.mine

        def plus(left, right):
            return left + right

        if number == 0:
            self.start("core")
        if number == 1:
            self.landed("core")

            @pl.loop(0, 4)
            def _(z):
                for y in range(2):
                    for x in range(2):
                        grads[z, y, x, :, mine] = plus(
                            grads[z, y, x, :, mine], from_core[z, y, x]
                        )

            self.start("a1", "b1")
        if number == 2:
            self.landed("a1", "b1")

            @pl.loop(0, 4)
            def _(z):
                for k in range(2):
                    grads[z, me.y, k, :, a] = plus(grads[z, me.y, k, :, a], from_a1[z, k])
                    grads[z, k, me.x, :, b] = plus(grads[z, k, me.x, :, b], from_b1[z, k])

            self.start("a2", "b2")
        if number == 3:
            self.landed("a2", "b2")

            @pl.loop(0, 4)
            def _(z):
                grads[z, me.y, me.x, :, a] = plus(grads[z, me.y, me.x, :, a], from_a2[z])
                grads[z, me.y, me.x, :, b] = plus(grads[z, me.y, me.x, :, b], from_b2[z])

            self.start(("z", 2), ("z", 1), ("z", 3))
        if number == 4:
            self.landed(("z", 1), ("z", 2), ("z", 3))
            terms = [from_z[k].astype(F32) for k in range(3)]
            own = grads[me.z, me.y, me.x, :, mine].astype(F32)
            self.total[self.group, :, mine] = (own + terms[0]) + (terms[1] + terms[2])
            self.start("last")
        if number == 5:
            self.landed("last")
            self.sent()


def boxes_for(half):
    cut = half * 2 // 3 if half == 384 else half // 2
    return [
        pltpu.VMEM((4, 2, 2, PIECE, half), BF),
        pltpu.VMEM((4, 2, PIECE, cut), BF),
        pltpu.VMEM((4, 2, PIECE, half - cut), BF),
        pltpu.VMEM((4, PIECE, cut), BF),
        pltpu.VMEM((4, PIECE, half - cut), BF),
        pltpu.VMEM((3, PIECE, half), BF),
    ]


class VectorSum(Moves):
    def __init__(self, me, table, parts, boxes, mine, send, recv, first):
        super().__init__(send, recv, first)
        from_core, from_y, from_x, from_z = boxes
        self.me, self.table, self.parts, self.boxes, self.mine = me, table, parts, boxes, mine
        self.add("core", lambda: parts, lambda: from_core, me.core_peer)
        self.add("y", lambda: from_core.at[:, 1 - me.y], lambda: from_y, me.y_peer)
        self.add("x", lambda: from_core.at[:, me.y, 1 - me.x], lambda: from_x, me.x_peer)
        for step in (1, 2, 3):
            self.add(
                ("z", step),
                lambda step=step: from_core.at[me.z_after(step), me.y, me.x],
                lambda step=step: from_z.at[step - 1],
                lambda step=step: me.z_peer(step),
            )

    def cut(self):
        table, parts = self.table, self.parts
        totals = jnp.sum(table[8:24], axis=1, keepdims=True)
        lane = lanes(1)
        row = jnp.zeros((1, 128), F32)
        for k in range(5):
            row = jnp.where(lane == k, totals[4 + k : 5 + k], row)
        for m in range(16):
            first = pltpu.roll(table[0:8], (WIDTH - PIECE * m) % WIDTH, 1)[:, :128]
            inner = pltpu.roll(table[8:16], (WIDTH - PIECE * m) % WIDTH, 1)[:, :128]
            parts[m // 4, m // 2 % 2, m % 2, 0:8] = first
            parts[m // 4, m // 2 % 2, m % 2, 12:13] = row
            for b in range(4):
                f = 4 * b + m // 4
                spot = 8 + m % 4
                parts[f // 4, f // 2 % 2, f % 2, spot : spot + 1] = inner[b : b + 1]

    def step(self, number):
        me, parts = self.me, self.parts
        from_core, from_y, from_x, from_z = self.boxes
        along_z = (("z", 1), ("z", 2), ("z", 3))
        if number == 0:
            self.cut()
            self.start("core")
        if number == 1:
            self.landed("core")
            from_core[...] = from_core[...] + parts[...]
            self.start("y")
        if number == 2:
            self.landed("y")
            from_core[:, me.y] = from_core[:, me.y] + from_y[...]
            self.start("x")
        if number == 3:
            self.landed("x")
            from_core[:, me.y, me.x] = from_core[:, me.y, me.x] + from_x[...]
            self.start(*along_z)
        if number == 4:
            self.landed(*along_z)
            own = from_core[me.z, me.y, me.x]
            self.mine[...] = (own + from_z[0]) + (from_z[1] + from_z[2])
            self.sent()


def normalized(values):
    average = jnp.mean(values, axis=-1, keepdims=True)
    centered = values - average
    spread = jnp.mean(centered * centered, axis=-1, keepdims=True)
    scale = lax.rsqrt(spread + 1e-06)
    return centered * scale, scale


def norm_grad(grad_scaled, unit, scale):
    mean_grad = jnp.mean(grad_scaled, axis=-1, keepdims=True)
    mean_both = jnp.mean(grad_scaled * unit, axis=-1, keepdims=True)
    return scale * (grad_scaled - mean_grad - unit * mean_both)


def tile_of(whole, group_cols):
    return whole[:, :, :, :, aligned(group_cols, WIDTH)].reshape(WIDTH, WIDTH)


def inner_tile(whole, k):
    parts = [whole[k, :, :, :, piece(r)].reshape(4, PIECE, WIDTH) for r in range(4)]
    return jnp.stack(parts, axis=1).reshape(WIDTH, WIDTH)


def blocks(count, body):
    @pl.loop(0, SEQ // count)
    def _(step):
        body(aligned(step * count, count, count))


N_GATHERS, N_REDUCES = 8, 8
N_COPIES = N_GATHERS * GATHER_MOVES + 5 + N_REDUCES * REDUCE_MOVES + 6


def three_terms(values, lane, first, rest):
    high = values.astype(BF).astype(F32)
    left = values - high
    middle = left.astype(BF).astype(F32)
    low = left - middle
    for k, term in enumerate((high, middle, low)):
        rest = jnp.where(lane == first + k, term, rest)
    return rest.astype(BF)


def layer_kernel(
    tok, cot, seg_row, sh_q, sh_k, sh_v, sh_o, sh_in, sh_out,
    v0, v1, v2, v3, v4, v5, v6, v7, inner_bias, pick, rows_of,
    result, grad_tok, total, sums, w_qkvo, qkv_kept, normed_kept,
    pack, seg, got, vec, big_a, big_b, first, middle, last, small_a, small_b, mid, lse, qa, ka, va, da, acc, table, parts,
    send, recv, local, *boxes,
):
    me = Place()
    pack[...] = jnp.zeros_like(pack)
    for k, values in enumerate((v0, v1, v2, v3, v4, v5, v6, v7)):
        pack[k : k + 1, :PIECE] = values[...]
    for k in range(4):
        wide = (4 * PIECE, 128)
        part = (iota_of(wide, 0) == iota_of(wide, 1) + PIECE * k) & (iota_of(wide, 1) < PIECE)
        pack[8 + k : 9 + k, :] = dg(inner_bias[...], chosen(part).astype(BF), 1, 0).astype(BF)
    me.greet()
    base = N_GATHERS * GATHER_MOVES
    vectors = VectorGather(me, pack, got, local.at[N_GATHERS], send, recv, base)
    def columns(ref, start, half):
        return lambda: ref.at[:, aligned(start + me.core * half, half)]

    def inner_rows(start):
        return lambda: sh_in.at[aligned((start + me.core) * PIECE, PIECE, PIECE)]

    spans = [(columns(ref, 0, 384), last, 768 * k, 384) for k, ref in enumerate((sh_q, sh_k, sh_v, sh_o))]
    spans += [(inner_rows(0), middle, 0, 768), (inner_rows(2), middle, 1536, 768)]
    spans += [(columns(sh_out, 0, 768), first, 0, 768), (columns(sh_out, 1536, 768), first, 1536, 768)]
    g_q, g_k, g_v, g_o, g_i01, g_i23, g_u01, g_u23 = [
        Gather(me, src, out, local, send, recv, k, start, half)
        for k, (src, out, start, half) in enumerate(spans)
    ]
    base += 5
    spans = [(last, 0, 768, 2), (last, 1536, 768, 2), (middle, 0, 768, 1), (middle, 1536, 768, 1)]
    spans += [(first, 2304, 384, 0)] + [(first, 768 * k, 384, 0) for k in range(3)]
    u01, u23, i01, i23, out, que, key, val = [
        Reduce(me, grads, total, boxes[6 * k : 6 * k + 6], send, recv, base + k * REDUCE_MOVES, start, half, group)
        for k, (grads, start, half, group) in enumerate(spans)
    ]
    vector_sum = VectorSum(me, table, parts, boxes[-4:], sums, send, recv, base + N_REDUCES * REDUCE_MOVES)

    def move(slot, src, dst):
        return lambda: pltpu.make_async_copy(src(), dst(), local.at[N_GATHERS + slot])

    q_cols, o_cols = slice(0, 3 * WIDTH), slice(3 * WIDTH, 4 * WIDTH)
    keep_normed = move(1, lambda: big_b.at[:, o_cols], lambda: normed_kept)
    keep_qkv = move(2, lambda: big_a.at[:, q_cols], lambda: qkv_kept)
    keep_w = move(3, lambda: last, lambda: w_qkvo)
    save_result = [
        move(k, lambda v=view: v(), lambda n=n: result.at[:, n * 256 : n * 256 + 256])
        for n, (k, view) in enumerate(
            ((4, lambda: qa.at[0]), (10, lambda: qa.at[1]), (11, lambda: da.at[0]))
        )
    ]
    load_qkv = move(5, lambda: qkv_kept, lambda: big_a.at[:, q_cols])
    load_w_o = move(
        6, lambda: w_qkvo.at[:, :, :, :, o_cols], lambda: first.at[:, :, :, :, o_cols]
    )
    load_w_qkv = move(
        7, lambda: w_qkvo.at[:, :, :, :, q_cols], lambda: last.at[:, :, :, :, q_cols]
    )
    load_normed = move(8, lambda: normed_kept, lambda: big_b.at[:, o_cols])
    save_grad_tok = move(9, lambda: small_a, lambda: grad_tok)

    sums_ref = table

    def tally(row, values):
        sums_ref[row : row + 1] += jnp.sum(values, axis=0, keepdims=True)

    def valid_of(rows):
        return jnp.where(seg[rows].astype(F32)[:, 0:1] != 0.0, 1.0, 0.0)

    vectors.step(0)
    g_q.step(0)
    g_k.step(0)
    ids = jnp.broadcast_to(seg_row[...].astype(F32), (8, SEQ))
    ids = jnp.where(iota_of((8, SEQ), 0) == 0, ids, 0.0).astype(BF)
    seg[...] = dg(ids, jnp.ones((8, 128), BF), 0, 0).astype(BF)
    sums_ref[...] = jnp.zeros_like(sums_ref)
    lse[...] = jnp.zeros_like(lse)
    vectors.step(1)
    g_q.step(1)
    g_v.step(0)
    vectors.step(2)
    g_k.step(1)
    g_o.step(0)
    vectors.step(3)
    g_v.step(1)
    g_q.step(2)
    g_o.step(1)
    spread = dg(got[...].reshape(256, 128), pick[...], 1, 0)
    names = jnp.zeros((16, WIDTH), F32)
    for k in range(16):
        names += spread[16 * k : 16 * k + 16] * rows_of[k : k + 1]
    vec[...] = names
    for k in range(4):
        row = jnp.zeros((1, WIDTH), F32)
        for f in range(4):
            for r in range(4):
                spot = 16 * (4 * k + f) + 8 + r
                row += spread[spot : spot + 1] * rows_of[4 * f + r : 4 * f + r + 1]
        vec[8 + k : 9 + k] = row
    g_k.step(2)
    lane = lanes(SEQ)
    hot = seg[...].astype(F32) == lane.astype(F32)
    for h in range(2):
        qa[h, :, 128:] = jnp.where(hot, 1.0, 0.0).astype(BF)
    ka[:, 128:] = jnp.where(hot | (lane > 8), 0.0, -1e30).astype(BF)
    va[:, 128:] = jnp.ones((SEQ, 128), BF)

    def first_norm(rows):
        stream = tok[rows].astype(F32)
        valid = valid_of(rows)
        tally(12, stream * stream * valid)
        tally(16, jnp.broadcast_to(valid, stream.shape))
        unit, _ = normalized(stream)
        big_b[rows, o_cols] = (unit * vec[0:1] + vec[1:2]).astype(BF)

    blocks(BLOCK, first_norm)
    keep_normed().start()

    def project(k, bias):
        def part(rows):
            made = dg(big_b[rows, o_cols], tile_of(last, WIDTH * k), 1, 1)
            if bias is not None:
                made = made + vec[bias : bias + 1]
            big_a[rows, piece(k)] = made.astype(BF)

        blocks(512, part)

    g_q.step(3)
    g_v.step(2)
    g_i01.step(0)
    g_k.step(3)
    g_q.step(4)
    project(0, 2)
    g_k.step(4)
    g_o.step(2)
    g_i01.step(1)
    g_i23.step(0)
    project(1, None)
    g_v.step(3)
    g_v.step(4)
    project(2, 3)
    keep_qkv().start()

    def ticks(table):
        def at(pair, half):
            for moment, steps in table.items():
                if moment % 2 == half:

                    @pl.when(pair == moment // 2)
                    def _(steps=steps):
                        for step in steps:
                            step()

        return at

    def s(chunk, number):
        return lambda: chunk.step(number)

    forward_ticks = ticks(
        {
            1: [s(g_i23, 1), s(g_u01, 0)],
            2: [s(g_i01, 2)],
            3: [s(g_o, 3), s(g_u01, 1), s(g_u23, 0)],
            4: [s(g_o, 4), lambda: keep_w().start(), s(g_i23, 2)],
            5: [s(g_u23, 1)],
            6: [s(g_i01, 3)],
            7: [s(g_u01, 2), s(g_i01, 4)],
            9: [s(g_i23, 3)],
            10: [s(g_u23, 2)],
            11: [s(g_i23, 4)],
        }
    )

    @pl.loop(0, WIDTH // 128)
    def _(pair):
        forward_ticks(pair, 0)
        spot = pair * 128
        query = big_a[:, aligned(spot, 128)].astype(F32) * 0.125
        lane = lanes(SEQ)
        qa[0, :, :128] = jnp.where(lane < 64, query, 0.0).astype(BF)
        qa[1, :, :128] = jnp.where(lane < 64, 0.0, query).astype(BF)
        ka[:, :128] = big_a[:, aligned(WIDTH + spot, 128)]
        va[:, :128] = big_a[:, aligned(2 * WIDTH + spot, 128)]
        lane = lanes(BLOCK)
        work = [(step, h) for step in range(SEQ // BLOCK) for h in range(2)]
        mixed = [None, None]

        def score(step, h):
            return dg(qa[h, step * BLOCK : (step + 1) * BLOCK], ka[...], 1, 1)

        coming = score(*work[0])
        for number, (step, h) in enumerate(work):
            if number == len(work) // 2:
                forward_ticks(pair, 1)
            scores = coming
            if number + 1 < len(work):
                coming = score(*work[number + 1])
            rows = slice(step * BLOCK, (step + 1) * BLOCK)
            largest = jnp.max(scores, axis=1, keepdims=True)
            prob = jnp.exp(scores - largest).astype(BF)
            both = dg(prob, va[...], 1, 0)
            weight = both[:, 128:]
            mixed[h] = both[:, :128] / weight
            lse[rows] = jnp.where(lane == 2 * pair + h, largest + jnp.log(weight), lse[rows])
            if h == 1:
                both = jnp.where(lane < 64, mixed[0], mixed[1])
                small_b[rows, aligned(spot, 128)] = both.astype(BF)

    def second_norm(rows):
        valid = valid_of(rows)
        branch = dg(small_b[rows], tile_of(last, 3 * WIDTH), 1, 1) + vec[4:5]
        stream = tok[rows].astype(F32) + branch
        tally(13, branch * branch * valid)
        tally(14, stream * stream * valid)
        mid[rows] = stream
        unit, _ = normalized(stream)
        small_a[rows] = (unit * vec[6:7] + vec[7:8]).astype(BF)

    blocks(BLOCK, second_norm)
    g_u01.step(3)
    keep_normed().wait()
    keep_qkv().wait()
    for k in range(4):
        def expand(rows, k=k):
            hidden = dg(small_a[rows], inner_tile(middle, k), 1, 1) + vec[8 + k : 9 + k]
            phi = 0.5 + 0.5 * lax.erf(hidden * (0.5**0.5))
            bell = jnp.exp(hidden * hidden * -0.5) * 0.3989422804014327
            big_a[rows, piece(k)] = (hidden * phi).astype(BF)
            big_b[rows, piece(k)] = (phi + hidden * bell).astype(BF)

        blocks(BLOCK, expand)
        if k == 0:
            g_u01.step(4)
        if k == 1:
            g_u23.step(3)

    def store_grad(whole, k, left, right):
        made = dg(left, right, 0, 0).astype(BF)
        whole[:, :, :, :, piece(k)] = made.reshape(4, 2, 2, PIECE, WIDTH)

    keep_w().wait()
    store_grad(last, 0, cot[...], big_a[:, piece(0)])
    store_grad(last, 1, cot[...], big_a[:, piece(1)])
    u01.step(0)
    store_grad(last, 2, cot[...], big_a[:, piece(2)])
    store_grad(last, 3, cot[...], big_a[:, piece(3)])
    g_u23.step(4)
    u01.step(1)
    u23.step(0)
    for k in range(4):
        def through_gelu(rows, k=k):
            grad_active = dg(cot[rows], tile_of(first, k * WIDTH), 1, 0)
            grad_hidden = (grad_active * big_b[rows, piece(k)].astype(F32)).astype(BF)
            big_b[rows, piece(k)] = grad_hidden
            tally(8 + k, grad_hidden.astype(F32))

        blocks(BLOCK, through_gelu)
        if k == 1:
            u23.step(1)
    u01.step(2)

    def contract(rows):
        valid = valid_of(rows)
        ffn_out = dg(big_a[rows], first[...].reshape(WIDTH, 4 * WIDTH), 1, 1) + vec[5:6]
        tally(15, ffn_out * ffn_out * valid)
        made = (mid[rows] + ffn_out).astype(BF)
        qa[0, rows] = made[:, :256]
        qa[1, rows] = made[:, 256:512]
        da[0, rows] = made[:, 512:]

    blocks(BLOCK, contract)
    for make in save_result:
        make().start()
    load_qkv().start()
    load_w_o().start()
    u01.step(3)
    u23.step(2)

    def ffn_norm_back(rows):
        grad_second = dg(big_b[rows, piece(0)], inner_tile(middle, 0), 1, 0)
        for k in range(1, 4):
            grad_second += dg(big_b[rows, piece(k)], inner_tile(middle, k), 1, 0)
        unit, scale = normalized(mid[rows])
        tally(6, grad_second * unit)
        tally(7, grad_second)
        upper = cot[rows].astype(F32)
        tally(5, upper)
        grad_middle = upper + norm_grad(grad_second * vec[6:7], unit, scale)
        mid[rows] = grad_middle
        tally(4, grad_middle.astype(BF).astype(F32))

    blocks(BLOCK, ffn_norm_back)
    u23.step(3)
    u01.step(4)
    for k in range(4):
        made = dg(big_b[:, piece(k)], small_a[...], 0, 0).astype(BF).reshape(4, 4, PIECE, WIDTH)
        for r in range(4):
            middle[k, :, :, :, piece(r)] = made[:, r].reshape(2, 2, PIECE, WIDTH)
    i01.step(0)
    u01.step(5)
    load_normed().start()
    load_w_o().wait()

    def to_attended(rows):
        grad = dg(mid[rows].astype(BF), tile_of(first, 3 * WIDTH), 1, 0)
        big_a[rows, o_cols] = grad.astype(BF)

    blocks(512, to_attended)
    i23.step(0)
    u23.step(4)
    store_grad(first, 3, mid[...].astype(BF), small_b[...])
    i01.step(1)
    out.step(0)
    u23.step(5)
    load_w_qkv().start()
    load_qkv().wait()
    for make in save_result:
        make().wait()

    lane = lanes(SEQ)
    hot = seg[...].astype(F32) == lane.astype(F32)
    ones = (lane > 8) & (lane < 12)
    ka[:, 128:] = jnp.where(ones, 1.0, jnp.where(hot | (lane > 8), 0.0, -1e30)).astype(BF)
    va[:, 128:] = jnp.where(lane < 3, 1.0, 0.0).astype(BF)

    backward_ticks = ticks(
        {
            2: [s(i23, 1), s(out, 1)],
            4: [s(i01, 2)],
            6: [s(i01, 3), s(i23, 2)],
            8: [s(out, 2), s(i23, 3), s(i01, 4)],
            10: [s(out, 3), s(i23, 4), s(i01, 5)],
        }
    )

    @pl.loop(0, WIDTH // 128)
    def _(pair):
        backward_ticks(pair, 0)
        spot = pair * 128
        lane = lanes(SEQ)
        hot = jnp.where(seg[...].astype(F32) == lane.astype(F32), 1.0, 0.0)
        query = big_a[:, aligned(spot, 128)].astype(F32) * 0.125
        ka[:, :128] = big_a[:, aligned(WIDTH + spot, 128)]
        va[:, :128] = big_a[:, aligned(2 * WIDTH + spot, 128)]
        upper = big_a[:, aligned(3 * WIDTH + spot, 128)].astype(F32)
        both = small_b[:, aligned(spot, 128)].astype(F32) * upper
        for h in range(2):
            mine = (lane < 64) if h == 0 else (lane >= 64)
            qa[h, :, :128] = jnp.where(mine, query, 0.0).astype(BF)
            da[h, :, :128] = jnp.where(mine, upper, 0.0).astype(BF)
            level = jnp.sum(jnp.where(lane == 2 * pair + h, lse[...], 0.0), axis=1, keepdims=True)
            qa[h, :, 128:] = three_terms(jnp.broadcast_to(-level, hot.shape), lane, 9, hot)
            weighted = jnp.sum(jnp.where(mine, both, 0.0), axis=1, keepdims=True)
            da[h, :, 128:] = three_terms(
                jnp.broadcast_to(-weighted, hot.shape), lane, 0, jnp.zeros_like(hot)
            )
        for step in range(SEQ // KEYS):
            rows = slice(step * KEYS, (step + 1) * KEYS)
            for_keys, for_values = [], []
            for h in range(2):
                prob = jnp.exp(dg(ka[rows], qa[h], 1, 1))
                grad_score = (prob * dg(va[rows], da[h], 1, 1)).astype(BF)
                for_values.append(dg(prob.astype(BF), da[h, :, :128], 1, 0))
                for_keys.append(dg(grad_score, qa[h, :, :128], 1, 0))
                for_queries = dg(ka[rows, :128], grad_score, 0, 0)
                acc[h] = for_queries if step == 0 else acc[h] + for_queries
            big_b[rows, aligned(WIDTH + spot, 128)] = (for_keys[0] + for_keys[1]).astype(BF)
            big_b[rows, aligned(2 * WIDTH + spot, 128)] = (for_values[0] + for_values[1]).astype(BF)
        pair_grad = jnp.concatenate([acc[0, :64], acc[1, 64:]], axis=0) * 0.125
        big_b[:, aligned(spot, 128)] = pair_grad.T.astype(BF)

    load_normed().wait()
    store_grad(first, 0, big_b[:, piece(0)], big_b[:, o_cols])
    que.step(0)
    out.step(4)
    store_grad(first, 1, big_b[:, piece(1)], big_b[:, o_cols])
    key.step(0)
    que.step(1)
    i23.step(5)
    store_grad(first, 2, big_b[:, piece(2)], big_b[:, o_cols])
    val.step(0)
    key.step(1)
    out.step(5)
    load_w_qkv().wait()

    @pl.loop(0, SEQ // BLOCK)
    def _(step):
        rows = aligned(step * BLOCK, BLOCK, BLOCK)
        grad_normed = dg(big_b[rows, piece(0)], tile_of(last, 0), 1, 0)
        for k in range(1, 3):
            grad_normed += dg(big_b[rows, piece(k)], tile_of(last, k * WIDTH), 1, 0)
        tally(2, big_b[rows, piece(0)].astype(F32))
        tally(3, big_b[rows, piece(2)].astype(F32))
        unit, scale = normalized(tok[rows].astype(F32))
        tally(0, grad_normed * unit)
        tally(1, grad_normed)
        grad_stream = mid[rows] + norm_grad(grad_normed * vec[0:1], unit, scale)
        small_a[rows] = grad_stream.astype(BF)

        @pl.when(step == 0)
        def _():
            val.step(1)

        @pl.when(step == 1)
        def _():
            que.step(2)

        @pl.when(step == 2)
        def _():
            key.step(2)

        @pl.when(step == 3)
        def _():
            que.step(3)

    save_grad_tok().start()
    vector_sum.step(0)
    val.step(2)
    vector_sum.step(1)
    que.step(4)
    key.step(3)
    vector_sum.step(2)
    val.step(3)
    vector_sum.step(3)
    key.step(4)
    que.step(5)
    vector_sum.step(4)
    val.step(4)
    key.step(5)
    val.step(5)
    save_grad_tok().wait()


def layer_call(tok, cot, seg_row, weights, vectors):
    vmem, anywhere = pl.BlockSpec(memory_space=pltpu.VMEM), pl.BlockSpec(memory_space=pl.ANY)
    whole = (4, 2, 2, PIECE, 4 * WIDTH)
    wide = lambda k, kind: pltpu.VMEM((SEQ, k), kind)
    outs = [jax.ShapeDtypeStruct((SEQ, WIDTH), BF)] * 2
    outs += [jax.ShapeDtypeStruct((3, PIECE, 4 * WIDTH), F32), jax.ShapeDtypeStruct((16, 128), F32)]
    outs += [jax.ShapeDtypeStruct(whole, BF)]
    outs += [jax.ShapeDtypeStruct((SEQ, 3 * WIDTH), BF), jax.ShapeDtypeStruct((SEQ, WIDTH), BF)]
    scratch = [pltpu.VMEM((16, 128), BF), wide(128, BF), pltpu.VMEM((4, 2, 2, 16, 128), BF), pltpu.VMEM((16, WIDTH), F32)]
    scratch += [wide(4 * WIDTH, BF)] * 2 + [pltpu.VMEM(whole, BF)] * 3
    scratch += [wide(WIDTH, BF)] * 2 + [wide(WIDTH, F32), wide(128, F32)]
    scratch += [pltpu.VMEM((2, SEQ, 256), BF), wide(256, BF), wide(256, BF), pltpu.VMEM((2, SEQ, 256), BF)]
    scratch += [pltpu.VMEM((2, 128, SEQ), F32), pltpu.VMEM((24, WIDTH), F32), pltpu.VMEM((4, 2, 2, 16, 128), F32)]
    scratch += [pltpu.SemaphoreType.DMA((N_COPIES,))] * 2 + [pltpu.SemaphoreType.DMA((20,))]
    for half in [768] * 4 + [384] * 4:
        scratch += boxes_for(half)
    for shape in ((4, 2, 2), (4, 2), (4,), (3,)):
        scratch.append(pltpu.VMEM((*shape, 16, 128), F32))
    place = np.arange(WIDTH)
    pick = jnp.asarray((place[None, :] % PIECE == np.arange(128)[:, None]), BF)
    rows_of = jnp.asarray((place[None, :] // PIECE == np.arange(16)[:, None]), F32)
    return pl.pallas_call(
        layer_kernel,
        out_shape=outs,
        in_specs=[vmem] * 20,
        out_specs=[anywhere] * 2 + [vmem] * 2 + [anywhere] * 3,
        scratch_shapes=scratch,
        compiler_params=pltpu.CompilerParams(
            collective_id=1, has_side_effects=True, vmem_limit_bytes=63 * 2**20
        ),
        name="layer",
    )(tok, cot, seg_row, *weights, *vectors, pick, rows_of)[:4]


def packed_inputs(
    weight_query, weight_key, weight_value, weight_output, weight_inner, weight_outer,
    bias_query, bias_value, bias_output, bias_inner, bias_outer, gain_attn, shift_attn, gain_ffn, shift_ffn,
):
    four = (weight_query, weight_key, weight_value, weight_output)
    sh_qkvo = jnp.concatenate([w.T for w in four], axis=1)
    sh_in = weight_inner.T.reshape(4, PIECE, WIDTH).transpose(1, 0, 2).reshape(PIECE, 4 * WIDTH)
    sh_out = weight_outer.T.reshape(PIECE, 16, 4, PIECE).transpose(0, 2, 1, 3).reshape(PIECE, 4 * WIDTH)
    vectors = (gain_attn, shift_attn, bias_query, bias_value, bias_output, bias_outer, gain_ffn, shift_ffn)
    pack = jnp.concatenate([jnp.stack(vectors), bias_inner.reshape(4, PIECE)])
    pack = jnp.pad(pack, ((0, 4), (0, 128 - PIECE)))
    return sh_qkvo, sh_in, sh_out, pack


def leave_kernel(result_in, grad_in, total, sums, result, grad_tok, *refs):
    weights, vectors, inner_bias, rms = refs[:6], refs[6:14], refs[14], refs[15]
    result[...] = result_in[...]
    grad_tok[...] = grad_in[...]
    for k in range(4):

        @pl.when(pl.program_id(0) == k)
        def _(k=k):
            weights[k][...] = total[0]

    weights[4][...] = total[1]
    weights[5][...] = total[2]
    for k in range(8):
        vectors[k][...] = sums[k : k + 1, :PIECE]
    inner = jnp.zeros((1, 256), F32)
    for k in range(4):
        row = jnp.where(lanes(1) < PIECE, sums[8 + k : 9 + k], 0.0)
        inner += pltpu.roll(jnp.concatenate([row, jnp.zeros_like(row)], axis=1), PIECE * k, 1)
    inner_bias[...] = inner[:, : 4 * PIECE]
    rms[...] = jnp.sqrt(sums[12:13, 0:4] / sums[12:13, 4:5])


def leave_call(result, grad_tok, total, sums):
    rows = pl.BlockSpec((BLOCK, WIDTH), lambda k: (k, 0))
    kept = lambda shape: pl.BlockSpec(shape, lambda k: (0, 0))
    outs = [jax.ShapeDtypeStruct((SEQ, WIDTH), BF)] * 2
    outs += [jax.ShapeDtypeStruct((PIECE, WIDTH), F32)] * 4
    outs += [jax.ShapeDtypeStruct((4 * PIECE, WIDTH), F32), jax.ShapeDtypeStruct((PIECE, 4 * WIDTH), F32)]
    outs += [jax.ShapeDtypeStruct((1, PIECE), F32)] * 8
    outs += [jax.ShapeDtypeStruct((1, 4 * PIECE), F32), jax.ShapeDtypeStruct((1, 4), F32)]
    return pl.pallas_call(
        leave_kernel,
        out_shape=outs,
        grid=(4,),
        in_specs=[rows, rows, pl.BlockSpec((3, PIECE, WIDTH), lambda k: (0, 0, k)), kept((16, 128))],
        out_specs=[rows, rows, *[kept((PIECE, WIDTH))] * 4]
        + [pl.BlockSpec((PIECE, WIDTH), lambda k: (k, 0)), pl.BlockSpec((PIECE, WIDTH), lambda k: (0, k))]
        + [kept((1, PIECE))] * 8
        + [kept((1, 4 * PIECE)), kept((1, 4))],
        compiler_params=pltpu.CompilerParams(vmem_limit_bytes=60 * 2**20),
        name="leave",
    )(result, grad_tok, total, sums)


def fast_body(
    tokens, segment_ids, cotangent,
    weight_query, weight_key, weight_value, weight_output, weight_inner, weight_outer,
    bias_query, bias_value, bias_output, bias_inner, bias_outer, gain_attn, shift_attn, gain_ffn, shift_ffn,
):
    tok, cot = tokens.reshape(SEQ, WIDTH), cotangent.reshape(SEQ, WIDTH)
    weights = (weight_query, weight_key, weight_value, weight_output, weight_inner, weight_outer)
    vectors = (gain_attn, shift_attn, bias_query, bias_value, bias_output, bias_outer, gain_ffn, shift_ffn)
    vectors = [v.reshape(1, -1) for v in (*vectors, bias_inner)]
    made = leave_call(*layer_call(tok, cot, segment_ids, [w.T for w in weights], vectors))
    grads, own, inner_bias, rms = [g.T for g in made[2:8]], [v.reshape(PIECE) for v in made[8:16]], made[16], made[17]
    g_attn, s_attn, b_query, b_value, b_output, b_outer, g_ffn, s_ffn = own
    return (
        made[0].reshape(tokens.shape), made[1].reshape(tokens.shape), *grads,
        b_query, b_value, b_output, inner_bias.reshape(4 * PIECE), b_outer, g_attn, s_attn, g_ffn, s_ffn,
        rms.reshape(4),
    )


def scaled(values, gain_vec):
    average = jnp.mean(values, axis=-1, keepdims=True)
    centered = values - average
    spread = jnp.mean(centered * centered, axis=-1, keepdims=True)
    return centered * lax.rsqrt(spread + 1e-06) * gain_vec


def matmul(operand, matrix):
    return jnp.dot(operand, matrix, preferred_element_type=jnp.float32)


def over_rows(operand, other):
    return lax.dot_general(
        operand, other, (((0,), (0,)), ((), ())), preferred_element_type=jnp.float32
    )


def against(operand, matrix):
    return lax.dot_general(
        operand, matrix, (((1,), (1,)), ((), ())), preferred_element_type=jnp.float32
    )


def pair_of(block, offset, seq_len):
    return lax.dynamic_slice_in_dim(block, offset, 2 * HD, 1).reshape(seq_len, 2, HD)


def masked_scores(query_pair, key_pair, same_doc, factor):
    scores = (
        jnp.einsum("qhd,khd->hqk", query_pair, key_pair, preferred_element_type=jnp.float32)
        * factor
    )
    return jnp.where(same_doc, scores, -1e30)


def attend_forward(queries, key_rows, value_rows, doc_ids):
    seq_len, features = queries.shape
    pair_width = 2 * HD
    factor = 1.0 / math.sqrt(HD)
    same_doc = (doc_ids[:, None] == doc_ids[None, :])[None]

    def one_pair(which, buffers):
        attended, logsum = buffers
        offset = which * pair_width
        query_pair = pair_of(queries, offset, seq_len)
        key_pair = pair_of(key_rows, offset, seq_len)
        value_pair = pair_of(value_rows, offset, seq_len)
        scores = masked_scores(query_pair, key_pair, same_doc, factor)
        largest = jnp.max(scores, axis=-1, keepdims=True)
        exponent = jnp.exp(scores - largest)
        denominator = jnp.sum(exponent, axis=-1, keepdims=True)
        probability = (exponent / denominator).astype(jnp.bfloat16)
        mixed_pair = jnp.einsum(
            "hqk,khd->qhd", probability, value_pair, preferred_element_type=jnp.float32
        )
        attended = lax.dynamic_update_slice_in_dim(
            attended, mixed_pair.reshape(seq_len, pair_width), offset, 1
        )
        logsum = lax.dynamic_update_slice_in_dim(
            logsum, (largest + jnp.log(denominator))[:, :, 0], which * 2, 0
        )
        return (attended, logsum)

    initial = (
        jnp.zeros((seq_len, features), jnp.float32),
        jnp.zeros((features // HD, seq_len), jnp.float32),
    )
    return lax.fori_loop(0, features // pair_width, one_pair, initial)


def attend_backward(queries, key_rows, value_rows, upstream, logsum, doc_ids):
    seq_len, features = queries.shape
    pair_width = 2 * HD
    factor = 1.0 / math.sqrt(HD)
    same_doc = (doc_ids[:, None] == doc_ids[None, :])[None]

    def one_pair(which, buffers):
        grad_queries, grad_keys, grad_values = buffers
        offset = which * pair_width
        query_pair = pair_of(queries, offset, seq_len)
        key_pair = pair_of(key_rows, offset, seq_len)
        value_pair = pair_of(value_rows, offset, seq_len)
        upper_pair = pair_of(upstream, offset, seq_len)
        logsum_pair = lax.dynamic_slice_in_dim(logsum, which * 2, 2, 0)
        scores = masked_scores(query_pair, key_pair, same_doc, factor)
        probability = jnp.exp(scores - logsum_pair[:, :, None])
        rounded = probability.astype(jnp.bfloat16)
        value_part = jnp.einsum(
            "hqk,qhd->khd", rounded, upper_pair, preferred_element_type=jnp.float32
        )
        prob_grad = jnp.einsum(
            "qhd,khd->hqk", upper_pair, value_pair, preferred_element_type=jnp.float32
        )
        weighted = jnp.sum(probability * prob_grad, axis=-1, keepdims=True)
        score_grad = (probability * (prob_grad - weighted)).astype(jnp.bfloat16)
        query_part = (
            jnp.einsum("hqk,khd->qhd", score_grad, key_pair, preferred_element_type=jnp.float32)
            * factor
        )
        key_part = (
            jnp.einsum("hqk,qhd->khd", score_grad, query_pair, preferred_element_type=jnp.float32)
            * factor
        )
        grad_queries = lax.dynamic_update_slice_in_dim(
            grad_queries, query_part.reshape(seq_len, pair_width), offset, 1
        )
        grad_keys = lax.dynamic_update_slice_in_dim(
            grad_keys, key_part.reshape(seq_len, pair_width), offset, 1
        )
        grad_values = lax.dynamic_update_slice_in_dim(
            grad_values, value_part.reshape(seq_len, pair_width), offset, 1
        )
        return (grad_queries, grad_keys, grad_values)

    empty_buf = jnp.zeros((seq_len, features), jnp.float32)
    return lax.fori_loop(0, features // pair_width, one_pair, (empty_buf, empty_buf, empty_buf))


def plain_body(
    tokens,
    segment_ids,
    cotangent,
    weight_query,
    weight_key,
    weight_value,
    weight_output,
    weight_inner,
    weight_outer,
    bias_query,
    bias_value,
    bias_output,
    bias_inner,
    bias_outer,
    gain_attn,
    shift_attn,
    gain_ffn,
    shift_ffn,
):
    gathered = (
        lax.all_gather(weight_query, "fsdp", axis=1, tiled=True),
        lax.all_gather(weight_key, "fsdp", axis=1, tiled=True),
        lax.all_gather(weight_value, "fsdp", axis=1, tiled=True),
        lax.all_gather(weight_output, "fsdp", axis=1, tiled=True),
        lax.all_gather(weight_inner, "fsdp", axis=1, tiled=True),
        lax.all_gather(weight_outer, "fsdp", axis=1, tiled=True),
        lax.all_gather(bias_query, "fsdp", axis=0, tiled=True),
        lax.all_gather(bias_value, "fsdp", axis=0, tiled=True),
        lax.all_gather(bias_output, "fsdp", axis=0, tiled=True),
        lax.all_gather(bias_inner, "fsdp", axis=0, tiled=True),
        lax.all_gather(bias_outer, "fsdp", axis=0, tiled=True),
        lax.all_gather(gain_attn, "fsdp", axis=0, tiled=True),
        lax.all_gather(shift_attn, "fsdp", axis=0, tiled=True),
        lax.all_gather(gain_ffn, "fsdp", axis=0, tiled=True),
        lax.all_gather(shift_ffn, "fsdp", axis=0, tiled=True),
    )
    (
        whole_query,
        whole_key,
        whole_value,
        whole_output,
        whole_inner,
        whole_outer,
        query_bias,
        value_bias,
        output_bias,
        inner_bias,
        outer_bias,
        attn_gain,
        attn_shift,
        ffn_gain,
        ffn_shift,
    ) = gathered
    count_seq, seq_len, features = tokens.shape
    row_count = count_seq * seq_len
    stream = tokens.reshape(row_count, features).astype(jnp.float32)
    normed = (
        scaled(stream, attn_gain.astype(jnp.float32)) + attn_shift.astype(jnp.float32)
    ).astype(jnp.bfloat16)
    queries = (matmul(normed, whole_query) + query_bias.astype(jnp.float32)).astype(jnp.bfloat16)
    key_rows = matmul(normed, whole_key).astype(jnp.bfloat16)
    value_rows = (matmul(normed, whole_value) + value_bias.astype(jnp.float32)).astype(jnp.bfloat16)
    query_seq = queries.reshape(count_seq, seq_len, features)
    key_seq = key_rows.reshape(count_seq, seq_len, features)
    value_seq = value_rows.reshape(count_seq, seq_len, features)
    attended, logsum = lax.map(
        lambda packed: attend_forward(*packed), (query_seq, key_seq, value_seq, segment_ids)
    )
    attended = attended.reshape(row_count, features).astype(jnp.bfloat16)
    branch = matmul(attended, whole_output) + output_bias.astype(jnp.float32)
    middle = stream + branch
    second = (scaled(middle, ffn_gain.astype(jnp.float32)) + ffn_shift.astype(jnp.float32)).astype(
        jnp.bfloat16
    )
    hidden = matmul(second, whole_inner) + inner_bias.astype(jnp.float32)
    active = jax.nn.gelu(hidden, approximate=False).astype(jnp.bfloat16)
    ffn_out = matmul(active, whole_outer) + outer_bias.astype(jnp.float32)
    result = middle + ffn_out
    valid_mask = (segment_ids != 0).reshape(row_count).astype(jnp.float32)
    squares = jnp.stack(
        [
            jnp.sum(jnp.sum(piece * piece, axis=-1) * valid_mask)
            for piece in (stream, branch, middle, ffn_out)
        ]
    )
    counted = jnp.sum(valid_mask)
    regathered = (
        lax.all_gather(weight_query, "fsdp", axis=1, tiled=True),
        lax.all_gather(weight_key, "fsdp", axis=1, tiled=True),
        lax.all_gather(weight_value, "fsdp", axis=1, tiled=True),
        lax.all_gather(weight_output, "fsdp", axis=1, tiled=True),
        lax.all_gather(weight_inner, "fsdp", axis=1, tiled=True),
        lax.all_gather(weight_outer, "fsdp", axis=1, tiled=True),
        lax.all_gather(gain_attn, "fsdp", axis=0, tiled=True),
        lax.all_gather(gain_ffn, "fsdp", axis=0, tiled=True),
    )
    (
        back_query,
        back_key,
        back_value,
        back_output,
        back_inner,
        back_outer,
        back_attn_gain,
        back_ffn_gain,
    ) = regathered
    grad_out = cotangent.reshape(row_count, features)
    grad_outer = over_rows(active, grad_out)
    biasgrad_outer = jnp.sum(grad_out.astype(jnp.float32), axis=0)
    grad_active = against(grad_out, back_outer)
    _, gelu_back = jax.vjp(lambda values: jax.nn.gelu(values, approximate=False), hidden)
    grad_hidden = gelu_back(grad_active)[0].astype(jnp.bfloat16)
    grad_inner = over_rows(second, grad_hidden)
    biasgrad_inner = jnp.sum(grad_hidden.astype(jnp.float32), axis=0)
    grad_second = against(grad_hidden, back_inner)
    _, norm_back_ffn = jax.vjp(scaled, middle, back_ffn_gain.astype(jnp.float32))
    grad_middle, gaingrad_ffn = norm_back_ffn(grad_second)
    shiftgrad_ffn = jnp.sum(grad_second, axis=0)
    grad_middle = grad_middle + grad_out.astype(jnp.float32)
    grad_branch = grad_middle.astype(jnp.bfloat16)
    grad_output = over_rows(attended, grad_branch)
    biasgrad_output = jnp.sum(grad_branch.astype(jnp.float32), axis=0)
    grad_attended = against(grad_branch, back_output).astype(jnp.bfloat16)
    upstream_seq = grad_attended.reshape(count_seq, seq_len, features)
    grad_q_seq, grad_k_seq, grad_v_seq = lax.map(
        lambda packed: attend_backward(*packed),
        (query_seq, key_seq, value_seq, upstream_seq, logsum, segment_ids),
    )
    grad_queries = grad_q_seq.reshape(row_count, features).astype(jnp.bfloat16)
    grad_keys = grad_k_seq.reshape(row_count, features).astype(jnp.bfloat16)
    grad_values = grad_v_seq.reshape(row_count, features).astype(jnp.bfloat16)
    grad_query = over_rows(normed, grad_queries)
    grad_key = over_rows(normed, grad_keys)
    grad_value = over_rows(normed, grad_values)
    biasgrad_query = jnp.sum(grad_queries.astype(jnp.float32), axis=0)
    biasgrad_value = jnp.sum(grad_values.astype(jnp.float32), axis=0)
    grad_normed = (
        against(grad_queries, back_query)
        + against(grad_keys, back_key)
        + against(grad_values, back_value)
    )
    _, norm_back_attn = jax.vjp(scaled, stream, back_attn_gain.astype(jnp.float32))
    grad_stream, gaingrad_attn = norm_back_attn(grad_normed)
    shiftgrad_attn = jnp.sum(grad_normed, axis=0)
    grad_input = (grad_middle + grad_stream).astype(jnp.bfloat16).reshape(tokens.shape)
    square_total, count_total = lax.psum((squares, counted), ("fsdp", "dp"))
    reduced = (
        lax.psum_scatter(grad_query, "fsdp", scatter_dimension=1, tiled=True),
        lax.psum_scatter(grad_key, "fsdp", scatter_dimension=1, tiled=True),
        lax.psum_scatter(grad_value, "fsdp", scatter_dimension=1, tiled=True),
        lax.psum_scatter(grad_output, "fsdp", scatter_dimension=1, tiled=True),
        lax.psum_scatter(grad_inner, "fsdp", scatter_dimension=1, tiled=True),
        lax.psum_scatter(grad_outer, "fsdp", scatter_dimension=1, tiled=True),
        lax.psum_scatter(biasgrad_query, "fsdp", scatter_dimension=0, tiled=True),
        lax.psum_scatter(biasgrad_value, "fsdp", scatter_dimension=0, tiled=True),
        lax.psum_scatter(biasgrad_output, "fsdp", scatter_dimension=0, tiled=True),
        lax.psum_scatter(biasgrad_inner, "fsdp", scatter_dimension=0, tiled=True),
        lax.psum_scatter(biasgrad_outer, "fsdp", scatter_dimension=0, tiled=True),
        lax.psum_scatter(gaingrad_attn, "fsdp", scatter_dimension=0, tiled=True),
        lax.psum_scatter(shiftgrad_attn, "fsdp", scatter_dimension=0, tiled=True),
        lax.psum_scatter(gaingrad_ffn, "fsdp", scatter_dimension=0, tiled=True),
        lax.psum_scatter(shiftgrad_ffn, "fsdp", scatter_dimension=0, tiled=True),
    )
    summed = (
        lax.psum(reduced[0].astype(jnp.bfloat16), "dp").astype(jnp.float32),
        lax.psum(reduced[1].astype(jnp.bfloat16), "dp").astype(jnp.float32),
        lax.psum(reduced[2].astype(jnp.bfloat16), "dp").astype(jnp.float32),
        lax.psum(reduced[3].astype(jnp.bfloat16), "dp").astype(jnp.float32),
        lax.psum(reduced[4].astype(jnp.bfloat16), "dp").astype(jnp.float32),
        lax.psum(reduced[5].astype(jnp.bfloat16), "dp").astype(jnp.float32),
        lax.psum(reduced[6].astype(jnp.bfloat16), "dp").astype(jnp.float32),
        lax.psum(reduced[7].astype(jnp.bfloat16), "dp").astype(jnp.float32),
        lax.psum(reduced[8].astype(jnp.bfloat16), "dp").astype(jnp.float32),
        lax.psum(reduced[9].astype(jnp.bfloat16), "dp").astype(jnp.float32),
        lax.psum(reduced[10].astype(jnp.bfloat16), "dp").astype(jnp.float32),
        lax.psum(reduced[11].astype(jnp.bfloat16), "dp").astype(jnp.float32),
        lax.psum(reduced[12].astype(jnp.bfloat16), "dp").astype(jnp.float32),
        lax.psum(reduced[13].astype(jnp.bfloat16), "dp").astype(jnp.float32),
        lax.psum(reduced[14].astype(jnp.bfloat16), "dp").astype(jnp.float32),
    )
    rms_stats = jnp.sqrt(square_total / (count_total * features))
    return (
        result.astype(jnp.bfloat16).reshape(tokens.shape),
        grad_input,
        summed[0],
        summed[1],
        summed[2],
        summed[3],
        summed[4],
        summed[5],
        summed[6],
        summed[7],
        summed[8],
        summed[9],
        summed[10],
        summed[11],
        summed[12],
        summed[13],
        summed[14],
        rms_stats,
    )


def solution(mesh):
    in_specs = (
        P(("fsdp", "dp"), None, None),
        P(("fsdp", "dp"), None),
        P(("fsdp", "dp"), None, None),
        P(None, "fsdp"),
        P(None, "fsdp"),
        P(None, "fsdp"),
        P(None, "fsdp"),
        P(None, "fsdp"),
        P(None, "fsdp"),
        P("fsdp"),
        P("fsdp"),
        P("fsdp"),
        P("fsdp"),
        P("fsdp"),
        P("fsdp"),
        P("fsdp"),
        P("fsdp"),
        P("fsdp"),
    )
    out_specs = (
        P(("fsdp", "dp"), None, None),
        P(("fsdp", "dp"), None, None),
        P(None, "fsdp"),
        P(None, "fsdp"),
        P(None, "fsdp"),
        P(None, "fsdp"),
        P(None, "fsdp"),
        P(None, "fsdp"),
        P("fsdp"),
        P("fsdp"),
        P("fsdp"),
        P("fsdp"),
        P("fsdp"),
        P("fsdp"),
        P("fsdp"),
        P("fsdp"),
        P("fsdp"),
        P(),
    )
    body = fast_body if dict(mesh.shape) == {"fsdp": 16, "dp": 2} else plain_body
    return jax.shard_map(body, mesh=mesh, in_specs=in_specs, out_specs=out_specs, check_vma=False)
```

```python
import math

import jax
import jax.numpy as jnp
import numpy as np
from jax import lax
from jax.experimental import pallas as pl
from jax.experimental.pallas import tpu as pltpu
from jax.sharding import PartitionSpec as P

HD = 64
BF, F32 = jnp.bfloat16, jnp.float32
MESH = pl.DeviceIdType.MESH
SEQ, WIDTH, PIECE, BLOCK, KEYS = 1024, 768, 48, 256, 512
EVERY = slice(None)


def dg(lhs, rhs, lhs_dim, rhs_dim):
    return lax.dot_general(
        lhs, rhs, (((lhs_dim,), (rhs_dim,)), ((), ())), preferred_element_type=F32
    )


def lanes(rows):
    return lax.broadcasted_iota(jnp.int32, (rows, 128), 1)


def piece(k):
    return slice(k * WIDTH, (k + 1) * WIDTH)


def aligned(start, size, unit=128):
    return pl.ds(pl.multiple_of(start, unit), size)


def iota_of(shape, axis):
    return lax.broadcasted_iota(jnp.int32, shape, axis)


def chosen(mask):
    return jnp.where(mask, 1.0, 0.0)


class Place:
    def __init__(self):
        index = lax.axis_index("fsdp")
        self.core = lax.axis_index("dp")
        self.x = lax.rem(index, 2)
        self.y = lax.rem(lax.div(index, 2), 2)
        self.z = lax.div(index, 4)

    def at(self, z=None, y=None, x=None, core=None):
        z = self.z if z is None else z
        y = self.y if y is None else y
        x = self.x if x is None else x
        return (z * 4 + y * 2 + x, self.core if core is None else core)

    def z_after(self, step):
        return lax.rem(self.z + step, 4)

    def z_peer(self, step):
        return self.at(z=self.z_after(step))

    def y_peer(self):
        return self.at(y=1 - self.y)

    def x_peer(self):
        return self.at(x=1 - self.x)

    def core_peer(self):
        return self.at(core=1 - self.core)

    def greet(self):
        ready = pltpu.get_barrier_semaphore()
        peers = [self.z_peer(1), self.z_peer(2), self.z_peer(3)]
        peers += [self.y_peer(), self.x_peer(), self.core_peer()]
        for peer in peers:
            pl.semaphore_signal(ready, inc=1, device_id=peer, device_id_type=MESH)
        pl.semaphore_wait(ready, len(peers))


class Moves:
    def __init__(self, send, recv, first):
        self.send, self.recv, self.first, self.made = send, recv, first, {}

    def add(self, name, src, dst, peer):
        slot = self.first + len(self.made)
        self.made[name] = lambda: pltpu.make_async_remote_copy(
            src_ref=src(),
            dst_ref=dst(),
            send_sem=self.send.at[slot],
            recv_sem=self.recv.at[slot],
            device_id=peer(),
            device_id_type=MESH,
        )

    def start(self, *names):
        for name in names:
            self.made[name]().start()

    def landed(self, *names):
        for name in names:
            self.made[name]().wait_recv()

    def sent(self):
        for make in self.made.values():
            make().wait_send()


GATHER_MOVES = 14


class Gather(Moves):
    def __init__(self, me, view, out, local, send, recv, slot, first, half, z_between=False, share=2):
        super().__init__(send, recv, slot * GATHER_MOVES)
        self.view = view
        self.local_sem = local.at[slot]
        cut = half * share // 3 if half == 384 else half // 2
        start = first + me.core * half
        a, b = aligned(start, cut), aligned(start + cut, half - cut)
        own = lambda: out.at[me.z, me.y, me.x, :, aligned(start, half)]
        self.own = own

        def same(name, view, peer):
            self.add(name, view, view, peer)

        def along_z(name, src, dst):
            for step in (1, 2, 3):
                self.add((name, step), src, dst, lambda step=step: me.z_peer(step))

        if z_between:
            part_a = lambda: out.at[me.z, me.y, me.x, :, a]
            part_b = lambda: out.at[me.z, me.y, me.x, :, b]
            self.add("a", lambda: view().at[:, 0:cut], part_a, me.x_peer)
            self.add("b", lambda: view().at[:, cut:half], part_b, me.y_peer)
            along_z("za", lambda: out.at[me.z, me.y, :, :, a], lambda: out.at[me.z, me.y, :, :, a])
            along_z("zb", lambda: out.at[me.z, :, me.x, :, b], lambda: out.at[me.z, :, me.x, :, b])
            near_a, near_b = lambda: out.at[:, me.y, :, :, a], lambda: out.at[:, :, me.x, :, b]
            same("a2", near_a, me.y_peer)
            same("b2", near_b, me.x_peer)
            far_a, far_b = lambda: out.at[:, 1 - me.y, :, :, a], lambda: out.at[:, :, 1 - me.x, :, b]
            self.phases = [["a", "b"], [("za", k) for k in (2, 1, 3)] + [("zb", k) for k in (2, 1, 3)]]
        else:
            along_z("z", view, own)
            same("a1", lambda: out.at[:, me.y, me.x, :, a], me.y_peer)
            same("b1", lambda: out.at[:, me.y, me.x, :, b], me.x_peer)
            near_a, near_b = lambda: out.at[:, :, me.x, :, a], lambda: out.at[:, me.y, :, :, b]
            same("a2", near_a, me.x_peer)
            same("b2", near_b, me.y_peer)
            far_a, far_b = lambda: out.at[:, :, 1 - me.x, :, a], lambda: out.at[:, 1 - me.y, :, :, b]
            self.phases = [[("z", 2), ("z", 1), ("z", 3)], ["a1", "b1"]]
        same("near a", near_a, me.core_peer)
        same("near b", near_b, me.core_peer)
        same("far a", far_a, me.core_peer)
        same("far b", far_b, me.core_peer)
        self.phases += [["a2", "b2"], ["far a", "far b"]]

    def local(self):
        return pltpu.make_async_copy(self.view(), self.own(), self.local_sem)

    def step(self, number):
        if number == 0:
            self.start(*self.phases[0])
            self.local().start()
            return
        self.landed(*self.phases[number - 1])
        if number == 1:
            self.local().wait()
        if number == 4:
            self.landed("near a", "near b")
            self.sent()
            return
        self.start(*self.phases[number])
        if number == 2:
            self.start("near a", "near b")


class VectorGather(Moves):
    def __init__(self, me, src, out, local, send, recv, first):
        super().__init__(send, recv, first)
        own = lambda: out.at[me.z, me.y, me.x]
        self.copy = lambda: pltpu.make_async_copy(src, own(), local)
        for step in (1, 2, 3):
            self.add(("z", step), lambda: src, own, lambda step=step: me.z_peer(step))
        self.add("y", lambda: out.at[:, me.y, me.x], lambda: out.at[:, me.y, me.x], me.y_peer)
        self.add("x", lambda: out.at[:, :, me.x], lambda: out.at[:, :, me.x], me.x_peer)

    def step(self, number):
        if number == 0:
            self.copy().start()
            self.start(("z", 1), ("z", 2), ("z", 3))
        if number == 1:
            self.copy().wait()
            self.landed(("z", 1), ("z", 2), ("z", 3))
            self.start("y")
        if number == 2:
            self.landed("y")
            self.start("x")
        if number == 3:
            self.landed("x")
            self.sent()


REDUCE_MOVES = 9


class Reduce(Moves):
    def __init__(self, me, grads, total, boxes, send, recv, slot, first, half, group):
        super().__init__(send, recv, slot)
        from_core, from_a1, from_b1, from_a2, from_b2, from_z = boxes
        self.me, self.grads, self.total, self.boxes = me, grads, total, boxes
        cut = half * 2 // 3 if half == 384 else half // 2
        start = first + me.core * half
        self.half = half
        self.mine = mine = aligned(start, half)
        theirs = aligned(first + (1 - me.core) * half, half)
        self.a, self.b = a, b = aligned(start, cut), aligned(start + cut, half - cut)
        self.group = group
        self.add("core", lambda: grads.at[:, :, :, :, theirs], lambda: from_core, me.core_peer)
        self.add("a1", lambda: grads.at[:, 1 - me.y, :, :, a], lambda: from_a1, me.y_peer)
        self.add("b1", lambda: grads.at[:, :, 1 - me.x, :, b], lambda: from_b1, me.x_peer)
        self.add("a2", lambda: grads.at[:, me.y, 1 - me.x, :, a], lambda: from_a2, me.x_peer)
        self.add("b2", lambda: grads.at[:, 1 - me.y, me.x, :, b], lambda: from_b2, me.y_peer)
        for step in (1, 2, 3):
            self.add(
                ("z", step),
                lambda step=step: grads.at[me.z_after(step), me.y, me.x, :, mine],
                lambda step=step: from_z.at[step - 1],
                lambda step=step: me.z_peer(step),
            )
        self.add("last", lambda: total.at[group, :, mine], lambda: total.at[group, :, mine], me.core_peer)

    def step(self, number):
        me, grads = self.me, self.grads
        from_core, from_a1, from_b1, from_a2, from_b2, from_z = self.boxes
        a, b, mine = self.a, self.b, self.mine

        def plus(left, right):
            return left + right

        if number == 0:
            self.start("core")
        if number == 1:
            self.landed("core")

            @pl.loop(0, 4)
            def _(z):
                for y in range(2):
                    for x in range(2):
                        grads[z, y, x, :, mine] = plus(
                            grads[z, y, x, :, mine], from_core[z, y, x]
                        )

            self.start("a1", "b1")
        if number == 2:
            self.landed("a1", "b1")

            @pl.loop(0, 4)
            def _(z):
                for k in range(2):
                    grads[z, me.y, k, :, a] = plus(grads[z, me.y, k, :, a], from_a1[z, k])
                    grads[z, k, me.x, :, b] = plus(grads[z, k, me.x, :, b], from_b1[z, k])

            self.start("a2", "b2")
        if number == 3:
            self.landed("a2", "b2")

            @pl.loop(0, 4)
            def _(z):
                grads[z, me.y, me.x, :, a] = plus(grads[z, me.y, me.x, :, a], from_a2[z])
                grads[z, me.y, me.x, :, b] = plus(grads[z, me.y, me.x, :, b], from_b2[z])

            self.start(("z", 2), ("z", 1), ("z", 3))
        if number == 4:
            self.landed(("z", 1), ("z", 2), ("z", 3))
            terms = [from_z[k].astype(F32) for k in range(3)]
            own = grads[me.z, me.y, me.x, :, mine].astype(F32)
            self.total[self.group, :, mine] = (own + terms[0]) + (terms[1] + terms[2])
            self.start("last")
        if number == 5:
            self.landed("last")
            self.sent()


def boxes_for(half):
    cut = half * 2 // 3 if half == 384 else half // 2
    return [
        pltpu.VMEM((4, 2, 2, PIECE, half), BF),
        pltpu.VMEM((4, 2, PIECE, cut), BF),
        pltpu.VMEM((4, 2, PIECE, half - cut), BF),
        pltpu.VMEM((4, PIECE, cut), BF),
        pltpu.VMEM((4, PIECE, half - cut), BF),
        pltpu.VMEM((3, PIECE, half), BF),
    ]


class VectorSum(Moves):
    def __init__(self, me, table, parts, boxes, mine, send, recv, first):
        super().__init__(send, recv, first)
        from_core, from_y, from_x, from_z = boxes
        self.me, self.table, self.parts, self.boxes, self.mine = me, table, parts, boxes, mine
        self.add("core", lambda: parts, lambda: from_core, me.core_peer)
        self.add("y", lambda: from_core.at[:, 1 - me.y], lambda: from_y, me.y_peer)
        self.add("x", lambda: from_core.at[:, me.y, 1 - me.x], lambda: from_x, me.x_peer)
        for step in (1, 2, 3):
            self.add(
                ("z", step),
                lambda step=step: from_core.at[me.z_after(step), me.y, me.x],
                lambda step=step: from_z.at[step - 1],
                lambda step=step: me.z_peer(step),
            )

    def cut(self):
        table, parts = self.table, self.parts
        totals = jnp.sum(table[8:24], axis=1, keepdims=True)
        lane = lanes(1)
        row = jnp.zeros((1, 128), F32)
        for k in range(5):
            row = jnp.where(lane == k, totals[4 + k : 5 + k], row)
        for m in range(16):
            first = pltpu.roll(table[0:8], (WIDTH - PIECE * m) % WIDTH, 1)[:, :128]
            inner = pltpu.roll(table[8:16], (WIDTH - PIECE * m) % WIDTH, 1)[:, :128]
            parts[m // 4, m // 2 % 2, m % 2, 0:8] = first
            parts[m // 4, m // 2 % 2, m % 2, 12:13] = row
            for b in range(4):
                f = 4 * b + m // 4
                spot = 8 + m % 4
                parts[f // 4, f // 2 % 2, f % 2, spot : spot + 1] = inner[b : b + 1]

    def step(self, number):
        me, parts = self.me, self.parts
        from_core, from_y, from_x, from_z = self.boxes
        along_z = (("z", 1), ("z", 2), ("z", 3))
        if number == 0:
            self.cut()
            self.start("core")
        if number == 1:
            self.landed("core")
            from_core[...] = from_core[...] + parts[...]
            self.start("y")
        if number == 2:
            self.landed("y")
            from_core[:, me.y] = from_core[:, me.y] + from_y[...]
            self.start("x")
        if number == 3:
            self.landed("x")
            from_core[:, me.y, me.x] = from_core[:, me.y, me.x] + from_x[...]
            self.start(*along_z)
        if number == 4:
            self.landed(*along_z)
            own = from_core[me.z, me.y, me.x]
            self.mine[...] = (own + from_z[0]) + (from_z[1] + from_z[2])
            self.sent()


def normalized(values):
    average = jnp.mean(values, axis=-1, keepdims=True)
    centered = values - average
    spread = jnp.mean(centered * centered, axis=-1, keepdims=True)
    scale = lax.rsqrt(spread + 1e-06)
    return centered * scale, scale


def norm_grad(grad_scaled, unit, scale):
    mean_grad = jnp.mean(grad_scaled, axis=-1, keepdims=True)
    mean_both = jnp.mean(grad_scaled * unit, axis=-1, keepdims=True)
    return scale * (grad_scaled - mean_grad - unit * mean_both)


def tile_of(whole, group_cols):
    return whole[:, :, :, :, aligned(group_cols, WIDTH)].reshape(WIDTH, WIDTH)


def inner_tile(whole, k):
    parts = [whole[k, :, :, :, piece(r)].reshape(4, PIECE, WIDTH) for r in range(4)]
    return jnp.stack(parts, axis=1).reshape(WIDTH, WIDTH)


def blocks(count, body):
    @pl.loop(0, SEQ // count)
    def _(step):
        body(aligned(step * count, count, count))


N_GATHERS, N_REDUCES = 8, 8
N_COPIES = N_GATHERS * GATHER_MOVES + 5 + N_REDUCES * REDUCE_MOVES + 6


def three_terms(values, lane, first, rest):
    high = values.astype(BF).astype(F32)
    left = values - high
    middle = left.astype(BF).astype(F32)
    low = left - middle
    for k, term in enumerate((high, middle, low)):
        rest = jnp.where(lane == first + k, term, rest)
    return rest.astype(BF)


def layer_kernel(
    tok, cot, seg_row, sh_q, sh_k, sh_v, sh_o, sh_in, sh_out,
    v0, v1, v2, v3, v4, v5, v6, v7, inner_bias, pick, rows_of,
    result, grad_tok, total, sums, w_qkvo, qkv_kept, normed_kept,
    pack, seg, got, vec, big_a, big_b, first, middle, last, small_a, small_b, mid, lse, qa, ka, va, da, acc, table, parts,
    send, recv, local, *boxes,
):
    me = Place()
    pack[...] = jnp.zeros_like(pack)
    for k, values in enumerate((v0, v1, v2, v3, v4, v5, v6, v7)):
        pack[k : k + 1, :PIECE] = values[...]
    for k in range(4):
        wide = (4 * PIECE, 128)
        part = (iota_of(wide, 0) == iota_of(wide, 1) + PIECE * k) & (iota_of(wide, 1) < PIECE)
        pack[8 + k : 9 + k, :] = dg(inner_bias[...], chosen(part).astype(BF), 1, 0).astype(BF)
    me.greet()
    base = N_GATHERS * GATHER_MOVES
    vectors = VectorGather(me, pack, got, local.at[N_GATHERS], send, recv, base)
    def columns(ref, start, half):
        return lambda: ref.at[:, aligned(start + me.core * half, half)]

    def inner_rows(start):
        return lambda: sh_in.at[aligned((start + me.core) * PIECE, PIECE, PIECE)]

    spans = [(columns(ref, 0, 384), last, 768 * k, 384) for k, ref in enumerate((sh_q, sh_k, sh_v, sh_o))]
    spans += [(inner_rows(0), middle, 0, 768), (inner_rows(2), middle, 1536, 768)]
    spans += [(columns(sh_out, 0, 768), first, 0, 768), (columns(sh_out, 1536, 768), first, 1536, 768)]
    g_q, g_k, g_v, g_o, g_i01, g_i23, g_u01, g_u23 = [
        Gather(me, src, out, local, send, recv, k, start, half, k in (5, 7), 1 if k in (1, 3) else 2)
        for k, (src, out, start, half) in enumerate(spans)
    ]
    base += 5
    spans = [(last, 0, 768, 2), (last, 1536, 768, 2), (middle, 0, 768, 1), (middle, 1536, 768, 1)]
    spans += [(first, 2304, 384, 0)] + [(first, 768 * k, 384, 0) for k in range(3)]
    u01, u23, i01, i23, out, que, key, val = [
        Reduce(me, grads, total, boxes[6 * k : 6 * k + 6], send, recv, base + k * REDUCE_MOVES, start, half, group)
        for k, (grads, start, half, group) in enumerate(spans)
    ]
    vector_sum = VectorSum(me, table, parts, boxes[-4:], sums, send, recv, base + N_REDUCES * REDUCE_MOVES)

    def move(slot, src, dst):
        return lambda: pltpu.make_async_copy(src(), dst(), local.at[N_GATHERS + slot])

    q_cols, o_cols = slice(0, 3 * WIDTH), slice(3 * WIDTH, 4 * WIDTH)
    keep_normed = move(1, lambda: big_b.at[:, o_cols], lambda: normed_kept)
    keep_qkv = move(2, lambda: big_a.at[:, q_cols], lambda: qkv_kept)
    keep_w = move(3, lambda: last, lambda: w_qkvo)
    save_result = [
        move(k, lambda v=view: v(), lambda n=n: result.at[:, n * 256 : n * 256 + 256])
        for n, (k, view) in enumerate(
            ((4, lambda: qa.at[0]), (10, lambda: qa.at[1]), (11, lambda: da.at[0]))
        )
    ]
    load_qkv = move(5, lambda: qkv_kept, lambda: big_a.at[:, q_cols])
    load_w_o = move(
        6, lambda: w_qkvo.at[:, :, :, :, o_cols], lambda: first.at[:, :, :, :, o_cols]
    )
    load_w_qkv = move(
        7, lambda: w_qkvo.at[:, :, :, :, q_cols], lambda: last.at[:, :, :, :, q_cols]
    )
    load_normed = move(8, lambda: normed_kept, lambda: big_b.at[:, o_cols])
    save_grad_tok = move(9, lambda: small_a, lambda: grad_tok)

    sums_ref = table

    def tally(row, values):
        sums_ref[row : row + 1] += jnp.sum(values, axis=0, keepdims=True)

    def valid_of(rows):
        return jnp.where(seg[rows].astype(F32)[:, 0:1] != 0.0, 1.0, 0.0)

    vectors.step(0)
    g_q.step(0)
    g_k.step(0)
    ids = jnp.broadcast_to(seg_row[...].astype(F32), (8, SEQ))
    ids = jnp.where(iota_of((8, SEQ), 0) == 0, ids, 0.0).astype(BF)
    seg[...] = dg(ids, jnp.ones((8, 128), BF), 0, 0).astype(BF)
    sums_ref[...] = jnp.zeros_like(sums_ref)
    lse[...] = jnp.zeros_like(lse)
    vectors.step(1)
    g_q.step(1)
    g_v.step(0)
    vectors.step(2)
    g_k.step(1)
    g_o.step(0)
    vectors.step(3)
    g_q.step(2)
    g_v.step(1)
    g_i01.step(0)
    spread = dg(got[...].reshape(256, 128), pick[...], 1, 0)
    names = jnp.zeros((16, WIDTH), F32)
    for k in range(16):
        names += spread[16 * k : 16 * k + 16] * rows_of[k : k + 1]
    vec[...] = names
    for k in range(4):
        row = jnp.zeros((1, WIDTH), F32)
        for f in range(4):
            for r in range(4):
                spot = 16 * (4 * k + f) + 8 + r
                row += spread[spot : spot + 1] * rows_of[4 * f + r : 4 * f + r + 1]
        vec[8 + k : 9 + k] = row
    g_k.step(2)
    g_o.step(1)
    g_i23.step(0)
    lane = lanes(SEQ)
    hot = seg[...].astype(F32) == lane.astype(F32)
    for h in range(2):
        qa[h, :, 128:] = jnp.where(hot, 1.0, 0.0).astype(BF)
    ka[:, 128:] = jnp.where(hot | (lane > 8), 0.0, -1e30).astype(BF)
    va[:, 128:] = jnp.ones((SEQ, 128), BF)

    def first_norm(rows):
        stream = tok[rows].astype(F32)
        valid = valid_of(rows)
        tally(12, stream * stream * valid)
        tally(16, jnp.broadcast_to(valid, stream.shape))
        unit, _ = normalized(stream)
        big_b[rows, o_cols] = (unit * vec[0:1] + vec[1:2]).astype(BF)

    blocks(BLOCK, first_norm)
    keep_normed().start()

    def project(k, bias):
        def part(rows):
            made = dg(big_b[rows, o_cols], tile_of(last, WIDTH * k), 1, 1)
            if bias is not None:
                made = made + vec[bias : bias + 1]
            big_a[rows, piece(k)] = made.astype(BF)

        blocks(512, part)

    g_q.step(3)
    g_v.step(2)
    g_i01.step(1)
    g_u01.step(0)
    g_k.step(3)
    g_q.step(4)
    project(0, 2)
    g_o.step(2)
    g_i23.step(1)
    g_u23.step(0)
    g_k.step(4)
    project(1, None)
    g_v.step(3)
    g_v.step(4)
    project(2, 3)
    keep_qkv().start()

    def ticks(table):
        def at(pair, half):
            for moment, steps in table.items():
                if moment % 2 == half:

                    @pl.when(pair == moment // 2)
                    def _(steps=steps):
                        for step in steps:
                            step()

        return at

    def s(chunk, number):
        return lambda: chunk.step(number)

    forward_ticks = ticks(
        {
            0: [s(g_i01, 2)],
            1: [s(g_u01, 1), s(g_o, 3)],
            2: [s(g_o, 4), lambda: keep_w().start()],
            4: [s(g_i23, 2), s(g_u23, 1)],
            5: [s(g_i01, 3)],
            6: [s(g_i01, 4), s(g_u01, 2)],
            8: [s(g_i23, 3)],
            10: [s(g_i23, 4), s(g_u23, 2)],
        }
    )

    @pl.loop(0, WIDTH // 128)
    def _(pair):
        forward_ticks(pair, 0)
        spot = pair * 128
        query = big_a[:, aligned(spot, 128)].astype(F32) * 0.125
        lane = lanes(SEQ)
        qa[0, :, :128] = jnp.where(lane < 64, query, 0.0).astype(BF)
        qa[1, :, :128] = jnp.where(lane < 64, 0.0, query).astype(BF)
        ka[:, :128] = big_a[:, aligned(WIDTH + spot, 128)]
        va[:, :128] = big_a[:, aligned(2 * WIDTH + spot, 128)]
        lane = lanes(BLOCK)
        work = [(step, h) for step in range(SEQ // BLOCK) for h in range(2)]
        mixed = [None, None]

        def score(step, h):
            return dg(qa[h, step * BLOCK : (step + 1) * BLOCK], ka[...], 1, 1)

        coming = score(*work[0])
        for number, (step, h) in enumerate(work):
            if number == len(work) // 2:
                forward_ticks(pair, 1)
            scores = coming
            if number + 1 < len(work):
                coming = score(*work[number + 1])
            rows = slice(step * BLOCK, (step + 1) * BLOCK)
            largest = jnp.max(scores, axis=1, keepdims=True)
            prob = jnp.exp(scores - largest).astype(BF)
            both = dg(prob, va[...], 1, 0)
            weight = both[:, 128:]
            mixed[h] = both[:, :128] / weight
            lse[rows] = jnp.where(lane == 2 * pair + h, largest + jnp.log(weight), lse[rows])
            if h == 1:
                both = jnp.where(lane < 64, mixed[0], mixed[1])
                small_b[rows, aligned(spot, 128)] = both.astype(BF)

    def second_norm(rows):
        valid = valid_of(rows)
        branch = dg(small_b[rows], tile_of(last, 3 * WIDTH), 1, 1) + vec[4:5]
        stream = tok[rows].astype(F32) + branch
        tally(13, branch * branch * valid)
        tally(14, stream * stream * valid)
        mid[rows] = stream
        unit, _ = normalized(stream)
        small_a[rows] = (unit * vec[6:7] + vec[7:8]).astype(BF)

    blocks(BLOCK, second_norm)
    g_u01.step(3)
    keep_normed().wait()
    keep_qkv().wait()
    for k in range(4):
        def expand(rows, k=k):
            hidden = dg(small_a[rows], inner_tile(middle, k), 1, 1) + vec[8 + k : 9 + k]
            phi = 0.5 + 0.5 * lax.erf(hidden * (0.5**0.5))
            bell = jnp.exp(hidden * hidden * -0.5) * 0.3989422804014327
            big_a[rows, piece(k)] = (hidden * phi).astype(BF)
            big_b[rows, piece(k)] = (phi + hidden * bell).astype(BF)

        blocks(BLOCK, expand)
        if k == 0:
            g_u01.step(4)
        if k == 1:
            g_u23.step(3)

    def store_grad(whole, k, left, right):
        made = dg(left, right, 0, 0).astype(BF)
        whole[:, :, :, :, piece(k)] = made.reshape(4, 2, 2, PIECE, WIDTH)

    keep_w().wait()
    store_grad(last, 0, cot[...], big_a[:, piece(0)])
    store_grad(last, 1, cot[...], big_a[:, piece(1)])
    u01.step(0)
    store_grad(last, 2, cot[...], big_a[:, piece(2)])
    store_grad(last, 3, cot[...], big_a[:, piece(3)])
    g_u23.step(4)
    u01.step(1)
    u23.step(0)
    for k in range(4):
        def through_gelu(rows, k=k):
            grad_active = dg(cot[rows], tile_of(first, k * WIDTH), 1, 0)
            grad_hidden = (grad_active * big_b[rows, piece(k)].astype(F32)).astype(BF)
            big_b[rows, piece(k)] = grad_hidden
            tally(8 + k, grad_hidden.astype(F32))

        blocks(BLOCK, through_gelu)
        if k == 1:
            u23.step(1)
    u01.step(2)

    def contract(rows):
        valid = valid_of(rows)
        ffn_out = dg(big_a[rows], first[...].reshape(WIDTH, 4 * WIDTH), 1, 1) + vec[5:6]
        tally(15, ffn_out * ffn_out * valid)
        made = (mid[rows] + ffn_out).astype(BF)
        qa[0, rows] = made[:, :256]
        qa[1, rows] = made[:, 256:512]
        da[0, rows] = made[:, 512:]

    blocks(BLOCK, contract)
    for make in save_result:
        make().start()
    load_qkv().start()
    load_w_o().start()
    u01.step(3)
    u23.step(2)

    def ffn_norm_back(rows):
        grad_second = dg(big_b[rows, piece(0)], inner_tile(middle, 0), 1, 0)
        for k in range(1, 4):
            grad_second += dg(big_b[rows, piece(k)], inner_tile(middle, k), 1, 0)
        unit, scale = normalized(mid[rows])
        tally(6, grad_second * unit)
        tally(7, grad_second)
        upper = cot[rows].astype(F32)
        tally(5, upper)
        grad_middle = upper + norm_grad(grad_second * vec[6:7], unit, scale)
        mid[rows] = grad_middle
        tally(4, grad_middle.astype(BF).astype(F32))

    blocks(BLOCK, ffn_norm_back)
    u23.step(3)
    u01.step(4)
    for k in range(4):
        made = dg(big_b[:, piece(k)], small_a[...], 0, 0).astype(BF).reshape(4, 4, PIECE, WIDTH)
        for r in range(4):
            middle[k, :, :, :, piece(r)] = made[:, r].reshape(2, 2, PIECE, WIDTH)
    i01.step(0)
    u01.step(5)
    load_normed().start()
    load_w_o().wait()

    def to_attended(rows):
        grad = dg(mid[rows].astype(BF), tile_of(first, 3 * WIDTH), 1, 0)
        big_a[rows, o_cols] = grad.astype(BF)

    blocks(512, to_attended)
    i23.step(0)
    u23.step(4)
    store_grad(first, 3, mid[...].astype(BF), small_b[...])
    i01.step(1)
    out.step(0)
    u23.step(5)
    load_w_qkv().start()
    load_qkv().wait()
    for make in save_result:
        make().wait()

    lane = lanes(SEQ)
    hot = seg[...].astype(F32) == lane.astype(F32)
    ones = (lane > 8) & (lane < 12)
    ka[:, 128:] = jnp.where(ones, 1.0, jnp.where(hot | (lane > 8), 0.0, -1e30)).astype(BF)
    va[:, 128:] = jnp.where(lane < 3, 1.0, 0.0).astype(BF)

    backward_ticks = ticks(
        {
            2: [s(i23, 1), s(out, 1)],
            4: [s(i01, 2)],
            6: [s(i01, 3), s(i23, 2)],
            8: [s(out, 2), s(i23, 3), s(i01, 4)],
            10: [s(out, 3), s(i23, 4), s(i01, 5)],
        }
    )

    @pl.loop(0, WIDTH // 128)
    def _(pair):
        backward_ticks(pair, 0)
        spot = pair * 128
        lane = lanes(SEQ)
        hot = jnp.where(seg[...].astype(F32) == lane.astype(F32), 1.0, 0.0)
        query = big_a[:, aligned(spot, 128)].astype(F32) * 0.125
        ka[:, :128] = big_a[:, aligned(WIDTH + spot, 128)]
        va[:, :128] = big_a[:, aligned(2 * WIDTH + spot, 128)]
        upper = big_a[:, aligned(3 * WIDTH + spot, 128)].astype(F32)
        both = small_b[:, aligned(spot, 128)].astype(F32) * upper
        for h in range(2):
            mine = (lane < 64) if h == 0 else (lane >= 64)
            qa[h, :, :128] = jnp.where(mine, query, 0.0).astype(BF)
            da[h, :, :128] = jnp.where(mine, upper, 0.0).astype(BF)
            level = jnp.sum(jnp.where(lane == 2 * pair + h, lse[...], 0.0), axis=1, keepdims=True)
            qa[h, :, 128:] = three_terms(jnp.broadcast_to(-level, hot.shape), lane, 9, hot)
            weighted = jnp.sum(jnp.where(mine, both, 0.0), axis=1, keepdims=True)
            da[h, :, 128:] = three_terms(
                jnp.broadcast_to(-weighted, hot.shape), lane, 0, jnp.zeros_like(hot)
            )
        for step in range(SEQ // KEYS):
            rows = slice(step * KEYS, (step + 1) * KEYS)
            for_keys, for_values = [], []
            for h in range(2):
                prob = jnp.exp(dg(ka[rows], qa[h], 1, 1))
                grad_score = (prob * dg(va[rows], da[h], 1, 1)).astype(BF)
                for_values.append(dg(prob.astype(BF), da[h, :, :128], 1, 0))
                for_keys.append(dg(grad_score, qa[h, :, :128], 1, 0))
                for_queries = dg(ka[rows, :128], grad_score, 0, 0)
                acc[h] = for_queries if step == 0 else acc[h] + for_queries
            big_b[rows, aligned(WIDTH + spot, 128)] = (for_keys[0] + for_keys[1]).astype(BF)
            big_b[rows, aligned(2 * WIDTH + spot, 128)] = (for_values[0] + for_values[1]).astype(BF)
        pair_grad = jnp.concatenate([acc[0, :64], acc[1, 64:]], axis=0) * 0.125
        big_b[:, aligned(spot, 128)] = pair_grad.T.astype(BF)

    load_normed().wait()
    store_grad(first, 0, big_b[:, piece(0)], big_b[:, o_cols])
    que.step(0)
    out.step(4)
    store_grad(first, 1, big_b[:, piece(1)], big_b[:, o_cols])
    key.step(0)
    que.step(1)
    i23.step(5)
    store_grad(first, 2, big_b[:, piece(2)], big_b[:, o_cols])
    val.step(0)
    key.step(1)
    out.step(5)
    load_w_qkv().wait()

    @pl.loop(0, SEQ // BLOCK)
    def _(step):
        rows = aligned(step * BLOCK, BLOCK, BLOCK)
        grad_normed = dg(big_b[rows, piece(0)], tile_of(last, 0), 1, 0)
        for k in range(1, 3):
            grad_normed += dg(big_b[rows, piece(k)], tile_of(last, k * WIDTH), 1, 0)
        tally(2, big_b[rows, piece(0)].astype(F32))
        tally(3, big_b[rows, piece(2)].astype(F32))
        unit, scale = normalized(tok[rows].astype(F32))
        tally(0, grad_normed * unit)
        tally(1, grad_normed)
        grad_stream = mid[rows] + norm_grad(grad_normed * vec[0:1], unit, scale)
        small_a[rows] = grad_stream.astype(BF)

        @pl.when(step == 0)
        def _():
            que.step(2)

        @pl.when(step == 1)
        def _():
            val.step(1)

        @pl.when(step == 2)
        def _():
            key.step(2)

        @pl.when(step == 3)
        def _():
            que.step(3)

    save_grad_tok().start()
    vector_sum.step(0)
    val.step(2)
    vector_sum.step(1)
    que.step(4)
    key.step(3)
    vector_sum.step(2)
    val.step(3)
    vector_sum.step(3)
    key.step(4)
    que.step(5)
    vector_sum.step(4)
    val.step(4)
    key.step(5)
    val.step(5)
    save_grad_tok().wait()


def layer_call(tok, cot, seg_row, weights, vectors):
    vmem, anywhere = pl.BlockSpec(memory_space=pltpu.VMEM), pl.BlockSpec(memory_space=pl.ANY)
    whole = (4, 2, 2, PIECE, 4 * WIDTH)
    wide = lambda k, kind: pltpu.VMEM((SEQ, k), kind)
    outs = [jax.ShapeDtypeStruct((SEQ, WIDTH), BF)] * 2
    outs += [jax.ShapeDtypeStruct((3, PIECE, 4 * WIDTH), F32), jax.ShapeDtypeStruct((16, 128), F32)]
    outs += [jax.ShapeDtypeStruct(whole, BF)]
    outs += [jax.ShapeDtypeStruct((SEQ, 3 * WIDTH), BF), jax.ShapeDtypeStruct((SEQ, WIDTH), BF)]
    scratch = [pltpu.VMEM((16, 128), BF), wide(128, BF), pltpu.VMEM((4, 2, 2, 16, 128), BF), pltpu.VMEM((16, WIDTH), F32)]
    scratch += [wide(4 * WIDTH, BF)] * 2 + [pltpu.VMEM(whole, BF)] * 3
    scratch += [wide(WIDTH, BF)] * 2 + [wide(WIDTH, F32), wide(128, F32)]
    scratch += [pltpu.VMEM((2, SEQ, 256), BF), wide(256, BF), wide(256, BF), pltpu.VMEM((2, SEQ, 256), BF)]
    scratch += [pltpu.VMEM((2, 128, SEQ), F32), pltpu.VMEM((24, WIDTH), F32), pltpu.VMEM((4, 2, 2, 16, 128), F32)]
    scratch += [pltpu.SemaphoreType.DMA((N_COPIES,))] * 2 + [pltpu.SemaphoreType.DMA((20,))]
    for half in [768] * 4 + [384] * 4:
        scratch += boxes_for(half)
    for shape in ((4, 2, 2), (4, 2), (4,), (3,)):
        scratch.append(pltpu.VMEM((*shape, 16, 128), F32))
    place = np.arange(WIDTH)
    pick = jnp.asarray((place[None, :] % PIECE == np.arange(128)[:, None]), BF)
    rows_of = jnp.asarray((place[None, :] // PIECE == np.arange(16)[:, None]), F32)
    return pl.pallas_call(
        layer_kernel,
        out_shape=outs,
        in_specs=[vmem] * 20,
        out_specs=[anywhere] * 2 + [vmem] * 2 + [anywhere] * 3,
        scratch_shapes=scratch,
        compiler_params=pltpu.CompilerParams(
            collective_id=1, has_side_effects=True, vmem_limit_bytes=63 * 2**20
        ),
        name="layer",
    )(tok, cot, seg_row, *weights, *vectors, pick, rows_of)[:4]


def packed_inputs(
    weight_query, weight_key, weight_value, weight_output, weight_inner, weight_outer,
    bias_query, bias_value, bias_output, bias_inner, bias_outer, gain_attn, shift_attn, gain_ffn, shift_ffn,
):
    four = (weight_query, weight_key, weight_value, weight_output)
    sh_qkvo = jnp.concatenate([w.T for w in four], axis=1)
    sh_in = weight_inner.T.reshape(4, PIECE, WIDTH).transpose(1, 0, 2).reshape(PIECE, 4 * WIDTH)
    sh_out = weight_outer.T.reshape(PIECE, 16, 4, PIECE).transpose(0, 2, 1, 3).reshape(PIECE, 4 * WIDTH)
    vectors = (gain_attn, shift_attn, bias_query, bias_value, bias_output, bias_outer, gain_ffn, shift_ffn)
    pack = jnp.concatenate([jnp.stack(vectors), bias_inner.reshape(4, PIECE)])
    pack = jnp.pad(pack, ((0, 4), (0, 128 - PIECE)))
    return sh_qkvo, sh_in, sh_out, pack


def leave_kernel(result_in, grad_in, total, sums, result, grad_tok, *refs):
    weights, vectors, inner_bias, rms = refs[:6], refs[6:14], refs[14], refs[15]
    result[...] = result_in[...]
    grad_tok[...] = grad_in[...]
    for k in range(4):

        @pl.when(pl.program_id(0) == k)
        def _(k=k):
            weights[k][...] = total[0]

    weights[4][...] = total[1]
    weights[5][...] = total[2]
    for k in range(8):
        vectors[k][...] = sums[k : k + 1, :PIECE]
    inner = jnp.zeros((1, 256), F32)
    for k in range(4):
        row = jnp.where(lanes(1) < PIECE, sums[8 + k : 9 + k], 0.0)
        inner += pltpu.roll(jnp.concatenate([row, jnp.zeros_like(row)], axis=1), PIECE * k, 1)
    inner_bias[...] = inner[:, : 4 * PIECE]
    rms[...] = jnp.sqrt(sums[12:13, 0:4] / sums[12:13, 4:5])


def leave_call(result, grad_tok, total, sums):
    rows = pl.BlockSpec((BLOCK, WIDTH), lambda k: (k, 0))
    kept = lambda shape: pl.BlockSpec(shape, lambda k: (0, 0))
    outs = [jax.ShapeDtypeStruct((SEQ, WIDTH), BF)] * 2
    outs += [jax.ShapeDtypeStruct((PIECE, WIDTH), F32)] * 4
    outs += [jax.ShapeDtypeStruct((4 * PIECE, WIDTH), F32), jax.ShapeDtypeStruct((PIECE, 4 * WIDTH), F32)]
    outs += [jax.ShapeDtypeStruct((1, PIECE), F32)] * 8
    outs += [jax.ShapeDtypeStruct((1, 4 * PIECE), F32), jax.ShapeDtypeStruct((1, 4), F32)]
    return pl.pallas_call(
        leave_kernel,
        out_shape=outs,
        grid=(4,),
        in_specs=[rows, rows, pl.BlockSpec((3, PIECE, WIDTH), lambda k: (0, 0, k)), kept((16, 128))],
        out_specs=[rows, rows, *[kept((PIECE, WIDTH))] * 4]
        + [pl.BlockSpec((PIECE, WIDTH), lambda k: (k, 0)), pl.BlockSpec((PIECE, WIDTH), lambda k: (0, k))]
        + [kept((1, PIECE))] * 8
        + [kept((1, 4 * PIECE)), kept((1, 4))],
        compiler_params=pltpu.CompilerParams(vmem_limit_bytes=60 * 2**20),
        name="leave",
    )(result, grad_tok, total, sums)


def fast_body(
    tokens, segment_ids, cotangent,
    weight_query, weight_key, weight_value, weight_output, weight_inner, weight_outer,
    bias_query, bias_value, bias_output, bias_inner, bias_outer, gain_attn, shift_attn, gain_ffn, shift_ffn,
):
    tok, cot = tokens.reshape(SEQ, WIDTH), cotangent.reshape(SEQ, WIDTH)
    weights = (weight_query, weight_key, weight_value, weight_output, weight_inner, weight_outer)
    vectors = (gain_attn, shift_attn, bias_query, bias_value, bias_output, bias_outer, gain_ffn, shift_ffn)
    vectors = [v.reshape(1, -1) for v in (*vectors, bias_inner)]
    made = leave_call(*layer_call(tok, cot, segment_ids, [w.T for w in weights], vectors))
    grads, own, inner_bias, rms = [g.T for g in made[2:8]], [v.reshape(PIECE) for v in made[8:16]], made[16], made[17]
    g_attn, s_attn, b_query, b_value, b_output, b_outer, g_ffn, s_ffn = own
    return (
        made[0].reshape(tokens.shape), made[1].reshape(tokens.shape), *grads,
        b_query, b_value, b_output, inner_bias.reshape(4 * PIECE), b_outer, g_attn, s_attn, g_ffn, s_ffn,
        rms.reshape(4),
    )


def scaled(values, gain_vec):
    average = jnp.mean(values, axis=-1, keepdims=True)
    centered = values - average
    spread = jnp.mean(centered * centered, axis=-1, keepdims=True)
    return centered * lax.rsqrt(spread + 1e-06) * gain_vec


def matmul(operand, matrix):
    return jnp.dot(operand, matrix, preferred_element_type=jnp.float32)


def over_rows(operand, other):
    return lax.dot_general(
        operand, other, (((0,), (0,)), ((), ())), preferred_element_type=jnp.float32
    )


def against(operand, matrix):
    return lax.dot_general(
        operand, matrix, (((1,), (1,)), ((), ())), preferred_element_type=jnp.float32
    )


def pair_of(block, offset, seq_len):
    return lax.dynamic_slice_in_dim(block, offset, 2 * HD, 1).reshape(seq_len, 2, HD)


def masked_scores(query_pair, key_pair, same_doc, factor):
    scores = (
        jnp.einsum("qhd,khd->hqk", query_pair, key_pair, preferred_element_type=jnp.float32)
        * factor
    )
    return jnp.where(same_doc, scores, -1e30)


def attend_forward(queries, key_rows, value_rows, doc_ids):
    seq_len, features = queries.shape
    pair_width = 2 * HD
    factor = 1.0 / math.sqrt(HD)
    same_doc = (doc_ids[:, None] == doc_ids[None, :])[None]

    def one_pair(which, buffers):
        attended, logsum = buffers
        offset = which * pair_width
        query_pair = pair_of(queries, offset, seq_len)
        key_pair = pair_of(key_rows, offset, seq_len)
        value_pair = pair_of(value_rows, offset, seq_len)
        scores = masked_scores(query_pair, key_pair, same_doc, factor)
        largest = jnp.max(scores, axis=-1, keepdims=True)
        exponent = jnp.exp(scores - largest)
        denominator = jnp.sum(exponent, axis=-1, keepdims=True)
        probability = (exponent / denominator).astype(jnp.bfloat16)
        mixed_pair = jnp.einsum(
            "hqk,khd->qhd", probability, value_pair, preferred_element_type=jnp.float32
        )
        attended = lax.dynamic_update_slice_in_dim(
            attended, mixed_pair.reshape(seq_len, pair_width), offset, 1
        )
        logsum = lax.dynamic_update_slice_in_dim(
            logsum, (largest + jnp.log(denominator))[:, :, 0], which * 2, 0
        )
        return (attended, logsum)

    initial = (
        jnp.zeros((seq_len, features), jnp.float32),
        jnp.zeros((features // HD, seq_len), jnp.float32),
    )
    return lax.fori_loop(0, features // pair_width, one_pair, initial)


def attend_backward(queries, key_rows, value_rows, upstream, logsum, doc_ids):
    seq_len, features = queries.shape
    pair_width = 2 * HD
    factor = 1.0 / math.sqrt(HD)
    same_doc = (doc_ids[:, None] == doc_ids[None, :])[None]

    def one_pair(which, buffers):
        grad_queries, grad_keys, grad_values = buffers
        offset = which * pair_width
        query_pair = pair_of(queries, offset, seq_len)
        key_pair = pair_of(key_rows, offset, seq_len)
        value_pair = pair_of(value_rows, offset, seq_len)
        upper_pair = pair_of(upstream, offset, seq_len)
        logsum_pair = lax.dynamic_slice_in_dim(logsum, which * 2, 2, 0)
        scores = masked_scores(query_pair, key_pair, same_doc, factor)
        probability = jnp.exp(scores - logsum_pair[:, :, None])
        rounded = probability.astype(jnp.bfloat16)
        value_part = jnp.einsum(
            "hqk,qhd->khd", rounded, upper_pair, preferred_element_type=jnp.float32
        )
        prob_grad = jnp.einsum(
            "qhd,khd->hqk", upper_pair, value_pair, preferred_element_type=jnp.float32
        )
        weighted = jnp.sum(probability * prob_grad, axis=-1, keepdims=True)
        score_grad = (probability * (prob_grad - weighted)).astype(jnp.bfloat16)
        query_part = (
            jnp.einsum("hqk,khd->qhd", score_grad, key_pair, preferred_element_type=jnp.float32)
            * factor
        )
        key_part = (
            jnp.einsum("hqk,qhd->khd", score_grad, query_pair, preferred_element_type=jnp.float32)
            * factor
        )
        grad_queries = lax.dynamic_update_slice_in_dim(
            grad_queries, query_part.reshape(seq_len, pair_width), offset, 1
        )
        grad_keys = lax.dynamic_update_slice_in_dim(
            grad_keys, key_part.reshape(seq_len, pair_width), offset, 1
        )
        grad_values = lax.dynamic_update_slice_in_dim(
            grad_values, value_part.reshape(seq_len, pair_width), offset, 1
        )
        return (grad_queries, grad_keys, grad_values)

    empty_buf = jnp.zeros((seq_len, features), jnp.float32)
    return lax.fori_loop(0, features // pair_width, one_pair, (empty_buf, empty_buf, empty_buf))


def plain_body(
    tokens,
    segment_ids,
    cotangent,
    weight_query,
    weight_key,
    weight_value,
    weight_output,
    weight_inner,
    weight_outer,
    bias_query,
    bias_value,
    bias_output,
    bias_inner,
    bias_outer,
    gain_attn,
    shift_attn,
    gain_ffn,
    shift_ffn,
):
    gathered = (
        lax.all_gather(weight_query, "fsdp", axis=1, tiled=True),
        lax.all_gather(weight_key, "fsdp", axis=1, tiled=True),
        lax.all_gather(weight_value, "fsdp", axis=1, tiled=True),
        lax.all_gather(weight_output, "fsdp", axis=1, tiled=True),
        lax.all_gather(weight_inner, "fsdp", axis=1, tiled=True),
        lax.all_gather(weight_outer, "fsdp", axis=1, tiled=True),
        lax.all_gather(bias_query, "fsdp", axis=0, tiled=True),
        lax.all_gather(bias_value, "fsdp", axis=0, tiled=True),
        lax.all_gather(bias_output, "fsdp", axis=0, tiled=True),
        lax.all_gather(bias_inner, "fsdp", axis=0, tiled=True),
        lax.all_gather(bias_outer, "fsdp", axis=0, tiled=True),
        lax.all_gather(gain_attn, "fsdp", axis=0, tiled=True),
        lax.all_gather(shift_attn, "fsdp", axis=0, tiled=True),
        lax.all_gather(gain_ffn, "fsdp", axis=0, tiled=True),
        lax.all_gather(shift_ffn, "fsdp", axis=0, tiled=True),
    )
    (
        whole_query,
        whole_key,
        whole_value,
        whole_output,
        whole_inner,
        whole_outer,
        query_bias,
        value_bias,
        output_bias,
        inner_bias,
        outer_bias,
        attn_gain,
        attn_shift,
        ffn_gain,
        ffn_shift,
    ) = gathered
    count_seq, seq_len, features = tokens.shape
    row_count = count_seq * seq_len
    stream = tokens.reshape(row_count, features).astype(jnp.float32)
    normed = (
        scaled(stream, attn_gain.astype(jnp.float32)) + attn_shift.astype(jnp.float32)
    ).astype(jnp.bfloat16)
    queries = (matmul(normed, whole_query) + query_bias.astype(jnp.float32)).astype(jnp.bfloat16)
    key_rows = matmul(normed, whole_key).astype(jnp.bfloat16)
    value_rows = (matmul(normed, whole_value) + value_bias.astype(jnp.float32)).astype(jnp.bfloat16)
    query_seq = queries.reshape(count_seq, seq_len, features)
    key_seq = key_rows.reshape(count_seq, seq_len, features)
    value_seq = value_rows.reshape(count_seq, seq_len, features)
    attended, logsum = lax.map(
        lambda packed: attend_forward(*packed), (query_seq, key_seq, value_seq, segment_ids)
    )
    attended = attended.reshape(row_count, features).astype(jnp.bfloat16)
    branch = matmul(attended, whole_output) + output_bias.astype(jnp.float32)
    middle = stream + branch
    second = (scaled(middle, ffn_gain.astype(jnp.float32)) + ffn_shift.astype(jnp.float32)).astype(
        jnp.bfloat16
    )
    hidden = matmul(second, whole_inner) + inner_bias.astype(jnp.float32)
    active = jax.nn.gelu(hidden, approximate=False).astype(jnp.bfloat16)
    ffn_out = matmul(active, whole_outer) + outer_bias.astype(jnp.float32)
    result = middle + ffn_out
    valid_mask = (segment_ids != 0).reshape(row_count).astype(jnp.float32)
    squares = jnp.stack(
        [
            jnp.sum(jnp.sum(piece * piece, axis=-1) * valid_mask)
            for piece in (stream, branch, middle, ffn_out)
        ]
    )
    counted = jnp.sum(valid_mask)
    regathered = (
        lax.all_gather(weight_query, "fsdp", axis=1, tiled=True),
        lax.all_gather(weight_key, "fsdp", axis=1, tiled=True),
        lax.all_gather(weight_value, "fsdp", axis=1, tiled=True),
        lax.all_gather(weight_output, "fsdp", axis=1, tiled=True),
        lax.all_gather(weight_inner, "fsdp", axis=1, tiled=True),
        lax.all_gather(weight_outer, "fsdp", axis=1, tiled=True),
        lax.all_gather(gain_attn, "fsdp", axis=0, tiled=True),
        lax.all_gather(gain_ffn, "fsdp", axis=0, tiled=True),
    )
    (
        back_query,
        back_key,
        back_value,
        back_output,
        back_inner,
        back_outer,
        back_attn_gain,
        back_ffn_gain,
    ) = regathered
    grad_out = cotangent.reshape(row_count, features)
    grad_outer = over_rows(active, grad_out)
    biasgrad_outer = jnp.sum(grad_out.astype(jnp.float32), axis=0)
    grad_active = against(grad_out, back_outer)
    _, gelu_back = jax.vjp(lambda values: jax.nn.gelu(values, approximate=False), hidden)
    grad_hidden = gelu_back(grad_active)[0].astype(jnp.bfloat16)
    grad_inner = over_rows(second, grad_hidden)
    biasgrad_inner = jnp.sum(grad_hidden.astype(jnp.float32), axis=0)
    grad_second = against(grad_hidden, back_inner)
    _, norm_back_ffn = jax.vjp(scaled, middle, back_ffn_gain.astype(jnp.float32))
    grad_middle, gaingrad_ffn = norm_back_ffn(grad_second)
    shiftgrad_ffn = jnp.sum(grad_second, axis=0)
    grad_middle = grad_middle + grad_out.astype(jnp.float32)
    grad_branch = grad_middle.astype(jnp.bfloat16)
    grad_output = over_rows(attended, grad_branch)
    biasgrad_output = jnp.sum(grad_branch.astype(jnp.float32), axis=0)
    grad_attended = against(grad_branch, back_output).astype(jnp.bfloat16)
    upstream_seq = grad_attended.reshape(count_seq, seq_len, features)
    grad_q_seq, grad_k_seq, grad_v_seq = lax.map(
        lambda packed: attend_backward(*packed),
        (query_seq, key_seq, value_seq, upstream_seq, logsum, segment_ids),
    )
    grad_queries = grad_q_seq.reshape(row_count, features).astype(jnp.bfloat16)
    grad_keys = grad_k_seq.reshape(row_count, features).astype(jnp.bfloat16)
    grad_values = grad_v_seq.reshape(row_count, features).astype(jnp.bfloat16)
    grad_query = over_rows(normed, grad_queries)
    grad_key = over_rows(normed, grad_keys)
    grad_value = over_rows(normed, grad_values)
    biasgrad_query = jnp.sum(grad_queries.astype(jnp.float32), axis=0)
    biasgrad_value = jnp.sum(grad_values.astype(jnp.float32), axis=0)
    grad_normed = (
        against(grad_queries, back_query)
        + against(grad_keys, back_key)
        + against(grad_values, back_value)
    )
    _, norm_back_attn = jax.vjp(scaled, stream, back_attn_gain.astype(jnp.float32))
    grad_stream, gaingrad_attn = norm_back_attn(grad_normed)
    shiftgrad_attn = jnp.sum(grad_normed, axis=0)
    grad_input = (grad_middle + grad_stream).astype(jnp.bfloat16).reshape(tokens.shape)
    square_total, count_total = lax.psum((squares, counted), ("fsdp", "dp"))
    reduced = (
        lax.psum_scatter(grad_query, "fsdp", scatter_dimension=1, tiled=True),
        lax.psum_scatter(grad_key, "fsdp", scatter_dimension=1, tiled=True),
        lax.psum_scatter(grad_value, "fsdp", scatter_dimension=1, tiled=True),
        lax.psum_scatter(grad_output, "fsdp", scatter_dimension=1, tiled=True),
        lax.psum_scatter(grad_inner, "fsdp", scatter_dimension=1, tiled=True),
        lax.psum_scatter(grad_outer, "fsdp", scatter_dimension=1, tiled=True),
        lax.psum_scatter(biasgrad_query, "fsdp", scatter_dimension=0, tiled=True),
        lax.psum_scatter(biasgrad_value, "fsdp", scatter_dimension=0, tiled=True),
        lax.psum_scatter(biasgrad_output, "fsdp", scatter_dimension=0, tiled=True),
        lax.psum_scatter(biasgrad_inner, "fsdp", scatter_dimension=0, tiled=True),
        lax.psum_scatter(biasgrad_outer, "fsdp", scatter_dimension=0, tiled=True),
        lax.psum_scatter(gaingrad_attn, "fsdp", scatter_dimension=0, tiled=True),
        lax.psum_scatter(shiftgrad_attn, "fsdp", scatter_dimension=0, tiled=True),
        lax.psum_scatter(gaingrad_ffn, "fsdp", scatter_dimension=0, tiled=True),
        lax.psum_scatter(shiftgrad_ffn, "fsdp", scatter_dimension=0, tiled=True),
    )
    summed = (
        lax.psum(reduced[0].astype(jnp.bfloat16), "dp").astype(jnp.float32),
        lax.psum(reduced[1].astype(jnp.bfloat16), "dp").astype(jnp.float32),
        lax.psum(reduced[2].astype(jnp.bfloat16), "dp").astype(jnp.float32),
        lax.psum(reduced[3].astype(jnp.bfloat16), "dp").astype(jnp.float32),
        lax.psum(reduced[4].astype(jnp.bfloat16), "dp").astype(jnp.float32),
        lax.psum(reduced[5].astype(jnp.bfloat16), "dp").astype(jnp.float32),
        lax.psum(reduced[6].astype(jnp.bfloat16), "dp").astype(jnp.float32),
        lax.psum(reduced[7].astype(jnp.bfloat16), "dp").astype(jnp.float32),
        lax.psum(reduced[8].astype(jnp.bfloat16), "dp").astype(jnp.float32),
        lax.psum(reduced[9].astype(jnp.bfloat16), "dp").astype(jnp.float32),
        lax.psum(reduced[10].astype(jnp.bfloat16), "dp").astype(jnp.float32),
        lax.psum(reduced[11].astype(jnp.bfloat16), "dp").astype(jnp.float32),
        lax.psum(reduced[12].astype(jnp.bfloat16), "dp").astype(jnp.float32),
        lax.psum(reduced[13].astype(jnp.bfloat16), "dp").astype(jnp.float32),
        lax.psum(reduced[14].astype(jnp.bfloat16), "dp").astype(jnp.float32),
    )
    rms_stats = jnp.sqrt(square_total / (count_total * features))
    return (
        result.astype(jnp.bfloat16).reshape(tokens.shape),
        grad_input,
        summed[0],
        summed[1],
        summed[2],
        summed[3],
        summed[4],
        summed[5],
        summed[6],
        summed[7],
        summed[8],
        summed[9],
        summed[10],
        summed[11],
        summed[12],
        summed[13],
        summed[14],
        rms_stats,
    )


def solution(mesh):
    in_specs = (
        P(("fsdp", "dp"), None, None),
        P(("fsdp", "dp"), None),
        P(("fsdp", "dp"), None, None),
        P(None, "fsdp"),
        P(None, "fsdp"),
        P(None, "fsdp"),
        P(None, "fsdp"),
        P(None, "fsdp"),
        P(None, "fsdp"),
        P("fsdp"),
        P("fsdp"),
        P("fsdp"),
        P("fsdp"),
        P("fsdp"),
        P("fsdp"),
        P("fsdp"),
        P("fsdp"),
        P("fsdp"),
    )
    out_specs = (
        P(("fsdp", "dp"), None, None),
        P(("fsdp", "dp"), None, None),
        P(None, "fsdp"),
        P(None, "fsdp"),
        P(None, "fsdp"),
        P(None, "fsdp"),
        P(None, "fsdp"),
        P(None, "fsdp"),
        P("fsdp"),
        P("fsdp"),
        P("fsdp"),
        P("fsdp"),
        P("fsdp"),
        P("fsdp"),
        P("fsdp"),
        P("fsdp"),
        P("fsdp"),
        P(),
    )
    body = fast_body if dict(mesh.shape) == {"fsdp": 16, "dp": 2} else plain_body
    return jax.shard_map(body, mesh=mesh, in_specs=in_specs, out_specs=out_specs, check_vma=False)
```

```python
import math

import jax
import jax.numpy as jnp
import numpy as np
from jax import lax
from jax.experimental import pallas as pl
from jax.experimental.pallas import tpu as pltpu
from jax.sharding import PartitionSpec as P

HD = 64
BF, F32 = jnp.bfloat16, jnp.float32
MESH = pl.DeviceIdType.MESH
SEQ, WIDTH, PIECE, BLOCK, KEYS = 1024, 768, 48, 256, 512
EVERY = slice(None)


def dg(lhs, rhs, lhs_dim, rhs_dim):
    return lax.dot_general(
        lhs, rhs, (((lhs_dim,), (rhs_dim,)), ((), ())), preferred_element_type=F32
    )


def lanes(rows):
    return lax.broadcasted_iota(jnp.int32, (rows, 128), 1)


def piece(k):
    return slice(k * WIDTH, (k + 1) * WIDTH)


def aligned(start, size, unit=128):
    return pl.ds(pl.multiple_of(start, unit), size)


def iota_of(shape, axis):
    return lax.broadcasted_iota(jnp.int32, shape, axis)


def chosen(mask):
    return jnp.where(mask, 1.0, 0.0)


class Place:
    def __init__(self):
        index = lax.axis_index("fsdp")
        self.core = lax.axis_index("dp")
        self.x = lax.rem(index, 2)
        self.y = lax.rem(lax.div(index, 2), 2)
        self.z = lax.div(index, 4)

    def at(self, z=None, y=None, x=None, core=None):
        z = self.z if z is None else z
        y = self.y if y is None else y
        x = self.x if x is None else x
        return (z * 4 + y * 2 + x, self.core if core is None else core)

    def z_after(self, step):
        return lax.rem(self.z + step, 4)

    def z_peer(self, step):
        return self.at(z=self.z_after(step))

    def y_peer(self):
        return self.at(y=1 - self.y)

    def x_peer(self):
        return self.at(x=1 - self.x)

    def core_peer(self):
        return self.at(core=1 - self.core)

    def greet(self):
        ready = pltpu.get_barrier_semaphore()
        peers = [self.z_peer(1), self.z_peer(2), self.z_peer(3)]
        peers += [self.y_peer(), self.x_peer(), self.core_peer()]
        for peer in peers:
            pl.semaphore_signal(ready, inc=1, device_id=peer, device_id_type=MESH)
        pl.semaphore_wait(ready, len(peers))


class Moves:
    def __init__(self, send, recv, first):
        self.send, self.recv, self.first, self.made = send, recv, first, {}

    def add(self, name, src, dst, peer):
        slot = self.first + len(self.made)
        self.made[name] = lambda: pltpu.make_async_remote_copy(
            src_ref=src(),
            dst_ref=dst(),
            send_sem=self.send.at[slot],
            recv_sem=self.recv.at[slot],
            device_id=peer(),
            device_id_type=MESH,
        )

    def start(self, *names):
        for name in names:
            self.made[name]().start()

    def landed(self, *names):
        for name in names:
            self.made[name]().wait_recv()

    def sent(self):
        for make in self.made.values():
            make().wait_send()


GATHER_MOVES = 14


class Gather(Moves):
    def __init__(self, me, view, out, local, send, recv, slot, first, half, z_between=False, share=2):
        super().__init__(send, recv, slot * GATHER_MOVES)
        self.view = view
        self.local_sem = local.at[slot]
        cut = half * share // 3 if half == 384 else half // 2
        start = first + me.core * half
        a, b = aligned(start, cut), aligned(start + cut, half - cut)
        own = lambda: out.at[me.z, me.y, me.x, :, aligned(start, half)]
        self.own = own

        def same(name, view, peer):
            self.add(name, view, view, peer)

        def along_z(name, src, dst):
            for step in (1, 2, 3):
                self.add((name, step), src, dst, lambda step=step: me.z_peer(step))

        if z_between:
            part_a = lambda: out.at[me.z, me.y, me.x, :, a]
            part_b = lambda: out.at[me.z, me.y, me.x, :, b]
            self.add("a", lambda: view().at[:, 0:cut], part_a, me.x_peer)
            self.add("b", lambda: view().at[:, cut:half], part_b, me.y_peer)
            along_z("za", lambda: out.at[me.z, me.y, :, :, a], lambda: out.at[me.z, me.y, :, :, a])
            along_z("zb", lambda: out.at[me.z, :, me.x, :, b], lambda: out.at[me.z, :, me.x, :, b])
            near_a, near_b = lambda: out.at[:, me.y, :, :, a], lambda: out.at[:, :, me.x, :, b]
            same("a2", near_a, me.y_peer)
            same("b2", near_b, me.x_peer)
            far_a, far_b = lambda: out.at[:, 1 - me.y, :, :, a], lambda: out.at[:, :, 1 - me.x, :, b]
            self.phases = [["a", "b"], [("za", k) for k in (2, 1, 3)] + [("zb", k) for k in (2, 1, 3)]]
        else:
            along_z("z", view, own)
            same("a1", lambda: out.at[:, me.y, me.x, :, a], me.y_peer)
            same("b1", lambda: out.at[:, me.y, me.x, :, b], me.x_peer)
            near_a, near_b = lambda: out.at[:, :, me.x, :, a], lambda: out.at[:, me.y, :, :, b]
            same("a2", near_a, me.x_peer)
            same("b2", near_b, me.y_peer)
            far_a, far_b = lambda: out.at[:, :, 1 - me.x, :, a], lambda: out.at[:, 1 - me.y, :, :, b]
            self.phases = [[("z", 2), ("z", 1), ("z", 3)], ["a1", "b1"]]
        same("near a", near_a, me.core_peer)
        same("near b", near_b, me.core_peer)
        same("far a", far_a, me.core_peer)
        same("far b", far_b, me.core_peer)
        self.phases += [["a2", "b2"], ["far a", "far b"]]

    def local(self):
        return pltpu.make_async_copy(self.view(), self.own(), self.local_sem)

    def step(self, number):
        if number == 0:
            self.start(*self.phases[0])
            self.local().start()
            return
        self.landed(*self.phases[number - 1])
        if number == 1:
            self.local().wait()
        if number == 4:
            self.landed("near a", "near b")
            self.sent()
            return
        self.start(*self.phases[number])
        if number == 2:
            self.start("near a", "near b")


class VectorGather(Moves):
    def __init__(self, me, src, out, local, send, recv, first):
        super().__init__(send, recv, first)
        own = lambda: out.at[me.z, me.y, me.x]
        self.copy = lambda: pltpu.make_async_copy(src, own(), local)
        for step in (1, 2, 3):
            self.add(("z", step), lambda: src, own, lambda step=step: me.z_peer(step))
        self.add("y", lambda: out.at[:, me.y, me.x], lambda: out.at[:, me.y, me.x], me.y_peer)
        self.add("x", lambda: out.at[:, :, me.x], lambda: out.at[:, :, me.x], me.x_peer)

    def step(self, number):
        if number == 0:
            self.copy().start()
            self.start(("z", 1), ("z", 2), ("z", 3))
        if number == 1:
            self.copy().wait()
            self.landed(("z", 1), ("z", 2), ("z", 3))
            self.start("y")
        if number == 2:
            self.landed("y")
            self.start("x")
        if number == 3:
            self.landed("x")
            self.sent()


REDUCE_MOVES = 9


class Reduce(Moves):
    def __init__(self, me, grads, total, boxes, send, recv, slot, first, half, group):
        super().__init__(send, recv, slot)
        from_core, from_a1, from_b1, from_a2, from_b2, from_z = boxes
        self.me, self.grads, self.total, self.boxes = me, grads, total, boxes
        cut = half * 2 // 3 if half == 384 else half // 2
        start = first + me.core * half
        self.half = half
        self.mine = mine = aligned(start, half)
        theirs = aligned(first + (1 - me.core) * half, half)
        self.a, self.b = a, b = aligned(start, cut), aligned(start + cut, half - cut)
        self.group = group
        self.add("core", lambda: grads.at[:, :, :, :, theirs], lambda: from_core, me.core_peer)
        self.add("a1", lambda: grads.at[:, 1 - me.y, :, :, a], lambda: from_a1, me.y_peer)
        self.add("b1", lambda: grads.at[:, :, 1 - me.x, :, b], lambda: from_b1, me.x_peer)
        self.add("a2", lambda: grads.at[:, me.y, 1 - me.x, :, a], lambda: from_a2, me.x_peer)
        self.add("b2", lambda: grads.at[:, 1 - me.y, me.x, :, b], lambda: from_b2, me.y_peer)
        for step in (1, 2, 3):
            self.add(
                ("z", step),
                lambda step=step: grads.at[me.z_after(step), me.y, me.x, :, mine],
                lambda step=step: from_z.at[step - 1],
                lambda step=step: me.z_peer(step),
            )
        self.add("last", lambda: total.at[group, :, mine], lambda: total.at[group, :, mine], me.core_peer)

    def step(self, number):
        me, grads = self.me, self.grads
        from_core, from_a1, from_b1, from_a2, from_b2, from_z = self.boxes
        a, b, mine = self.a, self.b, self.mine

        def plus(left, right):
            return left + right

        if number == 0:
            self.start("core")
        if number == 1:
            self.landed("core")

            @pl.loop(0, 4)
            def _(z):
                for y in range(2):
                    for x in range(2):
                        grads[z, y, x, :, mine] = plus(
                            grads[z, y, x, :, mine], from_core[z, y, x]
                        )

            self.start("a1", "b1")
        if number == 2:
            self.landed("a1", "b1")

            @pl.loop(0, 4)
            def _(z):
                for k in range(2):
                    grads[z, me.y, k, :, a] = plus(grads[z, me.y, k, :, a], from_a1[z, k])
                    grads[z, k, me.x, :, b] = plus(grads[z, k, me.x, :, b], from_b1[z, k])

            self.start("a2", "b2")
        if number == 3:
            self.landed("a2", "b2")

            @pl.loop(0, 4)
            def _(z):
                grads[z, me.y, me.x, :, a] = plus(grads[z, me.y, me.x, :, a], from_a2[z])
                grads[z, me.y, me.x, :, b] = plus(grads[z, me.y, me.x, :, b], from_b2[z])

            self.start(("z", 2), ("z", 1), ("z", 3))
        if number == 4:
            self.landed(("z", 1), ("z", 2), ("z", 3))
            terms = [from_z[k].astype(F32) for k in range(3)]
            own = grads[me.z, me.y, me.x, :, mine].astype(F32)
            self.total[self.group, :, mine] = (own + terms[0]) + (terms[1] + terms[2])
            self.start("last")
        if number == 5:
            self.landed("last")
            self.sent()


def boxes_for(half):
    cut = half * 2 // 3 if half == 384 else half // 2
    return [
        pltpu.VMEM((4, 2, 2, PIECE, half), BF),
        pltpu.VMEM((4, 2, PIECE, cut), BF),
        pltpu.VMEM((4, 2, PIECE, half - cut), BF),
        pltpu.VMEM((4, PIECE, cut), BF),
        pltpu.VMEM((4, PIECE, half - cut), BF),
        pltpu.VMEM((3, PIECE, half), BF),
    ]


class VectorSum(Moves):
    def __init__(self, me, table, parts, boxes, mine, send, recv, first):
        super().__init__(send, recv, first)
        from_core, from_y, from_x, from_z = boxes
        self.me, self.table, self.parts, self.boxes, self.mine = me, table, parts, boxes, mine
        self.add("core", lambda: parts, lambda: from_core, me.core_peer)
        self.add("y", lambda: from_core.at[:, 1 - me.y], lambda: from_y, me.y_peer)
        self.add("x", lambda: from_core.at[:, me.y, 1 - me.x], lambda: from_x, me.x_peer)
        for step in (1, 2, 3):
            self.add(
                ("z", step),
                lambda step=step: from_core.at[me.z_after(step), me.y, me.x],
                lambda step=step: from_z.at[step - 1],
                lambda step=step: me.z_peer(step),
            )

    def cut(self):
        table, parts = self.table, self.parts
        totals = jnp.sum(table[8:24], axis=1, keepdims=True)
        lane = lanes(1)
        row = jnp.zeros((1, 128), F32)
        for k in range(5):
            row = jnp.where(lane == k, totals[4 + k : 5 + k], row)
        for m in range(16):
            first = pltpu.roll(table[0:8], (WIDTH - PIECE * m) % WIDTH, 1)[:, :128]
            inner = pltpu.roll(table[8:16], (WIDTH - PIECE * m) % WIDTH, 1)[:, :128]
            parts[m // 4, m // 2 % 2, m % 2, 0:8] = first
            parts[m // 4, m // 2 % 2, m % 2, 12:13] = row
            for b in range(4):
                f = 4 * b + m // 4
                spot = 8 + m % 4
                parts[f // 4, f // 2 % 2, f % 2, spot : spot + 1] = inner[b : b + 1]

    def step(self, number):
        me, parts = self.me, self.parts
        from_core, from_y, from_x, from_z = self.boxes
        along_z = (("z", 1), ("z", 2), ("z", 3))
        if number == 0:
            self.cut()
            self.start("core")
        if number == 1:
            self.landed("core")
            from_core[...] = from_core[...] + parts[...]
            self.start("y")
        if number == 2:
            self.landed("y")
            from_core[:, me.y] = from_core[:, me.y] + from_y[...]
            self.start("x")
        if number == 3:
            self.landed("x")
            from_core[:, me.y, me.x] = from_core[:, me.y, me.x] + from_x[...]
            self.start(*along_z)
        if number == 4:
            self.landed(*along_z)
            own = from_core[me.z, me.y, me.x]
            self.mine[...] = (own + from_z[0]) + (from_z[1] + from_z[2])
            self.sent()


def normalized(values):
    average = jnp.mean(values, axis=-1, keepdims=True)
    centered = values - average
    spread = jnp.mean(centered * centered, axis=-1, keepdims=True)
    scale = lax.rsqrt(spread + 1e-06)
    return centered * scale, scale


def norm_grad(grad_scaled, unit, scale):
    mean_grad = jnp.mean(grad_scaled, axis=-1, keepdims=True)
    mean_both = jnp.mean(grad_scaled * unit, axis=-1, keepdims=True)
    return scale * (grad_scaled - mean_grad - unit * mean_both)


def tile_of(whole, group_cols):
    return whole[:, :, :, :, aligned(group_cols, WIDTH)].reshape(WIDTH, WIDTH)


def inner_tile(whole, k):
    parts = [whole[k, :, :, :, piece(r)].reshape(4, PIECE, WIDTH) for r in range(4)]
    return jnp.stack(parts, axis=1).reshape(WIDTH, WIDTH)


def blocks(count, body):
    @pl.loop(0, SEQ // count)
    def _(step):
        body(aligned(step * count, count, count))


N_GATHERS, N_REDUCES = 8, 8
N_COPIES = N_GATHERS * GATHER_MOVES + 5 + N_REDUCES * REDUCE_MOVES + 6


def three_terms(values, lane, first, rest):
    high = values.astype(BF).astype(F32)
    left = values - high
    middle = left.astype(BF).astype(F32)
    low = left - middle
    for k, term in enumerate((high, middle, low)):
        rest = jnp.where(lane == first + k, term, rest)
    return rest.astype(BF)


def layer_kernel(
    tok, cot, seg_row, sh_q, sh_k, sh_v, sh_o, sh_in, sh_out,
    v0, v1, v2, v3, v4, v5, v6, v7, inner_bias, pick, rows_of,
    result, grad_tok, total, sums, w_qkvo, qkv_kept, normed_kept,
    pack, seg, got, vec, big_a, big_b, first, middle, last, small_a, small_b, mid, lse, qa, ka, va, da, acc, table, parts,
    send, recv, local, *boxes,
):
    me = Place()
    pack[...] = jnp.zeros_like(pack)
    for k, values in enumerate((v0, v1, v2, v3, v4, v5, v6, v7)):
        pack[k : k + 1, :PIECE] = values[...]
    for k in range(4):
        wide = (4 * PIECE, 128)
        part = (iota_of(wide, 0) == iota_of(wide, 1) + PIECE * k) & (iota_of(wide, 1) < PIECE)
        pack[8 + k : 9 + k, :] = dg(inner_bias[...], chosen(part).astype(BF), 1, 0).astype(BF)
    me.greet()
    base = N_GATHERS * GATHER_MOVES
    vectors = VectorGather(me, pack, got, local.at[N_GATHERS], send, recv, base)
    def columns(ref, start, half):
        return lambda: ref.at[:, aligned(start + me.core * half, half)]

    def inner_rows(start):
        return lambda: sh_in.at[aligned((start + me.core) * PIECE, PIECE, PIECE)]

    spans = [(columns(ref, 0, 384), last, 768 * k, 384) for k, ref in enumerate((sh_q, sh_k, sh_v, sh_o))]
    spans += [(inner_rows(0), middle, 0, 768), (inner_rows(2), middle, 1536, 768)]
    spans += [(columns(sh_out, 0, 768), first, 0, 768), (columns(sh_out, 1536, 768), first, 1536, 768)]
    g_q, g_k, g_v, g_o, g_i01, g_i23, g_u01, g_u23 = [
        Gather(me, src, out, local, send, recv, k, start, half, k in (5, 7), 1 if k in (1, 3) else 2)
        for k, (src, out, start, half) in enumerate(spans)
    ]
    base += 5
    spans = [(last, 0, 768, 2), (last, 1536, 768, 2), (middle, 0, 768, 1), (middle, 1536, 768, 1)]
    spans += [(first, 2304, 384, 0)] + [(first, 768 * k, 384, 0) for k in range(3)]
    u01, u23, i01, i23, out, que, key, val = [
        Reduce(me, grads, total, boxes[6 * k : 6 * k + 6], send, recv, base + k * REDUCE_MOVES, start, half, group)
        for k, (grads, start, half, group) in enumerate(spans)
    ]
    vector_sum = VectorSum(me, table, parts, boxes[-4:], sums, send, recv, base + N_REDUCES * REDUCE_MOVES)

    def move(slot, src, dst):
        return lambda: pltpu.make_async_copy(src(), dst(), local.at[N_GATHERS + slot])

    q_cols, o_cols = slice(0, 3 * WIDTH), slice(3 * WIDTH, 4 * WIDTH)
    keep_normed = move(1, lambda: big_b.at[:, o_cols], lambda: normed_kept)
    keep_qkv = move(2, lambda: big_a.at[:, q_cols], lambda: qkv_kept)
    keep_w = move(3, lambda: last, lambda: w_qkvo)
    save_result = [
        move(k, lambda v=view: v(), lambda n=n: result.at[:, n * 256 : n * 256 + 256])
        for n, (k, view) in enumerate(
            ((4, lambda: qa.at[0]), (10, lambda: qa.at[1]), (11, lambda: da.at[0]))
        )
    ]
    load_qkv = move(5, lambda: qkv_kept, lambda: big_a.at[:, q_cols])
    load_w_o = move(
        6, lambda: w_qkvo.at[:, :, :, :, o_cols], lambda: first.at[:, :, :, :, o_cols]
    )
    load_w_qkv = move(
        7, lambda: w_qkvo.at[:, :, :, :, q_cols], lambda: last.at[:, :, :, :, q_cols]
    )
    load_normed = move(8, lambda: normed_kept, lambda: big_b.at[:, o_cols])
    save_grad_tok = move(9, lambda: small_a, lambda: grad_tok)

    sums_ref = table

    def tally(row, values):
        sums_ref[row : row + 1] += jnp.sum(values, axis=0, keepdims=True)

    def valid_of(rows):
        return jnp.where(seg[rows].astype(F32)[:, 0:1] != 0.0, 1.0, 0.0)

    vectors.step(0)
    g_q.step(0)
    g_k.step(0)
    ids = jnp.broadcast_to(seg_row[...].astype(F32), (8, SEQ))
    ids = jnp.where(iota_of((8, SEQ), 0) == 0, ids, 0.0).astype(BF)
    seg[...] = dg(ids, jnp.ones((8, 128), BF), 0, 0).astype(BF)
    sums_ref[...] = jnp.zeros_like(sums_ref)
    lse[...] = jnp.zeros_like(lse)
    vectors.step(1)
    g_q.step(1)
    g_v.step(0)
    vectors.step(2)
    g_k.step(1)
    g_o.step(0)
    vectors.step(3)
    g_q.step(2)
    g_v.step(1)
    g_i01.step(0)
    spread = dg(got[...].reshape(256, 128), pick[...], 1, 0)
    names = jnp.zeros((16, WIDTH), F32)
    for k in range(16):
        names += spread[16 * k : 16 * k + 16] * rows_of[k : k + 1]
    vec[...] = names
    for k in range(4):
        row = jnp.zeros((1, WIDTH), F32)
        for f in range(4):
            for r in range(4):
                spot = 16 * (4 * k + f) + 8 + r
                row += spread[spot : spot + 1] * rows_of[4 * f + r : 4 * f + r + 1]
        vec[8 + k : 9 + k] = row
    g_k.step(2)
    g_o.step(1)
    g_i23.step(0)
    lane = lanes(SEQ)
    hot = seg[...].astype(F32) == lane.astype(F32)
    for h in range(2):
        qa[h, :, 128:] = jnp.where(hot, 1.0, 0.0).astype(BF)
    ka[:, 128:] = jnp.where(hot | (lane > 8), 0.0, -1e30).astype(BF)
    va[:, 128:] = jnp.ones((SEQ, 128), BF)

    def first_norm(rows):
        stream = tok[rows].astype(F32)
        valid = valid_of(rows)
        tally(12, stream * stream * valid)
        tally(16, jnp.broadcast_to(valid, stream.shape))
        unit, _ = normalized(stream)
        big_b[rows, o_cols] = (unit * vec[0:1] + vec[1:2]).astype(BF)

    blocks(BLOCK, first_norm)
    keep_normed().start()

    def project(k, bias):
        def part(rows):
            made = dg(big_b[rows, o_cols], tile_of(last, WIDTH * k), 1, 1)
            if bias is not None:
                made = made + vec[bias : bias + 1]
            big_a[rows, piece(k)] = made.astype(BF)

        blocks(512, part)

    g_q.step(3)
    g_v.step(2)
    g_i01.step(1)
    g_u01.step(0)
    g_k.step(3)
    g_q.step(4)
    project(0, 2)
    g_o.step(2)
    g_i23.step(1)
    g_u23.step(0)
    g_k.step(4)
    project(1, None)
    g_v.step(3)
    g_v.step(4)
    project(2, 3)
    keep_qkv().start()

    def ticks(table):
        def at(pair, half):
            for moment, steps in table.items():
                if moment % 2 == half:

                    @pl.when(pair == moment // 2)
                    def _(steps=steps):
                        for step in steps:
                            step()

        return at

    def s(chunk, number):
        return lambda: chunk.step(number)

    forward_ticks = ticks(
        {
            0: [s(g_i01, 2)],
            1: [s(g_u01, 1), s(g_o, 3)],
            2: [s(g_o, 4), lambda: keep_w().start()],
            4: [s(g_i23, 2), s(g_u23, 1)],
            5: [s(g_i01, 3)],
            6: [s(g_i01, 4), s(g_u01, 2)],
            8: [s(g_i23, 3)],
            10: [s(g_i23, 4), s(g_u23, 2)],
        }
    )

    @pl.loop(0, WIDTH // 128)
    def _(pair):
        forward_ticks(pair, 0)
        spot = pair * 128
        query = big_a[:, aligned(spot, 128)].astype(F32) * 0.125
        lane = lanes(SEQ)
        qa[0, :, :128] = jnp.where(lane < 64, query, 0.0).astype(BF)
        qa[1, :, :128] = jnp.where(lane < 64, 0.0, query).astype(BF)
        ka[:, :128] = big_a[:, aligned(WIDTH + spot, 128)]
        va[:, :128] = big_a[:, aligned(2 * WIDTH + spot, 128)]
        lane = lanes(BLOCK)
        work = [(step, h) for step in range(SEQ // BLOCK) for h in range(2)]
        mixed = [None, None]

        def score(step, h):
            return dg(qa[h, step * BLOCK : (step + 1) * BLOCK], ka[...], 1, 1)

        coming = score(*work[0])
        for number, (step, h) in enumerate(work):
            if number == len(work) // 2:
                forward_ticks(pair, 1)
            scores = coming
            if number + 1 < len(work):
                coming = score(*work[number + 1])
            rows = slice(step * BLOCK, (step + 1) * BLOCK)
            largest = jnp.max(scores, axis=1, keepdims=True)
            prob = jnp.exp(scores - largest).astype(BF)
            both = dg(prob, va[...], 1, 0)
            weight = both[:, 128:]
            mixed[h] = both[:, :128] / weight
            lse[rows] = jnp.where(lane == 2 * pair + h, largest + jnp.log(weight), lse[rows])
            if h == 1:
                both = jnp.where(lane < 64, mixed[0], mixed[1])
                small_b[rows, aligned(spot, 128)] = both.astype(BF)

    def second_norm(rows):
        valid = valid_of(rows)
        branch = dg(small_b[rows], tile_of(last, 3 * WIDTH), 1, 1) + vec[4:5]
        stream = tok[rows].astype(F32) + branch
        tally(13, branch * branch * valid)
        tally(14, stream * stream * valid)
        mid[rows] = stream
        unit, _ = normalized(stream)
        small_a[rows] = (unit * vec[6:7] + vec[7:8]).astype(BF)

    blocks(BLOCK, second_norm)
    g_u01.step(3)
    keep_normed().wait()
    keep_qkv().wait()
    for k in range(4):
        def expand(rows, k=k):
            hidden = dg(small_a[rows], inner_tile(middle, k), 1, 1) + vec[8 + k : 9 + k]
            phi = 0.5 + 0.5 * lax.erf(hidden * (0.5**0.5))
            bell = jnp.exp(hidden * hidden * -0.5) * 0.3989422804014327
            big_a[rows, piece(k)] = (hidden * phi).astype(BF)
            big_b[rows, piece(k)] = (phi + hidden * bell).astype(BF)

        blocks(BLOCK, expand)
        if k == 0:
            g_u01.step(4)
        if k == 1:
            g_u23.step(3)

    def store_grad(whole, k, left, right):
        made = dg(left, right, 0, 0).astype(BF)
        whole[:, :, :, :, piece(k)] = made.reshape(4, 2, 2, PIECE, WIDTH)

    keep_w().wait()
    store_grad(last, 0, cot[...], big_a[:, piece(0)])
    store_grad(last, 1, cot[...], big_a[:, piece(1)])
    u01.step(0)
    store_grad(last, 2, cot[...], big_a[:, piece(2)])
    store_grad(last, 3, cot[...], big_a[:, piece(3)])
    g_u23.step(4)
    u01.step(1)
    u23.step(0)
    for k in range(4):
        def through_gelu(rows, k=k):
            grad_active = dg(cot[rows], tile_of(first, k * WIDTH), 1, 0)
            grad_hidden = (grad_active * big_b[rows, piece(k)].astype(F32)).astype(BF)
            big_b[rows, piece(k)] = grad_hidden
            tally(8 + k, grad_hidden.astype(F32))

        blocks(BLOCK, through_gelu)
        if k == 1:
            u23.step(1)
    u01.step(2)

    def contract(rows):
        valid = valid_of(rows)
        ffn_out = dg(big_a[rows], first[...].reshape(WIDTH, 4 * WIDTH), 1, 1) + vec[5:6]
        tally(15, ffn_out * ffn_out * valid)
        made = (mid[rows] + ffn_out).astype(BF)
        qa[0, rows] = made[:, :256]
        qa[1, rows] = made[:, 256:512]
        da[0, rows] = made[:, 512:]

    blocks(BLOCK, contract)
    for make in save_result:
        make().start()
    load_qkv().start()
    load_w_o().start()
    u01.step(3)
    u23.step(2)

    def ffn_norm_back(rows):
        grad_second = dg(big_b[rows, piece(0)], inner_tile(middle, 0), 1, 0)
        for k in range(1, 4):
            grad_second += dg(big_b[rows, piece(k)], inner_tile(middle, k), 1, 0)
        unit, scale = normalized(mid[rows])
        tally(6, grad_second * unit)
        tally(7, grad_second)
        upper = cot[rows].astype(F32)
        tally(5, upper)
        grad_middle = upper + norm_grad(grad_second * vec[6:7], unit, scale)
        mid[rows] = grad_middle
        tally(4, grad_middle.astype(BF).astype(F32))

    blocks(BLOCK, ffn_norm_back)
    u23.step(3)
    u01.step(4)
    for k in range(4):
        made = dg(big_b[:, piece(k)], small_a[...], 0, 0).astype(BF).reshape(4, 4, PIECE, WIDTH)
        for r in range(4):
            middle[k, :, :, :, piece(r)] = made[:, r].reshape(2, 2, PIECE, WIDTH)
    i01.step(0)
    u01.step(5)
    load_normed().start()
    load_w_o().wait()

    def to_attended(rows):
        grad = dg(mid[rows].astype(BF), tile_of(first, 3 * WIDTH), 1, 0)
        big_a[rows, o_cols] = grad.astype(BF)

    blocks(512, to_attended)
    i23.step(0)
    u23.step(4)
    store_grad(first, 3, mid[...].astype(BF), small_b[...])
    i01.step(1)
    out.step(0)
    u23.step(5)
    load_w_qkv().start()
    load_qkv().wait()
    for make in save_result:
        make().wait()

    lane = lanes(SEQ)
    hot = seg[...].astype(F32) == lane.astype(F32)
    ones = (lane > 8) & (lane < 12)
    ka[:, 128:] = jnp.where(ones, 1.0, jnp.where(hot | (lane > 8), 0.0, -1e30)).astype(BF)
    va[:, 128:] = jnp.where(lane < 3, 1.0, 0.0).astype(BF)

    backward_ticks = ticks(
        {
            2: [s(i23, 1), s(out, 1)],
            4: [s(i01, 2)],
            6: [s(i01, 3), s(i23, 2)],
            8: [s(out, 2), s(i23, 3), s(i01, 4)],
            10: [s(out, 3), s(i23, 4), s(i01, 5)],
        }
    )

    @pl.loop(0, WIDTH // 128)
    def _(pair):
        backward_ticks(pair, 0)
        spot = pair * 128
        lane = lanes(SEQ)
        hot = jnp.where(seg[...].astype(F32) == lane.astype(F32), 1.0, 0.0)
        query = big_a[:, aligned(spot, 128)].astype(F32) * 0.125
        ka[:, :128] = big_a[:, aligned(WIDTH + spot, 128)]
        va[:, :128] = big_a[:, aligned(2 * WIDTH + spot, 128)]
        upper = big_a[:, aligned(3 * WIDTH + spot, 128)].astype(F32)
        both = small_b[:, aligned(spot, 128)].astype(F32) * upper
        for h in range(2):
            mine = (lane < 64) if h == 0 else (lane >= 64)
            qa[h, :, :128] = jnp.where(mine, query, 0.0).astype(BF)
            da[h, :, :128] = jnp.where(mine, upper, 0.0).astype(BF)
            level = jnp.sum(jnp.where(lane == 2 * pair + h, lse[...], 0.0), axis=1, keepdims=True)
            qa[h, :, 128:] = three_terms(jnp.broadcast_to(-level, hot.shape), lane, 9, hot)
            weighted = jnp.sum(jnp.where(mine, both, 0.0), axis=1, keepdims=True)
            da[h, :, 128:] = three_terms(
                jnp.broadcast_to(-weighted, hot.shape), lane, 0, jnp.zeros_like(hot)
            )
        for step in range(SEQ // KEYS):
            rows = slice(step * KEYS, (step + 1) * KEYS)
            for_keys, for_values = [], []
            for h in range(2):
                prob = jnp.exp(dg(ka[rows], qa[h], 1, 1))
                grad_score = (prob * dg(va[rows], da[h], 1, 1)).astype(BF)
                for_values.append(dg(prob.astype(BF), da[h, :, :128], 1, 0))
                for_keys.append(dg(grad_score, qa[h, :, :128], 1, 0))
                for_queries = dg(ka[rows, :128], grad_score, 0, 0)
                acc[h] = for_queries if step == 0 else acc[h] + for_queries
            big_b[rows, aligned(WIDTH + spot, 128)] = (for_keys[0] + for_keys[1]).astype(BF)
            big_b[rows, aligned(2 * WIDTH + spot, 128)] = (for_values[0] + for_values[1]).astype(BF)
        pair_grad = jnp.concatenate([acc[0, :64], acc[1, 64:]], axis=0) * 0.125
        big_b[:, aligned(spot, 128)] = pair_grad.T.astype(BF)

    load_normed().wait()
    store_grad(first, 0, big_b[:, piece(0)], big_b[:, o_cols])
    que.step(0)
    out.step(4)
    store_grad(first, 1, big_b[:, piece(1)], big_b[:, o_cols])
    key.step(0)
    que.step(1)
    i23.step(5)
    store_grad(first, 2, big_b[:, piece(2)], big_b[:, o_cols])
    val.step(0)
    key.step(1)
    out.step(5)
    load_w_qkv().wait()

    @pl.loop(0, SEQ // BLOCK)
    def _(step):
        rows = aligned(step * BLOCK, BLOCK, BLOCK)
        grad_normed = dg(big_b[rows, piece(0)], tile_of(last, 0), 1, 0)
        for k in range(1, 3):
            grad_normed += dg(big_b[rows, piece(k)], tile_of(last, k * WIDTH), 1, 0)
        tally(2, big_b[rows, piece(0)].astype(F32))
        tally(3, big_b[rows, piece(2)].astype(F32))
        unit, scale = normalized(tok[rows].astype(F32))
        tally(0, grad_normed * unit)
        tally(1, grad_normed)
        grad_stream = mid[rows] + norm_grad(grad_normed * vec[0:1], unit, scale)
        small_a[rows] = grad_stream.astype(BF)

        @pl.when(step == 0)
        def _():
            que.step(2)

        @pl.when(step == 1)
        def _():
            val.step(1)

        @pl.when(step == 2)
        def _():
            key.step(2)

        @pl.when(step == 3)
        def _():
            que.step(3)

    save_grad_tok().start()
    vector_sum.step(0)
    val.step(2)
    vector_sum.step(1)
    que.step(4)
    key.step(3)
    vector_sum.step(2)
    val.step(3)
    vector_sum.step(3)
    key.step(4)
    que.step(5)
    vector_sum.step(4)
    val.step(4)
    key.step(5)
    val.step(5)
    save_grad_tok().wait()


def layer_call(tok, cot, seg_row, weights, vectors):
    vmem, anywhere = pl.BlockSpec(memory_space=pltpu.VMEM), pl.BlockSpec(memory_space=pl.ANY)
    whole = (4, 2, 2, PIECE, 4 * WIDTH)
    wide = lambda k, kind: pltpu.VMEM((SEQ, k), kind)
    outs = [jax.ShapeDtypeStruct((SEQ, WIDTH), BF)] * 2
    outs += [jax.ShapeDtypeStruct((3, PIECE, 4 * WIDTH), F32), jax.ShapeDtypeStruct((16, 128), F32)]
    outs += [jax.ShapeDtypeStruct(whole, BF)]
    outs += [jax.ShapeDtypeStruct((SEQ, 3 * WIDTH), BF), jax.ShapeDtypeStruct((SEQ, WIDTH), BF)]
    scratch = [pltpu.VMEM((16, 128), BF), wide(128, BF), pltpu.VMEM((4, 2, 2, 16, 128), BF), pltpu.VMEM((16, WIDTH), F32)]
    scratch += [wide(4 * WIDTH, BF)] * 2 + [pltpu.VMEM(whole, BF)] * 3
    scratch += [wide(WIDTH, BF)] * 2 + [wide(WIDTH, F32), wide(128, F32)]
    scratch += [pltpu.VMEM((2, SEQ, 256), BF), wide(256, BF), wide(256, BF), pltpu.VMEM((2, SEQ, 256), BF)]
    scratch += [pltpu.VMEM((2, 128, SEQ), F32), pltpu.VMEM((24, WIDTH), F32), pltpu.VMEM((4, 2, 2, 16, 128), F32)]
    scratch += [pltpu.SemaphoreType.DMA((N_COPIES,))] * 2 + [pltpu.SemaphoreType.DMA((20,))]
    for half in [768] * 4 + [384] * 4:
        scratch += boxes_for(half)
    for shape in ((4, 2, 2), (4, 2), (4,), (3,)):
        scratch.append(pltpu.VMEM((*shape, 16, 128), F32))
    place = np.arange(WIDTH)
    pick = jnp.asarray((place[None, :] % PIECE == np.arange(128)[:, None]), BF)
    rows_of = jnp.asarray((place[None, :] // PIECE == np.arange(16)[:, None]), F32)
    return pl.pallas_call(
        layer_kernel,
        out_shape=outs,
        in_specs=[vmem] * 20,
        out_specs=[anywhere] * 2 + [vmem] * 2 + [anywhere] * 3,
        scratch_shapes=scratch,
        compiler_params=pltpu.CompilerParams(
            collective_id=1, has_side_effects=True, vmem_limit_bytes=63 * 2**20
        ),
        name="layer",
    )(tok, cot, seg_row, *weights, *vectors, pick, rows_of)[:4]


def packed_inputs(
    weight_query, weight_key, weight_value, weight_output, weight_inner, weight_outer,
    bias_query, bias_value, bias_output, bias_inner, bias_outer, gain_attn, shift_attn, gain_ffn, shift_ffn,
):
    four = (weight_query, weight_key, weight_value, weight_output)
    sh_qkvo = jnp.concatenate([w.T for w in four], axis=1)
    sh_in = weight_inner.T.reshape(4, PIECE, WIDTH).transpose(1, 0, 2).reshape(PIECE, 4 * WIDTH)
    sh_out = weight_outer.T.reshape(PIECE, 16, 4, PIECE).transpose(0, 2, 1, 3).reshape(PIECE, 4 * WIDTH)
    vectors = (gain_attn, shift_attn, bias_query, bias_value, bias_output, bias_outer, gain_ffn, shift_ffn)
    pack = jnp.concatenate([jnp.stack(vectors), bias_inner.reshape(4, PIECE)])
    pack = jnp.pad(pack, ((0, 4), (0, 128 - PIECE)))
    return sh_qkvo, sh_in, sh_out, pack


def leave_kernel(total, sums, *refs):
    weights, vectors, inner_bias, rms = refs[:6], refs[6:14], refs[14], refs[15]
    for k in range(4):

        @pl.when(pl.program_id(0) == k)
        def _(k=k):
            weights[k][...] = total[0]

    weights[4][...] = total[1]
    weights[5][...] = total[2]
    for k in range(8):
        vectors[k][...] = sums[k : k + 1, :PIECE]
    inner = jnp.zeros((1, 256), F32)
    for k in range(4):
        row = jnp.where(lanes(1) < PIECE, sums[8 + k : 9 + k], 0.0)
        inner += pltpu.roll(jnp.concatenate([row, jnp.zeros_like(row)], axis=1), PIECE * k, 1)
    inner_bias[...] = inner[:, : 4 * PIECE]
    rms[...] = jnp.sqrt(sums[12:13, 0:4] / sums[12:13, 4:5])


def leave_call(total, sums):
    kept = lambda shape: pl.BlockSpec(shape, lambda k: (0, 0))
    outs = [jax.ShapeDtypeStruct((PIECE, WIDTH), F32)] * 4
    outs += [jax.ShapeDtypeStruct((4 * PIECE, WIDTH), F32), jax.ShapeDtypeStruct((PIECE, 4 * WIDTH), F32)]
    outs += [jax.ShapeDtypeStruct((1, PIECE), F32)] * 8
    outs += [jax.ShapeDtypeStruct((1, 4 * PIECE), F32), jax.ShapeDtypeStruct((1, 4), F32)]
    return pl.pallas_call(
        leave_kernel,
        out_shape=outs,
        grid=(4,),
        in_specs=[pl.BlockSpec((3, PIECE, WIDTH), lambda k: (0, 0, k)), kept((16, 128))],
        out_specs=[*[kept((PIECE, WIDTH))] * 4]
        + [pl.BlockSpec((PIECE, WIDTH), lambda k: (k, 0)), pl.BlockSpec((PIECE, WIDTH), lambda k: (0, k))]
        + [kept((1, PIECE))] * 8
        + [kept((1, 4 * PIECE)), kept((1, 4))],
        compiler_params=pltpu.CompilerParams(vmem_limit_bytes=60 * 2**20),
        name="leave",
    )(total, sums)


def fast_body(
    tokens, segment_ids, cotangent,
    weight_query, weight_key, weight_value, weight_output, weight_inner, weight_outer,
    bias_query, bias_value, bias_output, bias_inner, bias_outer, gain_attn, shift_attn, gain_ffn, shift_ffn,
):
    tok, cot = tokens.reshape(SEQ, WIDTH), cotangent.reshape(SEQ, WIDTH)
    weights = (weight_query, weight_key, weight_value, weight_output, weight_inner, weight_outer)
    vectors = (gain_attn, shift_attn, bias_query, bias_value, bias_output, bias_outer, gain_ffn, shift_ffn)
    vectors = [v.reshape(1, -1) for v in (*vectors, bias_inner)]
    result, grad_tok, total, sums = layer_call(tok, cot, segment_ids, [w.T for w in weights], vectors)
    made = (result, grad_tok, *leave_call(total, sums))
    grads, own, inner_bias, rms = [g.T for g in made[2:8]], [v.reshape(PIECE) for v in made[8:16]], made[16], made[17]
    g_attn, s_attn, b_query, b_value, b_output, b_outer, g_ffn, s_ffn = own
    return (
        made[0].reshape(tokens.shape), made[1].reshape(tokens.shape), *grads,
        b_query, b_value, b_output, inner_bias.reshape(4 * PIECE), b_outer, g_attn, s_attn, g_ffn, s_ffn,
        rms.reshape(4),
    )


def scaled(values, gain_vec):
    average = jnp.mean(values, axis=-1, keepdims=True)
    centered = values - average
    spread = jnp.mean(centered * centered, axis=-1, keepdims=True)
    return centered * lax.rsqrt(spread + 1e-06) * gain_vec


def matmul(operand, matrix):
    return jnp.dot(operand, matrix, preferred_element_type=jnp.float32)


def over_rows(operand, other):
    return lax.dot_general(
        operand, other, (((0,), (0,)), ((), ())), preferred_element_type=jnp.float32
    )


def against(operand, matrix):
    return lax.dot_general(
        operand, matrix, (((1,), (1,)), ((), ())), preferred_element_type=jnp.float32
    )


def pair_of(block, offset, seq_len):
    return lax.dynamic_slice_in_dim(block, offset, 2 * HD, 1).reshape(seq_len, 2, HD)


def masked_scores(query_pair, key_pair, same_doc, factor):
    scores = (
        jnp.einsum("qhd,khd->hqk", query_pair, key_pair, preferred_element_type=jnp.float32)
        * factor
    )
    return jnp.where(same_doc, scores, -1e30)


def attend_forward(queries, key_rows, value_rows, doc_ids):
    seq_len, features = queries.shape
    pair_width = 2 * HD
    factor = 1.0 / math.sqrt(HD)
    same_doc = (doc_ids[:, None] == doc_ids[None, :])[None]

    def one_pair(which, buffers):
        attended, logsum = buffers
        offset = which * pair_width
        query_pair = pair_of(queries, offset, seq_len)
        key_pair = pair_of(key_rows, offset, seq_len)
        value_pair = pair_of(value_rows, offset, seq_len)
        scores = masked_scores(query_pair, key_pair, same_doc, factor)
        largest = jnp.max(scores, axis=-1, keepdims=True)
        exponent = jnp.exp(scores - largest)
        denominator = jnp.sum(exponent, axis=-1, keepdims=True)
        probability = (exponent / denominator).astype(jnp.bfloat16)
        mixed_pair = jnp.einsum(
            "hqk,khd->qhd", probability, value_pair, preferred_element_type=jnp.float32
        )
        attended = lax.dynamic_update_slice_in_dim(
            attended, mixed_pair.reshape(seq_len, pair_width), offset, 1
        )
        logsum = lax.dynamic_update_slice_in_dim(
            logsum, (largest + jnp.log(denominator))[:, :, 0], which * 2, 0
        )
        return (attended, logsum)

    initial = (
        jnp.zeros((seq_len, features), jnp.float32),
        jnp.zeros((features // HD, seq_len), jnp.float32),
    )
    return lax.fori_loop(0, features // pair_width, one_pair, initial)


def attend_backward(queries, key_rows, value_rows, upstream, logsum, doc_ids):
    seq_len, features = queries.shape
    pair_width = 2 * HD
    factor = 1.0 / math.sqrt(HD)
    same_doc = (doc_ids[:, None] == doc_ids[None, :])[None]

    def one_pair(which, buffers):
        grad_queries, grad_keys, grad_values = buffers
        offset = which * pair_width
        query_pair = pair_of(queries, offset, seq_len)
        key_pair = pair_of(key_rows, offset, seq_len)
        value_pair = pair_of(value_rows, offset, seq_len)
        upper_pair = pair_of(upstream, offset, seq_len)
        logsum_pair = lax.dynamic_slice_in_dim(logsum, which * 2, 2, 0)
        scores = masked_scores(query_pair, key_pair, same_doc, factor)
        probability = jnp.exp(scores - logsum_pair[:, :, None])
        rounded = probability.astype(jnp.bfloat16)
        value_part = jnp.einsum(
            "hqk,qhd->khd", rounded, upper_pair, preferred_element_type=jnp.float32
        )
        prob_grad = jnp.einsum(
            "qhd,khd->hqk", upper_pair, value_pair, preferred_element_type=jnp.float32
        )
        weighted = jnp.sum(probability * prob_grad, axis=-1, keepdims=True)
        score_grad = (probability * (prob_grad - weighted)).astype(jnp.bfloat16)
        query_part = (
            jnp.einsum("hqk,khd->qhd", score_grad, key_pair, preferred_element_type=jnp.float32)
            * factor
        )
        key_part = (
            jnp.einsum("hqk,qhd->khd", score_grad, query_pair, preferred_element_type=jnp.float32)
            * factor
        )
        grad_queries = lax.dynamic_update_slice_in_dim(
            grad_queries, query_part.reshape(seq_len, pair_width), offset, 1
        )
        grad_keys = lax.dynamic_update_slice_in_dim(
            grad_keys, key_part.reshape(seq_len, pair_width), offset, 1
        )
        grad_values = lax.dynamic_update_slice_in_dim(
            grad_values, value_part.reshape(seq_len, pair_width), offset, 1
        )
        return (grad_queries, grad_keys, grad_values)

    empty_buf = jnp.zeros((seq_len, features), jnp.float32)
    return lax.fori_loop(0, features // pair_width, one_pair, (empty_buf, empty_buf, empty_buf))


def plain_body(
    tokens,
    segment_ids,
    cotangent,
    weight_query,
    weight_key,
    weight_value,
    weight_output,
    weight_inner,
    weight_outer,
    bias_query,
    bias_value,
    bias_output,
    bias_inner,
    bias_outer,
    gain_attn,
    shift_attn,
    gain_ffn,
    shift_ffn,
):
    gathered = (
        lax.all_gather(weight_query, "fsdp", axis=1, tiled=True),
        lax.all_gather(weight_key, "fsdp", axis=1, tiled=True),
        lax.all_gather(weight_value, "fsdp", axis=1, tiled=True),
        lax.all_gather(weight_output, "fsdp", axis=1, tiled=True),
        lax.all_gather(weight_inner, "fsdp", axis=1, tiled=True),
        lax.all_gather(weight_outer, "fsdp", axis=1, tiled=True),
        lax.all_gather(bias_query, "fsdp", axis=0, tiled=True),
        lax.all_gather(bias_value, "fsdp", axis=0, tiled=True),
        lax.all_gather(bias_output, "fsdp", axis=0, tiled=True),
        lax.all_gather(bias_inner, "fsdp", axis=0, tiled=True),
        lax.all_gather(bias_outer, "fsdp", axis=0, tiled=True),
        lax.all_gather(gain_attn, "fsdp", axis=0, tiled=True),
        lax.all_gather(shift_attn, "fsdp", axis=0, tiled=True),
        lax.all_gather(gain_ffn, "fsdp", axis=0, tiled=True),
        lax.all_gather(shift_ffn, "fsdp", axis=0, tiled=True),
    )
    (
        whole_query,
        whole_key,
        whole_value,
        whole_output,
        whole_inner,
        whole_outer,
        query_bias,
        value_bias,
        output_bias,
        inner_bias,
        outer_bias,
        attn_gain,
        attn_shift,
        ffn_gain,
        ffn_shift,
    ) = gathered
    count_seq, seq_len, features = tokens.shape
    row_count = count_seq * seq_len
    stream = tokens.reshape(row_count, features).astype(jnp.float32)
    normed = (
        scaled(stream, attn_gain.astype(jnp.float32)) + attn_shift.astype(jnp.float32)
    ).astype(jnp.bfloat16)
    queries = (matmul(normed, whole_query) + query_bias.astype(jnp.float32)).astype(jnp.bfloat16)
    key_rows = matmul(normed, whole_key).astype(jnp.bfloat16)
    value_rows = (matmul(normed, whole_value) + value_bias.astype(jnp.float32)).astype(jnp.bfloat16)
    query_seq = queries.reshape(count_seq, seq_len, features)
    key_seq = key_rows.reshape(count_seq, seq_len, features)
    value_seq = value_rows.reshape(count_seq, seq_len, features)
    attended, logsum = lax.map(
        lambda packed: attend_forward(*packed), (query_seq, key_seq, value_seq, segment_ids)
    )
    attended = attended.reshape(row_count, features).astype(jnp.bfloat16)
    branch = matmul(attended, whole_output) + output_bias.astype(jnp.float32)
    middle = stream + branch
    second = (scaled(middle, ffn_gain.astype(jnp.float32)) + ffn_shift.astype(jnp.float32)).astype(
        jnp.bfloat16
    )
    hidden = matmul(second, whole_inner) + inner_bias.astype(jnp.float32)
    active = jax.nn.gelu(hidden, approximate=False).astype(jnp.bfloat16)
    ffn_out = matmul(active, whole_outer) + outer_bias.astype(jnp.float32)
    result = middle + ffn_out
    valid_mask = (segment_ids != 0).reshape(row_count).astype(jnp.float32)
    squares = jnp.stack(
        [
            jnp.sum(jnp.sum(piece * piece, axis=-1) * valid_mask)
            for piece in (stream, branch, middle, ffn_out)
        ]
    )
    counted = jnp.sum(valid_mask)
    regathered = (
        lax.all_gather(weight_query, "fsdp", axis=1, tiled=True),
        lax.all_gather(weight_key, "fsdp", axis=1, tiled=True),
        lax.all_gather(weight_value, "fsdp", axis=1, tiled=True),
        lax.all_gather(weight_output, "fsdp", axis=1, tiled=True),
        lax.all_gather(weight_inner, "fsdp", axis=1, tiled=True),
        lax.all_gather(weight_outer, "fsdp", axis=1, tiled=True),
        lax.all_gather(gain_attn, "fsdp", axis=0, tiled=True),
        lax.all_gather(gain_ffn, "fsdp", axis=0, tiled=True),
    )
    (
        back_query,
        back_key,
        back_value,
        back_output,
        back_inner,
        back_outer,
        back_attn_gain,
        back_ffn_gain,
    ) = regathered
    grad_out = cotangent.reshape(row_count, features)
    grad_outer = over_rows(active, grad_out)
    biasgrad_outer = jnp.sum(grad_out.astype(jnp.float32), axis=0)
    grad_active = against(grad_out, back_outer)
    _, gelu_back = jax.vjp(lambda values: jax.nn.gelu(values, approximate=False), hidden)
    grad_hidden = gelu_back(grad_active)[0].astype(jnp.bfloat16)
    grad_inner = over_rows(second, grad_hidden)
    biasgrad_inner = jnp.sum(grad_hidden.astype(jnp.float32), axis=0)
    grad_second = against(grad_hidden, back_inner)
    _, norm_back_ffn = jax.vjp(scaled, middle, back_ffn_gain.astype(jnp.float32))
    grad_middle, gaingrad_ffn = norm_back_ffn(grad_second)
    shiftgrad_ffn = jnp.sum(grad_second, axis=0)
    grad_middle = grad_middle + grad_out.astype(jnp.float32)
    grad_branch = grad_middle.astype(jnp.bfloat16)
    grad_output = over_rows(attended, grad_branch)
    biasgrad_output = jnp.sum(grad_branch.astype(jnp.float32), axis=0)
    grad_attended = against(grad_branch, back_output).astype(jnp.bfloat16)
    upstream_seq = grad_attended.reshape(count_seq, seq_len, features)
    grad_q_seq, grad_k_seq, grad_v_seq = lax.map(
        lambda packed: attend_backward(*packed),
        (query_seq, key_seq, value_seq, upstream_seq, logsum, segment_ids),
    )
    grad_queries = grad_q_seq.reshape(row_count, features).astype(jnp.bfloat16)
    grad_keys = grad_k_seq.reshape(row_count, features).astype(jnp.bfloat16)
    grad_values = grad_v_seq.reshape(row_count, features).astype(jnp.bfloat16)
    grad_query = over_rows(normed, grad_queries)
    grad_key = over_rows(normed, grad_keys)
    grad_value = over_rows(normed, grad_values)
    biasgrad_query = jnp.sum(grad_queries.astype(jnp.float32), axis=0)
    biasgrad_value = jnp.sum(grad_values.astype(jnp.float32), axis=0)
    grad_normed = (
        against(grad_queries, back_query)
        + against(grad_keys, back_key)
        + against(grad_values, back_value)
    )
    _, norm_back_attn = jax.vjp(scaled, stream, back_attn_gain.astype(jnp.float32))
    grad_stream, gaingrad_attn = norm_back_attn(grad_normed)
    shiftgrad_attn = jnp.sum(grad_normed, axis=0)
    grad_input = (grad_middle + grad_stream).astype(jnp.bfloat16).reshape(tokens.shape)
    square_total, count_total = lax.psum((squares, counted), ("fsdp", "dp"))
    reduced = (
        lax.psum_scatter(grad_query, "fsdp", scatter_dimension=1, tiled=True),
        lax.psum_scatter(grad_key, "fsdp", scatter_dimension=1, tiled=True),
        lax.psum_scatter(grad_value, "fsdp", scatter_dimension=1, tiled=True),
        lax.psum_scatter(grad_output, "fsdp", scatter_dimension=1, tiled=True),
        lax.psum_scatter(grad_inner, "fsdp", scatter_dimension=1, tiled=True),
        lax.psum_scatter(grad_outer, "fsdp", scatter_dimension=1, tiled=True),
        lax.psum_scatter(biasgrad_query, "fsdp", scatter_dimension=0, tiled=True),
        lax.psum_scatter(biasgrad_value, "fsdp", scatter_dimension=0, tiled=True),
        lax.psum_scatter(biasgrad_output, "fsdp", scatter_dimension=0, tiled=True),
        lax.psum_scatter(biasgrad_inner, "fsdp", scatter_dimension=0, tiled=True),
        lax.psum_scatter(biasgrad_outer, "fsdp", scatter_dimension=0, tiled=True),
        lax.psum_scatter(gaingrad_attn, "fsdp", scatter_dimension=0, tiled=True),
        lax.psum_scatter(shiftgrad_attn, "fsdp", scatter_dimension=0, tiled=True),
        lax.psum_scatter(gaingrad_ffn, "fsdp", scatter_dimension=0, tiled=True),
        lax.psum_scatter(shiftgrad_ffn, "fsdp", scatter_dimension=0, tiled=True),
    )
    summed = (
        lax.psum(reduced[0].astype(jnp.bfloat16), "dp").astype(jnp.float32),
        lax.psum(reduced[1].astype(jnp.bfloat16), "dp").astype(jnp.float32),
        lax.psum(reduced[2].astype(jnp.bfloat16), "dp").astype(jnp.float32),
        lax.psum(reduced[3].astype(jnp.bfloat16), "dp").astype(jnp.float32),
        lax.psum(reduced[4].astype(jnp.bfloat16), "dp").astype(jnp.float32),
        lax.psum(reduced[5].astype(jnp.bfloat16), "dp").astype(jnp.float32),
        lax.psum(reduced[6].astype(jnp.bfloat16), "dp").astype(jnp.float32),
        lax.psum(reduced[7].astype(jnp.bfloat16), "dp").astype(jnp.float32),
        lax.psum(reduced[8].astype(jnp.bfloat16), "dp").astype(jnp.float32),
        lax.psum(reduced[9].astype(jnp.bfloat16), "dp").astype(jnp.float32),
        lax.psum(reduced[10].astype(jnp.bfloat16), "dp").astype(jnp.float32),
        lax.psum(reduced[11].astype(jnp.bfloat16), "dp").astype(jnp.float32),
        lax.psum(reduced[12].astype(jnp.bfloat16), "dp").astype(jnp.float32),
        lax.psum(reduced[13].astype(jnp.bfloat16), "dp").astype(jnp.float32),
        lax.psum(reduced[14].astype(jnp.bfloat16), "dp").astype(jnp.float32),
    )
    rms_stats = jnp.sqrt(square_total / (count_total * features))
    return (
        result.astype(jnp.bfloat16).reshape(tokens.shape),
        grad_input,
        summed[0],
        summed[1],
        summed[2],
        summed[3],
        summed[4],
        summed[5],
        summed[6],
        summed[7],
        summed[8],
        summed[9],
        summed[10],
        summed[11],
        summed[12],
        summed[13],
        summed[14],
        rms_stats,
    )


def solution(mesh):
    in_specs = (
        P(("fsdp", "dp"), None, None),
        P(("fsdp", "dp"), None),
        P(("fsdp", "dp"), None, None),
        P(None, "fsdp"),
        P(None, "fsdp"),
        P(None, "fsdp"),
        P(None, "fsdp"),
        P(None, "fsdp"),
        P(None, "fsdp"),
        P("fsdp"),
        P("fsdp"),
        P("fsdp"),
        P("fsdp"),
        P("fsdp"),
        P("fsdp"),
        P("fsdp"),
        P("fsdp"),
        P("fsdp"),
    )
    out_specs = (
        P(("fsdp", "dp"), None, None),
        P(("fsdp", "dp"), None, None),
        P(None, "fsdp"),
        P(None, "fsdp"),
        P(None, "fsdp"),
        P(None, "fsdp"),
        P(None, "fsdp"),
        P(None, "fsdp"),
        P("fsdp"),
        P("fsdp"),
        P("fsdp"),
        P("fsdp"),
        P("fsdp"),
        P("fsdp"),
        P("fsdp"),
        P("fsdp"),
        P("fsdp"),
        P(),
    )
    body = fast_body if dict(mesh.shape) == {"fsdp": 16, "dp": 2} else plain_body
    return jax.shard_map(body, mesh=mesh, in_specs=in_specs, out_specs=out_specs, check_vma=False)
```
